32 devices in a mesh: member: 2 (over y), lat: 16 (over z, x, core).
Axes of the slice: x: 2, y: 2, z: 4, core: 2. Of those that a mesh axis runs over, the one named last changes fastest.
Arguments:
- grid_latent: bfloat16 [32768, 512], P(('member', 'lat')), parts along dimension 0, may hold values from -6 to 6
- mesh_latent: bfloat16 [10240, 512], P(('member', 'lat')), parts along dimension 0, may hold values from -6 to 6
- grid_cotangent: bfloat16 [32768, 512], P(('member', 'lat')), parts along dimension 0, may hold values from -6 to 6
- enc_sender: int32 [65536], P(('member', 'lat')), parts along dimension 0, may hold values from 0 to 1023
- enc_receiver: int32 [65536], P(('member', 'lat')), parts along dimension 0, may hold values from 0 to 63
- enc_feat: float32 [4, 65536], P(None, ('member', 'lat')), parts along dimension 1, may hold values from -6 to 6
- enc_count: int32 [32], P(('member', 'lat')), parts along dimension 0, may hold values from 1 to 2048, 16384 in all
- dec_sender: int32 [3, 32768], P(None, ('member', 'lat')), parts along dimension 1, may hold values from 0 to 63
- dec_feat: float32 [3, 4, 32768], P(None, None, ('member', 'lat')), parts along dimension 2, may hold values from -6 to 6
- serve_rows: int32 [32, 16, 4], P(('member', 'lat')), parts along dimension 0, may hold values from 0 to 319
- enc_proj: bfloat16 [512, 512], replicated, may hold values from -0.25 to 0.25
- node_proj: bfloat16 [512, 512], replicated, may hold values from -0.25 to 0.25
- dec_proj: bfloat16 [512, 512], replicated, may hold values from -0.25 to 0.25
- enc_feat_w: float32 [512, 4], replicated, may hold values from -3 to 3
- dec_feat_w: float32 [512, 4], replicated, may hold values from -3 to 3
Outputs:
- grid_grad: bfloat16 [32768, 512], P(('member', 'lat')), parts along dimension 0
- mesh_grad: bfloat16 [10240, 512], P(('member', 'lat')), parts along dimension 0
- enc_proj_grad: float32 [1024, 512], P(('member', 'lat')), parts along dimension 0
- node_proj_grad: float32 [1024, 512], P(('member', 'lat')), parts along dimension 0
- dec_proj_grad: float32 [1024, 512], P(('member', 'lat')), parts along dimension 0
- enc_feat_w_grad: float32 [1024, 4], P(('member', 'lat')), parts along dimension 0
- dec_feat_w_grad: float32 [1024, 4], P(('member', 'lat')), parts along dimension 0
The draws below stay inside these ranges and needn't reach their ends.
There are 2 independent parts, one for each index of `member`. The reference program is written for one: setup_inputs(seed, part) draws one part's arguments, and reference() takes and returns one part's arrays. A program takes and returns all parts, laid end to end along the dimension named above; an argument that names none is the same for every part. Nothing has to cross between parts.
Inputs may be any that keep to these rules, and one draw needn't show every extreme that they name: Each band's live edges are its first enc_count entries; some band has all 2048 live. `enc_sender`: band-local grid rows. `enc_receiver`: slots of the sending band. `dec_sender`: slots of the band holding the grid point. `serve_rows`: local mesh rows of the owner; a node may fill several slots.
All inputs are finite; a program needn't handle non-finite values. No bound on the sum of `enc_count` on one device may be relied on, other than what follows from the above.
Results may differ from the reference program's by a relative error of at most 0.012.
Values may be sent and summed in bfloat16 or wider, within the bound.
No kernel may reach another device: no remote copies, remote signals or barrier semaphores. Data moves between devices by JAX's collectives and lax.ppermute only.
A program may use at most 64 MiB of HBM per device.

```python
import math
import jax
import jax.numpy as jnp
import numpy as np
from jax import lax

L = 512
EFEAT = 4
GRID_DEV = 1024
MESH_DEV = 320
CAP = 4
ENC_CAP = 2048
WIN = 64
GRID = 16384
MESH = 5120
ENC_EDGES = 32768
N_LAT = 16


def touch_ends(drawn, rng, low, high):
    shape = drawn.shape
    place = [jax.random.randint(jax.random.fold_in(rng, axis), (), 0, shape[axis]) for axis in range(len(shape))]
    drawn = drawn.at[tuple(place)].set(low)
    longest = shape.index(max(shape))
    place[longest] = (place[longest] + 1) % shape[longest]
    return drawn.at[tuple(place)].set(high)


def levels(own_key, dims, pieces, least, top_value):
    def one(axis_at, shards_of):
        heights = jax.random.uniform(jax.random.fold_in(jax.random.fold_in(own_key, 6), axis_at), (shards_of,), jnp.float32, least / len(pieces), top_value / len(pieces))
        return jnp.repeat(jnp.exp(heights), dims[axis_at] // shards_of).reshape((-1,) + (1,) * (len(dims) - axis_at - 1))

    factor_of = one(*pieces[0])
    for cut in pieces[1:]:
        factor_of = factor_of * one(*cut)
    return factor_of


def split_up(count, total, bound, lean):
    loads = [(1 << 20) // math.isqrt(grade ** lean) + 1 for grade in range(2, count + 1)]
    surplus, holding = total - bound - (count - 1), [1] * (count - 1)
    while surplus > 0:
        movable = [i for i in range(count - 1) if holding[i] < bound]
        mass, left = sum([loads[i] for i in movable]), surplus
        for i in movable:
            more = min(bound - holding[i], max(1, left * loads[i] // mass), surplus)
            holding[i] = holding[i] + more
            surplus = surplus - more
    return np.array([bound] + holding)


def uneven_parts(rng, count, total, bound, slope):
    if count == 2:
        one = jax.random.randint(rng, (), max(1, total - bound), min(bound, total - 1) + 1)
        return jnp.stack([one, total - one])
    tallies = jnp.asarray(split_up(count, total, bound, slope), jnp.int32)
    couples = (count - 1) // 2
    donor, taker = tallies[1:1 + 2 * couples:2], tallies[2:2 + 2 * couples:2]
    slack = jnp.minimum(donor - 1, bound - taker)
    shifted = jax.random.randint(jax.random.fold_in(rng, 1), (couples,), 0, 1 << 20) % (slack + 1)
    tallies = tallies.at[1:1 + 2 * couples:2].set(donor - shifted).at[2:2 + 2 * couples:2].set(taker + shifted)
    return tallies[jax.random.permutation(jax.random.fold_in(rng, 2), count)]


def centred(own_key, shape, width, limit, cuts=(), held_as=jnp.bfloat16):
    loudness = levels(own_key, shape, cuts, -0.22, 0.18) if cuts else 1.0
    result = jax.random.normal(own_key, shape, jnp.float32) * width * loudness
    return jnp.minimum(jnp.maximum(result, -limit), limit).astype(held_as)


def setup_inputs(seed: int = 0, part: int = 0) -> dict:
    keys = jax.random.split(jax.random.key(seed), 16)
    part_splits = jax.random.split(jax.random.fold_in(keys[15], part), 16)
    return {
        "grid_latent": centred(part_splits[0], (GRID, L), 1.0, 6.0, ((0, 16),)),
        "mesh_latent": centred(part_splits[1], (MESH, L), 1.0, 6.0, ((0, 16),)),
        "grid_cotangent": centred(part_splits[2], (GRID, L), 1.0, 6.0, ((0, 16),)),
        "enc_sender": touch_ends(jax.random.randint(part_splits[3], (ENC_EDGES,), 0, GRID_DEV), jax.random.fold_in(part_splits[3], 1), 0, GRID_DEV - 1).astype(jnp.int32),
        "enc_receiver": touch_ends(jax.random.randint(part_splits[4], (ENC_EDGES,), 0, WIN), jax.random.fold_in(part_splits[4], 1), 0, WIN - 1).astype(jnp.int32),
        "enc_feat": centred(part_splits[5], (EFEAT, ENC_EDGES), 1.0, 6.0, ((1, 16),), jnp.float32),
        "enc_count": uneven_parts(part_splits[6], N_LAT, ENC_CAP * N_LAT // 2, ENC_CAP, 2).astype(jnp.int32),
        "dec_sender": touch_ends(jax.random.randint(part_splits[7], (3, GRID), 0, WIN), jax.random.fold_in(part_splits[7], 1), 0, WIN - 1).astype(jnp.int32),
        "dec_feat": centred(part_splits[8], (3, EFEAT, GRID), 1.0, 6.0, ((2, 16),), jnp.float32),
        "serve_rows": touch_ends(jax.random.randint(part_splits[9], (N_LAT, N_LAT, CAP), 0, MESH_DEV), jax.random.fold_in(part_splits[9], 1), 0, MESH_DEV - 1).astype(jnp.int32),
        "enc_proj": centred(keys[10], (L, L), L ** -0.5, 0.25),
        "node_proj": centred(keys[11], (L, L), L ** -0.5, 0.25),
        "dec_proj": centred(keys[12], (L, L), L ** -0.5, 0.25),
        "enc_feat_w": centred(keys[13], (L, EFEAT), EFEAT ** -0.5, 3.0, (), jnp.float32),
        "dec_feat_w": centred(keys[14], (L, EFEAT), EFEAT ** -0.5, 3.0, (), jnp.float32),
    }


def silu_grad(value):
    sig = jax.nn.sigmoid(value)
    return sig * (1.0 + value * (1.0 - sig))

def reference(grid_latent, mesh_latent, grid_cotangent, enc_sender, enc_receiver, enc_feat, enc_count, dec_sender, dec_feat, serve_rows, enc_proj, node_proj, dec_proj, enc_feat_w, dec_feat_w):
    highest = lax.Precision.HIGHEST
    owners = jnp.arange(N_LAT, dtype=jnp.int32)[:, None, None] * MESH_DEV + serve_rows
    table = jnp.transpose(owners, (1, 0, 2)).reshape(N_LAT, WIN).astype(jnp.int32)
    px = jnp.dot(grid_latent, enc_proj, preferred_element_type=jnp.float32).astype(jnp.bfloat16)
    px_bands = px.reshape(N_LAT, GRID_DEV, L)
    send_bands = enc_sender.reshape(N_LAT, ENC_CAP)
    recv_bands = enc_receiver.reshape(N_LAT, ENC_CAP)
    feat_bands = jnp.transpose(enc_feat.reshape(EFEAT, N_LAT, ENC_CAP), (1, 0, 2))
    enc_xs = (px_bands, send_bands, recv_bands, feat_bands, enc_count, table)

    def enc_band(item):
        px_band, sends, recvs, feats, count, slots = item
        pre = jnp.take(px_band, sends, axis=0).astype(jnp.float32) + jnp.einsum('fe,lf->el', feats, enc_feat_w, precision=highest)
        live = (jnp.arange(ENC_CAP, dtype=jnp.int32) < count)[:, None]
        nodes = jnp.take(slots, recvs, axis=0)
        return (pre, live, nodes)

    def enc_forward(agg, item):
        pre, live, nodes = enc_band(item)
        message = jnp.where(live, jax.nn.silu(pre), 0.0).astype(jnp.bfloat16)
        return (agg.at[nodes].add(message.astype(jnp.float32)), None)
    agg, _ = lax.scan(enc_forward, jnp.zeros((MESH, L), jnp.float32), enc_xs)
    act = jax.nn.silu(agg).astype(jnp.bfloat16)
    hmesh = (mesh_latent.astype(jnp.float32) + jnp.dot(act, node_proj, preferred_element_type=jnp.float32)).astype(jnp.bfloat16)
    proj = jnp.dot(hmesh, dec_proj, preferred_element_type=jnp.float32).astype(jnp.bfloat16)
    cot_bands = grid_cotangent.reshape(N_LAT, GRID_DEV, L)
    dsend_bands = jnp.transpose(dec_sender.reshape(3, N_LAT, GRID_DEV), (1, 0, 2))
    dfeat_bands = jnp.transpose(dec_feat.reshape(3, EFEAT, N_LAT, GRID_DEV), (2, 0, 1, 3))

    def dec_backward(carry, item):
        dproj, dfw = carry
        cot, sends, feats, slots = item
        for k in range(3):
            nodes = jnp.take(slots, sends[k], axis=0)
            pre = jnp.take(proj, nodes, axis=0).astype(jnp.float32) + jnp.einsum('fg,lf->gl', feats[k], dec_feat_w, precision=highest)
            grad = (cot.astype(jnp.float32) * silu_grad(pre)).astype(jnp.bfloat16).astype(jnp.float32)
            dproj = dproj.at[nodes].add(grad)
            dfw = dfw + jnp.einsum('gl,fg->lf', grad, feats[k], precision=highest)
        return ((dproj, dfw), None)
    start = (jnp.zeros((MESH, L), jnp.float32), jnp.zeros((L, EFEAT), jnp.float32))
    (dproj, dec_feat_w_grad), _ = lax.scan(dec_backward, start, (cot_bands, dsend_bands, dfeat_bands, table))
    dhmesh = jnp.dot(dproj, dec_proj.astype(jnp.float32).T, precision=highest)
    dec_proj_grad = jnp.dot(hmesh.astype(jnp.float32).T, dproj, precision=highest)
    mesh_grad = dhmesh.astype(jnp.bfloat16)
    node_proj_grad = jnp.dot(act.T, mesh_grad, preferred_element_type=jnp.float32)
    dagg = (jnp.dot(mesh_grad, node_proj.T, preferred_element_type=jnp.float32) * silu_grad(agg)).astype(jnp.bfloat16)

    def enc_backward(dew, item):
        pre, live, nodes = enc_band(item)
        upstream = jnp.take(dagg, nodes, axis=0).astype(jnp.float32)
        grad = jnp.where(live, upstream * silu_grad(pre), 0.0).astype(jnp.bfloat16).astype(jnp.float32)
        dew = dew + jnp.einsum('el,fe->lf', grad, item[3], precision=highest)
        dpx_band = jnp.zeros((GRID_DEV, L), jnp.float32).at[item[1]].add(grad)
        return (dew, dpx_band)
    enc_feat_w_grad, dpx_bands = lax.scan(enc_backward, jnp.zeros((L, EFEAT), jnp.float32), enc_xs)
    dpx = dpx_bands.reshape(GRID, L).astype(jnp.bfloat16)
    enc_proj_grad = jnp.dot(grid_latent.T, dpx, preferred_element_type=jnp.float32)
    grid_grad = (grid_cotangent.astype(jnp.float32) + jnp.dot(dpx, enc_proj.T, preferred_element_type=jnp.float32)).astype(jnp.bfloat16)
    return (grid_grad, mesh_grad, enc_proj_grad, node_proj_grad, dec_proj_grad, enc_feat_w_grad, dec_feat_w_grad)
```

```python
import math

import jax
import jax.numpy as jnp
from jax import lax
from jax.experimental import pallas as pl
from jax.experimental.pallas import tpu as pltpu
from jax.sharding import PartitionSpec as P

BF = jnp.bfloat16
F32 = jnp.float32
HI = lax.Precision.HIGHEST
MIB = 1 << 20
TAIL = 16
NN = (((1,), (0,)), ((), ()))
NT = (((1,), (1,)), ((), ()))
TN = (((0,), (0,)), ((), ()))


def silu_grad(value):
    sig = jax.nn.sigmoid(value)
    return sig * (1.0 + value * (1.0 - sig))


def owner_plan(
    grid_latent,
    mesh_latent,
    grid_cotangent,
    enc_sender,
    enc_receiver,
    enc_feat,
    enc_count,
    dec_sender,
    dec_feat,
    serve_rows,
    enc_proj,
    node_proj,
    dec_proj,
    enc_feat_w,
    dec_feat_w,
):
    highest = lax.Precision.HIGHEST
    owners_count = lax.axis_size("lat")
    serve_flat = serve_rows.reshape(-1)
    slot_total = serve_flat.shape[0]
    per_owner = slot_total // owners_count
    mesh_rows = mesh_latent.shape[0]
    grid_rows = grid_latent.shape[0]
    width = grid_latent.shape[1]
    edge_slots = enc_sender.shape[0]
    edge_block = math.gcd(edge_slots, 512)
    grid_block = math.gcd(grid_rows, 512)
    live_count = enc_count[0]
    slot_ids = lax.iota(jnp.int32, slot_total)[:, None]
    row_ids = lax.iota(jnp.int32, grid_rows)[:, None]

    def to_window(rows):
        outgoing = jnp.take(rows, serve_flat, axis=0).reshape(owners_count, per_owner, width)
        arrived = lax.all_to_all(outgoing, "lat", split_axis=0, concat_axis=0, tiled=True)
        return arrived.reshape(slot_total, width)

    def to_owners(partial_value):
        arrived = lax.all_to_all(
            partial_value.reshape(owners_count, per_owner, width),
            "lat",
            split_axis=0,
            concat_axis=0,
            tiled=True,
        )
        return jax.ops.segment_sum(
            arrived.reshape(slot_total, width), serve_flat, num_segments=mesh_rows
        )

    px = jnp.dot(grid_latent, enc_proj, preferred_element_type=jnp.float32).astype(jnp.bfloat16)

    def enc_block(start):
        senders = lax.dynamic_slice_in_dim(enc_sender, start, edge_block)
        receivers = lax.dynamic_slice_in_dim(enc_receiver, start, edge_block)
        feats = lax.dynamic_slice_in_dim(enc_feat, start, edge_block, 1)
        pre = jnp.take(px, senders, axis=0).astype(jnp.float32) + jnp.einsum(
            "fb,lf->bl", feats, enc_feat_w, precision=highest
        )
        live = (lax.iota(jnp.int32, edge_block) + start < live_count)[:, None]
        onehot = (receivers[None, :] == slot_ids).astype(jnp.bfloat16)
        return (pre, live, onehot, senders, feats)

    block_steps = edge_slots // edge_block

    def enc_forward(index, partial_value):
        pre, live, onehot, senders, feats = enc_block(index * edge_block)
        message = jnp.where(live, jax.nn.silu(pre), 0.0).astype(jnp.bfloat16)
        return partial_value + jnp.dot(onehot, message, preferred_element_type=jnp.float32)

    enc_partial = lax.fori_loop(
        0, block_steps, enc_forward, jnp.zeros((slot_total, width), jnp.float32)
    )
    agg = to_owners(enc_partial)
    act = jax.nn.silu(agg).astype(jnp.bfloat16)
    hmesh = (
        mesh_latent.astype(jnp.float32)
        + jnp.dot(act, node_proj, preferred_element_type=jnp.float32)
    ).astype(jnp.bfloat16)
    proj_window = to_window(
        jnp.dot(hmesh, dec_proj, preferred_element_type=jnp.float32).astype(jnp.bfloat16)
    )

    def dec_backward(index, carry):
        dproj, dfw = carry
        start = index * grid_block
        cot = lax.dynamic_slice_in_dim(grid_cotangent, start, grid_block).astype(jnp.float32)
        for k in range(3):
            senders = lax.dynamic_slice_in_dim(dec_sender[k], start, grid_block)
            feats = lax.dynamic_slice_in_dim(dec_feat[k], start, grid_block, 1)
            pre = jnp.take(proj_window, senders, axis=0).astype(jnp.float32) + jnp.einsum(
                "fg,lf->gl", feats, dec_feat_w, precision=highest
            )
            grad_half = (cot * silu_grad(pre)).astype(jnp.bfloat16)
            slot_hot = (senders[None, :] == slot_ids).astype(jnp.bfloat16)
            dproj = dproj + jnp.dot(slot_hot, grad_half, preferred_element_type=jnp.float32)
            dfw = dfw + jnp.einsum(
                "gl,fg->lf", grad_half.astype(jnp.float32), feats, precision=highest
            )
        return (dproj, dfw)

    start_carry = (
        jnp.zeros((slot_total, width), jnp.float32),
        jnp.zeros((width, dec_feat_w.shape[1]), jnp.float32),
    )
    dproj_window, dec_fw_part = lax.fori_loop(0, grid_rows // grid_block, dec_backward, start_carry)
    dec_weight = dec_proj.astype(jnp.float32)
    dproj = to_owners(dproj_window)
    dhmesh = jnp.dot(dproj, dec_weight.T, precision=highest)
    dec_proj_part = jnp.dot(hmesh.astype(jnp.float32).T, dproj, precision=highest)
    mesh_grad = dhmesh.astype(jnp.bfloat16)
    node_proj_part = jnp.dot(act.T, mesh_grad, preferred_element_type=jnp.float32)
    dagg = (
        jnp.dot(mesh_grad, node_proj.T, preferred_element_type=jnp.float32) * silu_grad(agg)
    ).astype(jnp.bfloat16)
    dagg_window = to_window(dagg)

    def enc_backward(index, carry):
        dpx, dew = carry
        pre, live, onehot, senders, feats = enc_block(index * edge_block)
        upstream = jnp.einsum("wb,wl->bl", onehot, dagg_window, preferred_element_type=jnp.float32)
        grad_half = jnp.where(live, upstream * silu_grad(pre), 0.0).astype(jnp.bfloat16)
        row_hot = (senders[None, :] == row_ids).astype(jnp.bfloat16)
        dpx = dpx + jnp.dot(row_hot, grad_half, preferred_element_type=jnp.float32)
        dew = dew + jnp.einsum("bl,fb->lf", grad_half.astype(jnp.float32), feats, precision=highest)
        return (dpx, dew)

    start_back = (
        jnp.zeros((grid_rows, width), jnp.float32),
        jnp.zeros((width, enc_feat_w.shape[1]), jnp.float32),
    )
    dpx_sum, enc_fw_part = lax.fori_loop(0, block_steps, enc_backward, start_back)
    dpx = dpx_sum.astype(jnp.bfloat16)
    enc_proj_part = jnp.dot(grid_latent.T, dpx, preferred_element_type=jnp.float32)
    grid_grad = (
        grid_cotangent.astype(jnp.float32)
        + jnp.dot(dpx, enc_proj.T, preferred_element_type=jnp.float32)
    ).astype(jnp.bfloat16)
    enc_proj_grad, node_proj_grad, dec_proj_grad, enc_feat_w_grad, dec_feat_w_grad = (
        lax.psum_scatter(enc_proj_part, "lat", scatter_dimension=0, tiled=True),
        lax.psum_scatter(node_proj_part, "lat", scatter_dimension=0, tiled=True),
        lax.psum_scatter(dec_proj_part, "lat", scatter_dimension=0, tiled=True),
        lax.psum_scatter(enc_fw_part, "lat", scatter_dimension=0, tiled=True),
        lax.psum_scatter(dec_fw_part, "lat", scatter_dimension=0, tiled=True),
    )
    return (
        grid_grad,
        mesh_grad,
        enc_proj_grad,
        node_proj_grad,
        dec_proj_grad,
        enc_feat_w_grad,
        dec_feat_w_grad,
    )


def mm(a, b, dims=NN, precision=None):
    return lax.dot_general(a, b, dims, precision=precision, preferred_element_type=F32)


def iota(shape, dim):
    return lax.broadcasted_iota(jnp.int32, shape, dim)


def sigmoid(value):
    return 0.5 * jnp.tanh(0.5 * value) + 0.5


def hot(mask):
    return jnp.where(mask, 1.0, 0.0).astype(BF)


def split3(value):
    high = value.astype(BF).astype(F32)
    rest = value - high
    middle = rest.astype(BF).astype(F32)
    return high, middle, rest - middle


def stack_terms(value, order):
    feats = value.shape[0]
    rows = -(-6 * feats // 16) * 16
    pick = (iota((rows, feats), 0) % feats == iota((rows, feats), 1)).astype(F32)
    spread = mm(pick, value, precision=HI)
    parts = split3(spread)
    group = iota(spread.shape, 0) // feats
    out = jnp.zeros_like(spread)
    for index, which in enumerate(order):
        out = jnp.where(group == index, parts[which], out)
    return out.astype(BF)


FEAT_ORDER = (0, 0, 1, 1, 2, 0)
WEIGHT_ORDER = (0, 1, 0, 1, 0, 2)


def weight_rows(weight):
    feats = weight.shape[1]
    eye = (iota((8, feats), 0) == iota((8, feats), 1)).astype(F32)
    return stack_terms(mm(eye, weight, NT, HI)[:feats], WEIGHT_ORDER)


def feature_grad(terms, feats):
    pick = iota((8, terms.shape[0]), 1)
    row = iota((8, terms.shape[0]), 0)
    want = (pick % feats == row) & (row < feats)
    want = want & ((pick // feats == 0) | (pick // feats == 2) | (pick // feats == 4))
    return mm(want.astype(F32), terms, precision=HI)


def encoder_kernel(count, latent, weight, send, receive, feat, feat_w, extra, message, slope, px):
    edges = send.shape[1]
    grid_rows = latent.shape[0]
    slots = message.shape[1] - TAIL
    block = math.gcd(edges, 512)
    px[...] = mm(latent[...], weight[...]).astype(BF)
    w_rows = weight_rows(feat_w[...])
    total = jnp.zeros((slots, latent.shape[1]), F32)
    for start in range(0, edges, block):
        part = slice(start, start + block)
        ids = jnp.broadcast_to(send[:, part].astype(F32), (128, block)).T
        picks = [
            hot(ids == (iota((block, 128), 1) + base).astype(F32))
            for base in range(0, grid_rows, 128)
        ]
        pre = mm(jnp.concatenate(picks, 1), px[...])
        pre = pre + mm(stack_terms(feat[:, part], FEAT_ORDER), w_rows, TN)
        sig = sigmoid(pre)
        silu = pre * sig
        slope[part, :] = (sig + silu * (1.0 - sig)).astype(BF)
        live = iota((1, block), 1) + start < count[0]
        slot = jnp.where(live, receive[:, part], -1)
        to_slot = hot(iota((slots, block), 0) == slot)
        total = total + mm(to_slot, silu.astype(BF))
    half = total.astype(BF)
    for chip in range(message.shape[0]):
        message[chip, :slots, :] = half
        message[chip, slots:, :] = extra[chip]


def gathered_rows(piece, chips, rows, core, cap, shape, dim):
    index = iota(shape, dim)
    chip = lax.div(index, rows)
    slot = index - chip * rows
    band = 2 * chip + jnp.where(piece == 0, core, 1 - core)
    return band, slot, lax.div(slot, cap)


def slot_matches(first, second, me, cap, mesh_rows):
    chips, rows = first.shape[0], first.shape[1]
    span = chips * rows
    slots = rows - TAIL
    owners = 2 * chips
    core = lax.rem(me, 2)
    flat = [ref[...].reshape(span, -1) for ref in (first, second)]
    table = jnp.zeros((owners, 256), F32)
    for piece in range(2):
        shape = (owners, span)
        at = (iota(shape, 0) - piece * chips) * rows + slots + 2 * cap
        table = table + mm(hot(iota(shape, 1) == at), flat[piece][:, :256])
    digits = jnp.concatenate([table[:, :128], table[:, 128:]], 0).astype(BF)
    half = iota((slots, 2 * owners), 1)
    holder = half % owners
    holder = 2 * (holder % chips) + jnp.where(holder < chips, core, 1 - core)
    wanted = holder == lax.div(iota((slots, 2 * owners), 0), cap)
    mine = 256.0 * mm(hot(wanted & (half < owners)), digits) + mm(hot(wanted & (half >= owners)), digits)
    lane = cap * me + iota((slots, 128), 0) % cap
    own_key = jnp.sum(jnp.where(iota((slots, 128), 1) == lane, mine, 0.0), 1, keepdims=True)
    own_key = own_key + (lax.div(iota((slots, 1), 0), cap) * mesh_rows).astype(F32)
    keys, same, served = [], [], []
    for piece in range(2):
        band, slot, owner = gathered_rows(piece, chips, rows, core, cap, (1, span), 1)
        spread = mm(digits, hot(iota((128, span), 0) == cap * band + slot % cap))
        value = 256.0 * spread[:owners] + spread[owners:]
        holder = iota((owners, 1), 0)
        holder = 2 * (holder % chips) + jnp.where(holder < chips, core, 1 - core)
        value = jnp.sum(jnp.where(holder == owner, value, 0.0), 0, keepdims=True)
        key = jnp.where(slot < slots, value + (owner * mesh_rows).astype(F32), -1.0)
        keys.append(key)
        same.append(hot(key == own_key))
        window = iota((slots, 1), 0)
        row = slots + cap * core + window % cap
        served.append(hot((band == lax.div(window, cap)) & (slot == row)))
    return flat, keys, same, served


def decoder_body(proj, send, feat, feat_w, cotangent):
    slots = proj.shape[0]
    grid_rows = cotangent.shape[0]
    block = math.gcd(grid_rows, 512)
    table = jnp.concatenate([proj, weight_rows(feat_w[...])], 0)
    total = jnp.zeros((table.shape[0], proj.shape[1]), F32)
    for start in range(0, grid_rows, block):
        part = slice(start, start + block)
        cot = cotangent[part, :].astype(F32)
        for k in range(3):
            to_slot = hot(iota((slots, block), 0) == send[k : k + 1, part])
            pick = jnp.concatenate([to_slot, stack_terms(feat[k, :, part], FEAT_ORDER)], 0)
            pre = mm(pick, table, TN)
            sig = sigmoid(pre)
            slope = sig + pre * sig * (1.0 - sig)
            total = total + mm(pick, (cot * slope).astype(BF))
    return total


def decoder_kernel(
    cap, mesh_rows, place, first, second, node_w, dec_w, send, feat, feat_w, cotangent, extra,
    message, keys_out, same_out, slope_out,
):
    slots = first.shape[1] - TAIL
    flat, keys, same, served = slot_matches(first, second, place[0], cap, mesh_rows)
    both = jnp.zeros((2 * slots, first.shape[2]), F32)
    for piece in range(2):
        keys_out[piece : piece + 1, :] = keys[piece]
        same_out[piece] = same[piece]
        both = both + mm(jnp.concatenate([same[piece], served[piece]], 0), flat[piece])
    agg, latent = both[:slots], both[slots:]
    sig = sigmoid(agg)
    silu = agg * sig
    slope_out[...] = sig + silu * (1.0 - sig)
    hmesh = (latent + mm(silu.astype(BF), node_w[...])).astype(BF)
    proj = mm(hmesh, dec_w[...]).astype(BF)
    total = decoder_body(proj, send, feat, feat_w, cotangent)
    feats = feat_w.shape[1]
    half = total[:slots].astype(BF)
    grad = feature_grad(total[slots:], feats).astype(BF)
    for chip in range(message.shape[0]):
        message[chip, :slots, :] = half
        message[chip, slots:, :] = jnp.concatenate([grad, extra[chip]], 0)


def backward_kernel(
    place, count, first, second, same, agg_slope, node_w, dec_w, send, receive, feat, slope, latent,
    dpx_out, keep, give, hots, grads, part,
):
    slots = same.shape[1]
    edges = send.shape[1]
    grid_rows, width = latent.shape
    feats = feat.shape[0]
    core = lax.rem(place[0], 2)
    dproj = mm(same[0], first[...].reshape(-1, width)) + mm(same[1], second[...].reshape(-1, width))
    high = dproj.astype(BF)
    low = (dproj - high.astype(F32)).astype(BF)
    dhmesh = mm(jnp.concatenate([high, low], 0), dec_w[...], NT)
    mesh_grad = (dhmesh[:slots] + dhmesh[slots:]).astype(BF)
    dagg = (mm(mesh_grad, node_w[...], NT) * agg_slope[...]).astype(BF)
    block = math.gcd(edges, 512)
    for start in range(0, edges, block):
        cut = slice(start, start + block)
        live = iota((1, block), 1) + start < count[0]
        slot = jnp.where(live, receive[:, cut], -1)
        upstream = mm(hot(iota((slots, block), 0) == slot), dagg, TN)
        grads[cut, :] = (upstream * slope[cut, :].astype(F32)).astype(BF)
        hots[:grid_rows, cut] = hot(iota((grid_rows, block), 0) == send[:, cut])
        hots[grid_rows:, cut] = stack_terms(feat[:, cut], FEAT_ORDER)
    step = math.gcd(grid_rows, 256)
    for start in range(0, grid_rows, step):
        cut = slice(start, start + step)
        dpx_out[cut, :] = mm(hots[cut, :], grads[...]).astype(BF)
    terms = mm(hots[grid_rows:, :], grads[...])
    pick = iota((128, terms.shape[0]), 1)
    row = iota((128, terms.shape[0]), 0)
    want = (pick % feats == row) & (row < feats)
    group = lax.div(pick, feats)
    want = want & ((group == 0) | (group == 2) | (group == 4))
    part[:, width:] = mm(want.astype(F32), terms, precision=HI).T
    part[:, :width] = mm(latent[...], dpx_out[...], TN)
    chips, rows = keep.shape[0], keep.shape[1]
    for chip in range(chips):
        keep[chip] = part[pl.ds((2 * chip + core) * rows, rows), :]
        give[chip] = part[pl.ds((2 * chip + 1 - core) * rows, rows), :].astype(BF)


def weight_kernel(
    cap, mesh_rows, feats, place, first, second, first_back, second_back, keys, node_w, dec_w,
    mesh_out, dec_out, node_out, feat_out,
):
    chips, rows, width = first.shape
    slots = rows - TAIL
    span = chips * rows
    owners = 2 * chips
    me = place[0]
    core = lax.rem(me, 2)
    block = width // owners
    forward = jnp.concatenate([first[...].reshape(span, width), second[...].reshape(span, width)], 0)
    back = jnp.concatenate([first_back[...].reshape(span, width), second_back[...].reshape(span, width)], 0)
    key = jnp.concatenate([keys[0:1, :], keys[1:2, :]], 1)
    down = jnp.broadcast_to(key, (128, 2 * span)).T
    down = jnp.where(down < 0.0, -2.0, down)
    same = jnp.concatenate([hot(down == key[:, base : base + 128]) for base in range(0, 2 * span, 128)], 1)
    agg = mm(same, forward)
    act = (agg * sigmoid(agg)).astype(BF)
    shape = (width, 128)
    mine = hot((iota(shape, 0) == block * me + iota(shape, 1)) & (iota(shape, 1) < block))
    node_cols = mm(node_w[...], mine).astype(BF)
    both = mm(act, jnp.concatenate([node_cols, mine], 1))
    pieces = [gathered_rows(piece, chips, rows, core, cap, (span, 1), 0) for piece in range(2)]
    band, slot, owner = [jnp.concatenate([a, b], 0) for a, b in zip(*pieces)]
    number = cap * band + slot % cap
    source = jnp.where(lax.rem(owner, 2) == core, 0, chips) + lax.div(owner, 2)
    at = jnp.where(slot < slots, source * TAIL + TAIL - 2 * cap + lax.div(number, chips), -1)
    tails = jnp.concatenate(
        [ref[chip, slots:, :] for ref in (first_back, second_back) for chip in range(chips)], 0
    )
    shape = (2 * span, tails.shape[0])
    wide = mm(hot(iota(shape, 1) == at), tails)
    shape = (2 * span, width)
    wide = jnp.where(lax.div(iota(shape, 1), 2 * block) == lax.rem(number, chips), wide, 0.0).astype(BF)
    shape = (width, 128)
    fold = hot((iota(shape, 0) % (2 * block) == block * core + iota(shape, 1)) & (iota(shape, 1) < block))
    hmesh = (both[:, :128] + mm(wide, fold)).astype(BF)
    left = jnp.concatenate([hmesh, both[:, 128:].astype(BF)], 1)
    sums = mm(left, back, TN)
    dec_out[...] = sums[:block]
    lead = sums[128 : 128 + block]
    high = lead.astype(BF)
    low = (lead - high.astype(F32)).astype(BF)
    node_out[...] = mm(high, dec_w[...], NT) + mm(low, dec_w[...], NT)
    shape = (8, 2 * span)
    index = lax.rem(iota(shape, 1), rows)
    feat_out[...] = mm(hot((index == slots + iota(shape, 0)) & (iota(shape, 0) < feats)), back)
    mesh = mesh_out.shape[0]
    shape = (mesh, 2 * span)
    own = (me * mesh_rows + iota(shape, 0)).astype(F32)
    dproj = mm(hot(own == key), back)
    high = dproj.astype(BF)
    low = (dproj - high.astype(F32)).astype(BF)
    mesh_out[...] = (mm(high, dec_w[...], NT) + mm(low, dec_w[...], NT)).astype(BF)


SMEM = pl.BlockSpec(memory_space=pltpu.SMEM)
VMEM = pl.BlockSpec(memory_space=pltpu.VMEM)


def kernel_call(body, name, scalars, arrays, outs, scratch, flops, limit):
    shapes = [jax.ShapeDtypeStruct(shape, dtype) for shape, dtype in outs]
    moved = sum(a.size * a.dtype.itemsize for a in arrays) + sum(s.size * s.dtype.itemsize for s in shapes)
    return pl.pallas_call(
        body,
        name=name,
        out_shape=shapes,
        in_specs=[SMEM] * len(scalars) + [VMEM] * len(arrays),
        out_specs=[VMEM] * len(shapes),
        scratch_shapes=scratch,
        compiler_params=pltpu.CompilerParams(vmem_limit_bytes=limit * MIB),
        cost_estimate=pl.CostEstimate(flops=flops, bytes_accessed=moved, transcendentals=0),
    )(*scalars, *arrays)


def gather_plan(
    grid_latent,
    mesh_latent,
    grid_cotangent,
    enc_sender,
    enc_receiver,
    enc_feat,
    enc_count,
    dec_sender,
    dec_feat,
    serve_rows,
    enc_proj,
    node_proj,
    dec_proj,
    enc_feat_w,
    dec_feat_w,
):
    owners = lax.axis_size("lat")
    chips = owners // 2
    cap = serve_rows.shape[2]
    slots = owners * cap
    mesh_rows, width = mesh_latent.shape
    grid_rows = grid_latent.shape[0]
    edges = enc_sender.shape[0]
    feats = enc_feat.shape[0]
    block = width // owners
    rows = slots + TAIL
    span = chips * rows
    groups = [[core + 2 * chip for chip in range(chips)] for core in range(2)]
    swap = [(index, index ^ 1) for index in range(owners)]
    place = lax.axis_index("lat").astype(jnp.int32).reshape(1)

    def gather(message):
        first = lax.all_to_all(message, "lat", 0, 0, tiled=True, axis_index_groups=groups)
        return first, lax.ppermute(first, "lat", swap)

    served_ids = serve_rows.reshape(1, slots)
    served = jnp.take(mesh_latent, served_ids[0], axis=0)
    id_row = jnp.zeros((1, width), jnp.int32)
    id_row = lax.dynamic_update_slice(id_row, served_ids // 256, (0, 0))
    id_row = lax.dynamic_update_slice(id_row, served_ids % 256, (0, 128))
    own_rows = served.reshape(chips, 2 * cap, width)
    id_rows = jnp.broadcast_to(id_row.astype(BF)[None], (chips, 1, width))
    extra = jnp.concatenate([own_rows, id_rows, jnp.zeros((chips, TAIL - 2 * cap - 1, width), BF)], 1)
    columns = served.reshape(slots, chips, 2 * block).transpose(1, 0, 2).reshape(chips, 2 * cap, width)

    send = enc_sender.reshape(1, edges)
    receive = enc_receiver.reshape(1, edges)
    message, slope = kernel_call(
        encoder_kernel,
        "encoder",
        [enc_count],
        [grid_latent, enc_proj, send, receive, enc_feat, enc_feat_w, extra],
        [((chips, rows, width), BF), ((edges, width), BF)],
        [pltpu.VMEM((grid_rows, width), BF)],
        2 * edges * grid_rows * width,
        32,
    )
    first, second = gather(message)
    message, keys, same, agg_slope = kernel_call(
        lambda *refs: decoder_kernel(cap, mesh_rows, *refs),
        "decoder",
        [place],
        [first, second, node_proj, dec_proj, dec_sender, dec_feat, dec_feat_w, grid_cotangent, columns],
        [((chips, rows, width), BF), ((2, span), F32), ((2, slots, span), BF), ((slots, width), F32)],
        [],
        24 * grid_rows * 128 * width,
        32,
    )
    first_back, second_back = gather(message)
    wide = width + 128
    term_rows = -(-6 * feats // 16) * 16
    dpx, keep, give = kernel_call(
        backward_kernel,
        "backward",
        [place, enc_count],
        [first_back, second_back, same, agg_slope, node_proj, dec_proj, send, receive, enc_feat, slope, grid_latent],
        [((grid_rows, width), BF), ((chips, block, wide), F32), ((chips, block, wide), BF)],
        [
            pltpu.VMEM((grid_rows + term_rows, edges), BF),
            pltpu.VMEM((edges, width), BF),
            pltpu.VMEM((width, wide), F32),
        ],
        2 * edges * grid_rows * width,
        32,
    )
    pair = (keep + lax.ppermute(give, "lat", swap).astype(F32)).astype(BF)
    arrived = lax.all_to_all(pair, "lat", 0, 0, tiled=True, axis_index_groups=groups)
    mesh_grad, dec_proj_grad, node_proj_grad, dec_feat_sum = kernel_call(
        lambda *refs: weight_kernel(cap, mesh_rows, feats, *refs),
        "weights",
        [place],
        [first, second, first_back, second_back, keys, node_proj, dec_proj],
        [((mesh_rows, width), BF), ((block, width), F32), ((block, width), F32), ((8, width), F32)],
        [],
        2 * (2 * span) * (2 * span) * width,
        32,
    )
    grid_grad = (
        grid_cotangent.astype(F32) + lax.dot_general(dpx, enc_proj, NT, preferred_element_type=F32)
    ).astype(BF)
    total = jnp.sum(arrived.astype(F32), axis=0)
    dec_feat_w_grad = lax.dynamic_slice(dec_feat_sum, (0, place[0] * block), (feats, block)).T
    return (
        grid_grad,
        mesh_grad,
        total[:, :width],
        node_proj_grad,
        dec_proj_grad,
        total[:, width : width + feats],
        dec_feat_w_grad,
    )


def gather_fits(args):
    mesh_latent, serve_rows = args[1], args[9]
    owners, cap = serve_rows.shape[1], serve_rows.shape[2]
    width = mesh_latent.shape[1]
    return (
        owners * cap <= 128
        and owners % 8 == 0
        and cap == 4
        and width % (128 * owners // 8) == 0
        and mesh_latent.shape[0] <= 65536
        and mesh_latent.shape[0] * owners < 1 << 24
        and args[0].shape[0] % 128 == 0
        and args[3].shape[0] % 128 == 0
        and args[5].shape[0] == 4
    )


def per_device(*args):
    return gather_plan(*args) if gather_fits(args) else owner_plan(*args)


def solution(mesh):
    placed = (
        P(("member", "lat"), None),
        P(("member", "lat"), None),
        P(("member", "lat"), None),
        P(("member", "lat")),
        P(("member", "lat")),
        P(None, ("member", "lat")),
        P(("member", "lat")),
        P(None, ("member", "lat")),
        P(None, None, ("member", "lat")),
        P(("member", "lat"), None, None),
        P(),
        P(),
        P(),
        P(),
        P(),
    )
    return jax.shard_map(
        per_device,
        mesh=mesh,
        in_specs=placed,
        out_specs=(
            P(("member", "lat"), None),
            P(("member", "lat"), None),
            P(("member", "lat"), None),
            P(("member", "lat"), None),
            P(("member", "lat"), None),
            P(("member", "lat"), None),
            P(("member", "lat"), None),
        ),
        check_vma=False,
    )
```

```python
import math

import jax
import jax.numpy as jnp
from jax import lax
from jax.experimental import pallas as pl
from jax.experimental.pallas import tpu as pltpu
from jax.sharding import PartitionSpec as P

BF = jnp.bfloat16
F32 = jnp.float32
HI = lax.Precision.HIGHEST
MIB = 1 << 20
NN = (((1,), (0,)), ((), ()))
NT = (((1,), (1,)), ((), ()))
TN = (((0,), (0,)), ((), ()))


def silu_grad(value):
    sig = jax.nn.sigmoid(value)
    return sig * (1.0 + value * (1.0 - sig))


def owner_plan(
    grid_latent,
    mesh_latent,
    grid_cotangent,
    enc_sender,
    enc_receiver,
    enc_feat,
    enc_count,
    dec_sender,
    dec_feat,
    serve_rows,
    enc_proj,
    node_proj,
    dec_proj,
    enc_feat_w,
    dec_feat_w,
):
    highest = lax.Precision.HIGHEST
    owners_count = lax.axis_size("lat")
    serve_flat = serve_rows.reshape(-1)
    slot_total = serve_flat.shape[0]
    per_owner = slot_total // owners_count
    mesh_rows = mesh_latent.shape[0]
    grid_rows = grid_latent.shape[0]
    width = grid_latent.shape[1]
    edge_slots = enc_sender.shape[0]
    edge_block = math.gcd(edge_slots, 512)
    grid_block = math.gcd(grid_rows, 512)
    live_count = enc_count[0]
    slot_ids = lax.iota(jnp.int32, slot_total)[:, None]
    row_ids = lax.iota(jnp.int32, grid_rows)[:, None]

    def to_window(rows):
        outgoing = jnp.take(rows, serve_flat, axis=0).reshape(owners_count, per_owner, width)
        arrived = lax.all_to_all(outgoing, "lat", split_axis=0, concat_axis=0, tiled=True)
        return arrived.reshape(slot_total, width)

    def to_owners(partial_value):
        arrived = lax.all_to_all(
            partial_value.reshape(owners_count, per_owner, width),
            "lat",
            split_axis=0,
            concat_axis=0,
            tiled=True,
        )
        return jax.ops.segment_sum(
            arrived.reshape(slot_total, width), serve_flat, num_segments=mesh_rows
        )

    px = jnp.dot(grid_latent, enc_proj, preferred_element_type=jnp.float32).astype(jnp.bfloat16)

    def enc_block(start):
        senders = lax.dynamic_slice_in_dim(enc_sender, start, edge_block)
        receivers = lax.dynamic_slice_in_dim(enc_receiver, start, edge_block)
        feats = lax.dynamic_slice_in_dim(enc_feat, start, edge_block, 1)
        pre = jnp.take(px, senders, axis=0).astype(jnp.float32) + jnp.einsum(
            "fb,lf->bl", feats, enc_feat_w, precision=highest
        )
        live = (lax.iota(jnp.int32, edge_block) + start < live_count)[:, None]
        onehot = (receivers[None, :] == slot_ids).astype(jnp.bfloat16)
        return (pre, live, onehot, senders, feats)

    block_steps = edge_slots // edge_block

    def enc_forward(index, partial_value):
        pre, live, onehot, senders, feats = enc_block(index * edge_block)
        message = jnp.where(live, jax.nn.silu(pre), 0.0).astype(jnp.bfloat16)
        return partial_value + jnp.dot(onehot, message, preferred_element_type=jnp.float32)

    enc_partial = lax.fori_loop(
        0, block_steps, enc_forward, jnp.zeros((slot_total, width), jnp.float32)
    )
    agg = to_owners(enc_partial)
    act = jax.nn.silu(agg).astype(jnp.bfloat16)
    hmesh = (
        mesh_latent.astype(jnp.float32)
        + jnp.dot(act, node_proj, preferred_element_type=jnp.float32)
    ).astype(jnp.bfloat16)
    proj_window = to_window(
        jnp.dot(hmesh, dec_proj, preferred_element_type=jnp.float32).astype(jnp.bfloat16)
    )

    def dec_backward(index, carry):
        dproj, dfw = carry
        start = index * grid_block
        cot = lax.dynamic_slice_in_dim(grid_cotangent, start, grid_block).astype(jnp.float32)
        for k in range(3):
            senders = lax.dynamic_slice_in_dim(dec_sender[k], start, grid_block)
            feats = lax.dynamic_slice_in_dim(dec_feat[k], start, grid_block, 1)
            pre = jnp.take(proj_window, senders, axis=0).astype(jnp.float32) + jnp.einsum(
                "fg,lf->gl", feats, dec_feat_w, precision=highest
            )
            grad_half = (cot * silu_grad(pre)).astype(jnp.bfloat16)
            slot_hot = (senders[None, :] == slot_ids).astype(jnp.bfloat16)
            dproj = dproj + jnp.dot(slot_hot, grad_half, preferred_element_type=jnp.float32)
            dfw = dfw + jnp.einsum(
                "gl,fg->lf", grad_half.astype(jnp.float32), feats, precision=highest
            )
        return (dproj, dfw)

    start_carry = (
        jnp.zeros((slot_total, width), jnp.float32),
        jnp.zeros((width, dec_feat_w.shape[1]), jnp.float32),
    )
    dproj_window, dec_fw_part = lax.fori_loop(0, grid_rows // grid_block, dec_backward, start_carry)
    dec_weight = dec_proj.astype(jnp.float32)
    dproj = to_owners(dproj_window)
    dhmesh = jnp.dot(dproj, dec_weight.T, precision=highest)
    dec_proj_part = jnp.dot(hmesh.astype(jnp.float32).T, dproj, precision=highest)
    mesh_grad = dhmesh.astype(jnp.bfloat16)
    node_proj_part = jnp.dot(act.T, mesh_grad, preferred_element_type=jnp.float32)
    dagg = (
        jnp.dot(mesh_grad, node_proj.T, preferred_element_type=jnp.float32) * silu_grad(agg)
    ).astype(jnp.bfloat16)
    dagg_window = to_window(dagg)

    def enc_backward(index, carry):
        dpx, dew = carry
        pre, live, onehot, senders, feats = enc_block(index * edge_block)
        upstream = jnp.einsum("wb,wl->bl", onehot, dagg_window, preferred_element_type=jnp.float32)
        grad_half = jnp.where(live, upstream * silu_grad(pre), 0.0).astype(jnp.bfloat16)
        row_hot = (senders[None, :] == row_ids).astype(jnp.bfloat16)
        dpx = dpx + jnp.dot(row_hot, grad_half, preferred_element_type=jnp.float32)
        dew = dew + jnp.einsum("bl,fb->lf", grad_half.astype(jnp.float32), feats, precision=highest)
        return (dpx, dew)

    start_back = (
        jnp.zeros((grid_rows, width), jnp.float32),
        jnp.zeros((width, enc_feat_w.shape[1]), jnp.float32),
    )
    dpx_sum, enc_fw_part = lax.fori_loop(0, block_steps, enc_backward, start_back)
    dpx = dpx_sum.astype(jnp.bfloat16)
    enc_proj_part = jnp.dot(grid_latent.T, dpx, preferred_element_type=jnp.float32)
    grid_grad = (
        grid_cotangent.astype(jnp.float32)
        + jnp.dot(dpx, enc_proj.T, preferred_element_type=jnp.float32)
    ).astype(jnp.bfloat16)
    enc_proj_grad, node_proj_grad, dec_proj_grad, enc_feat_w_grad, dec_feat_w_grad = (
        lax.psum_scatter(enc_proj_part, "lat", scatter_dimension=0, tiled=True),
        lax.psum_scatter(node_proj_part, "lat", scatter_dimension=0, tiled=True),
        lax.psum_scatter(dec_proj_part, "lat", scatter_dimension=0, tiled=True),
        lax.psum_scatter(enc_fw_part, "lat", scatter_dimension=0, tiled=True),
        lax.psum_scatter(dec_fw_part, "lat", scatter_dimension=0, tiled=True),
    )
    return (
        grid_grad,
        mesh_grad,
        enc_proj_grad,
        node_proj_grad,
        dec_proj_grad,
        enc_feat_w_grad,
        dec_feat_w_grad,
    )


def mm(a, b, dims=NN, precision=None):
    return lax.dot_general(a, b, dims, precision=precision, preferred_element_type=F32)


def iota(shape, dim):
    return lax.broadcasted_iota(jnp.int32, shape, dim)


def sigmoid(value):
    return 0.5 * jnp.tanh(0.5 * value) + 0.5


def hot(mask):
    return jnp.where(mask, 1.0, 0.0).astype(BF)


def split3(value):
    high = value.astype(BF).astype(F32)
    rest = value - high
    middle = rest.astype(BF).astype(F32)
    return high, middle, rest - middle


def stack_terms(value, order):
    feats = value.shape[0]
    rows = -(-6 * feats // 16) * 16
    pick = (iota((rows, feats), 0) % feats == iota((rows, feats), 1)).astype(F32)
    spread = mm(pick, value, precision=HI)
    parts = split3(spread)
    group = iota(spread.shape, 0) // feats
    out = jnp.zeros_like(spread)
    for index, which in enumerate(order):
        out = jnp.where(group == index, parts[which], out)
    return out.astype(BF)


FEAT_ORDER = (0, 0, 1, 1, 2, 0)
WEIGHT_ORDER = (0, 1, 0, 1, 0, 2)


def fetch(sources, targets, sems):
    copies = [pltpu.make_async_copy(src, dst, sems.at[i]) for i, (src, dst) in enumerate(zip(sources, targets))]
    for copy in copies:
        copy.start()
    return copies


def feature_grad(terms, feats):
    pick = iota((8, terms.shape[0]), 1)
    row = iota((8, terms.shape[0]), 0)
    want = (pick % feats == row) & (row < feats)
    want = want & ((pick // feats == 0) | (pick // feats == 2) | (pick // feats == 4))
    return mm(want.astype(F32), terms, precision=HI)


def encoder_kernel(
    cap, count, latent_any, weight_any, mesh_any, send_any, receive_any, feat_any, feat_w_any, serve_any,
    message, slope_far, served_out, px, picks, slope, slope_sems,
    latent, weight, mesh, send, receive, feat, feat_w, serve, sems,
):
    sources = (send_any, latent_any, weight_any, feat_any, feat_w_any, receive_any, mesh_any, serve_any)
    targets = (send, latent, weight, feat, feat_w, receive, mesh, serve)
    copies = fetch(sources, targets, sems)
    edges = send.shape[1]
    grid_rows, width = latent.shape
    chips = message.shape[0]
    slots = served_out.shape[0]
    block = math.gcd(edges, 512)
    copies[0].wait()
    for start in range(0, edges, block):
        part = slice(start, start + block)
        ids = jnp.broadcast_to(send[:, part].astype(F32), (128, block)).T
        for base in range(0, grid_rows, 128):
            lane = (iota((block, 128), 1) + base).astype(F32)
            picks[part, base : base + 128] = hot(ids == lane)
    copies[1].wait()
    copies[2].wait()
    px[...] = mm(latent[...], weight[...]).astype(BF)
    for copy in copies[3:6]:
        copy.wait()
    w_rows = stack_terms(feat_w[...], WEIGHT_ORDER)
    total = jnp.zeros((slots, width), F32)
    stores = []
    for start in range(0, edges, block):
        part = slice(start, start + block)
        pre = mm(picks[part, :], px[...])
        pre = pre + mm(stack_terms(feat[:, part], FEAT_ORDER), w_rows, TN)
        sig = sigmoid(pre)
        silu = pre * sig
        slope[part, :] = (sig + silu * (1.0 - sig)).astype(BF)
        out = pltpu.make_async_copy(slope.at[part, :], slope_far.at[part, :], slope_sems.at[len(stores)])
        out.start()
        stores.append(out)
        live = iota((1, block), 1) + start < count[0]
        slot = jnp.where(live, receive[:, part], -1)
        to_slot = hot(iota((slots, block), 0) == slot)
        total = total + mm(to_slot, silu.astype(BF))
    copies[6].wait()
    copies[7].wait()
    owners = slots // cap
    ids = serve[...]
    spread = hot(iota((owners, slots), 0) == lax.div(iota((owners, slots), 1), cap))
    turn = iota((cap, slots), 0) == iota((cap, slots), 1) % cap
    digits = []
    for value in (lax.shift_right_logical(ids, 8), ids & 255):
        wide = mm(value.astype(F32).astype(BF), spread)
        digits.append(jnp.sum(jnp.where(turn, wide, 0.0), 0, keepdims=True))
    id_row = (digits[0] * 256.0 + digits[1]).astype(jnp.int32)
    served = mm(hot(iota((mesh.shape[0], slots), 0) == id_row), mesh[...], TN)
    served_out[...] = served.astype(BF)
    lane = iota((slots, 128), 1)
    back = iota((slots, 128), 0)
    wide = mm(digits[0].astype(BF), hot(lane == back)) + mm(digits[1].astype(BF), hot(lane == back + slots))
    id_rows = jnp.where(iota((8, 128), 0) == 0, wide, 0.0)
    half = total.astype(BF)
    for chip in range(chips):
        write_slots(message, chip, half)
        rows = served[2 * cap * chip : 2 * cap * (chip + 1)]
        tail = [rows[:, base : base + 128] for base in range(0, width, 128)]
        message[chip, slots * (width // 128) :, :] = jnp.concatenate([*tail, id_rows], 0).astype(BF)
    for out in stores:
        out.wait()


def write_slots(message, chip, value):
    slots = value.shape[0]
    for part in range(value.shape[1] // 128):
        message[chip, part * slots : (part + 1) * slots, :] = value[:, part * 128 : (part + 1) * 128]


def slot_rows(ref, slots, width):
    parts = [
        jnp.concatenate([ref[chip, base : base + slots, :] for chip in range(ref.shape[0])], 0)
        for base in range(0, slots * (width // 128), slots)
    ]
    return jnp.concatenate(parts, 1)


def gathered_slots(piece, chips, core, cap, shape, dim):
    slots = 2 * chips * cap
    index = iota(shape, dim)
    chip = lax.div(index, slots)
    slot = index - chip * slots
    band = 2 * chip + jnp.where(piece == 0, core, 1 - core)
    return band, lax.div(slot, cap), lax.rem(slot, cap)


def holder_of(shape, dim, chips, core):
    index = iota(shape, dim)
    return jnp.where(index < chips, 2 * index + core, 2 * (index - chips) + 1 - core)


def slot_matches(first, second, me, cap, mesh_rows, width):
    chips = first.shape[0]
    owners = 2 * chips
    slots = owners * cap
    span = chips * slots
    parts = width // 128
    core = lax.rem(me, 2)
    table = jnp.zeros((owners, 128), F32)
    latent = jnp.zeros((slots, width), F32)
    for piece, ref in enumerate((first, second)):
        ids, rows = [], []
        for chip in range(chips):
            tail = ref[chip, slots * parts :, :].astype(F32)
            ids.append(tail[8 * parts :])
            rows.append(jnp.concatenate([tail[8 * part : 8 * part + 8] for part in range(parts)], 1))
        ids = jnp.concatenate(ids, 0).astype(BF)
        rows = jnp.concatenate(rows, 0).astype(BF)
        shape = (owners, 8 * chips)
        table = table + mm(hot(iota(shape, 1) == (iota(shape, 0) - piece * chips) * 8), ids)
        shape = (slots, 8 * chips)
        window = iota(shape, 0)
        owner = lax.div(window, cap)
        held = lax.rem(owner, 2) == (core if piece == 0 else 1 - core)
        at = lax.div(owner, 2) * 8 + cap * core + lax.rem(window, cap)
        latent = latent + mm(hot(held & (iota(shape, 1) == at)), rows)
    digits = table.astype(BF)
    shape = (slots, owners)
    mine = mm(hot(holder_of(shape, 1, chips, core) == lax.div(iota(shape, 0), cap)), digits)
    lane = iota((slots, 128), 1) - cap * me - lax.rem(iota((slots, 128), 0), cap)
    scaled = jnp.where(lane == 0, 256.0 * mine, jnp.where(lane == slots, mine, 0.0))
    own_key = jnp.sum(scaled, 1, keepdims=True)
    own_key = own_key + (lax.div(iota((slots, 1), 0), cap) * mesh_rows).astype(F32)
    keys, same = [], []
    for piece in range(2):
        band, owner, place = gathered_slots(piece, chips, core, cap, (1, span), 1)
        at = iota((128, span), 0) - cap * band - place
        weight = jnp.where(at == 0, 256.0, jnp.where(at == slots, 1.0, 0.0)).astype(BF)
        value = jnp.where(holder_of((owners, 1), 0, chips, core) == owner, mm(digits, weight), 0.0)
        key = jnp.sum(value, 0, keepdims=True) + (owner * mesh_rows).astype(F32)
        keys.append(key)
        same.append(hot(key == own_key))
    return keys, same, latent


def decoder_kernel(
    cap, mesh_rows, place, first, second, extra, node_any, dec_any, send_any, feat_any, feat_w_any, cot_any,
    message, keys_out, same_out, slope_out, grad_out, node_w, dec_w, send, feat, feat_w, cotangent, sems,
):
    sources = (node_any, dec_any, send_any, feat_any, feat_w_any, cot_any)
    copies = fetch(sources, (node_w, dec_w, send, feat, feat_w, cotangent), sems)
    slots, width = extra.shape
    keys, same, latent = slot_matches(first, second, place[0], cap, mesh_rows, width)
    agg = jnp.zeros((slots, width), F32)
    for piece, ref in enumerate((first, second)):
        keys_out[piece : piece + 1, :] = keys[piece]
        same_out[piece] = same[piece]
        agg = agg + mm(same[piece], slot_rows(ref, slots, width))
    sig = sigmoid(agg)
    silu = agg * sig
    slope_out[...] = sig + silu * (1.0 - sig)
    for copy in copies:
        copy.wait()
    hmesh = (latent + mm(silu.astype(BF), node_w[...])).astype(BF)
    proj = mm(hmesh, dec_w[...]).astype(BF)
    table = jnp.concatenate([proj, stack_terms(feat_w[...], WEIGHT_ORDER)], 0)
    grid_rows = cotangent.shape[0]
    block = math.gcd(grid_rows, 512)
    total = jnp.zeros((table.shape[0], width), F32)
    for start in range(0, grid_rows, block):
        part = slice(start, start + block)
        cot = cotangent[part, :].astype(F32)
        for k in range(3):
            to_slot = hot(iota((slots, block), 0) == send[k : k + 1, part])
            pick = jnp.concatenate([to_slot, stack_terms(feat[k, :, part], FEAT_ORDER)], 0)
            pre = mm(pick, table, TN)
            sig = sigmoid(pre)
            slope = sig + pre * sig * (1.0 - sig)
            total = total + mm(pick, (cot * slope).astype(BF))
    half = total[:slots].astype(BF)
    grad_out[...] = feature_grad(total[slots:], feat_w.shape[0])
    chips = message.shape[0]
    share = width // chips
    step = slots * share // 128
    for chip in range(chips):
        write_slots(message, chip, half)
        columns = extra[:, chip * share : (chip + 1) * share].astype(F32)
        columns = jnp.concatenate([columns[base : base + step] for base in range(0, slots, step)], 1)
        message[chip, slots * (width // 128) :, :] = columns.astype(BF)


def backward_kernel(
    place, count, first, second, same, agg_slope, dec_grad, node_any, dec_any, send_any, receive_any, feat_any,
    latent_any, slope_any, dpx_out, keep, give, hots, grads, part, node_w, dec_w, send, receive, feat, latent, slope,
    sems,
):
    sources = (send_any, feat_any, receive_any, dec_any, node_any, slope_any, latent_any)
    copies = fetch(sources, (send, feat, receive, dec_w, node_w, slope, latent), sems)
    slots = same.shape[1]
    edges = send.shape[1]
    grid_rows, width = latent.shape
    feats = feat.shape[0]
    core = lax.rem(place[0], 2)
    dproj = mm(same[0], slot_rows(first, slots, width)) + mm(same[1], slot_rows(second, slots, width))
    high = dproj.astype(BF)
    low = (dproj - high.astype(F32)).astype(BF)
    for copy in copies[:5]:
        copy.wait()
    dhmesh = mm(jnp.concatenate([high, low], 0), dec_w[...], NT)
    mesh_grad = (dhmesh[:slots] + dhmesh[slots:]).astype(BF)
    dagg = (mm(mesh_grad, node_w[...], NT) * agg_slope[...]).astype(BF)
    block = math.gcd(edges, 512)
    copies[5].wait()
    for start in range(0, edges, block):
        cut = slice(start, start + block)
        live = iota((1, block), 1) + start < count[0]
        slot = jnp.where(live, receive[:, cut], -1)
        upstream = mm(hot(iota((slots, block), 0) == slot), dagg, TN)
        grads[cut, :] = (upstream * slope[cut, :].astype(F32)).astype(BF)
        hots[:grid_rows, cut] = hot(iota((grid_rows, block), 0) == send[:, cut])
        hots[grid_rows:, cut] = stack_terms(feat[:, cut], FEAT_ORDER)
    step = math.gcd(grid_rows, 256)
    for start in range(0, grid_rows, step):
        cut = slice(start, start + step)
        dpx_out[cut, :] = mm(hots[cut, :], grads[...]).astype(BF)
    enc_grad = feature_grad(mm(hots[grid_rows:, :], grads[...]), feats)
    sums = jnp.where(iota(enc_grad.shape, 0) < feats, enc_grad, pltpu.roll(dec_grad[...], feats, 0))
    copies[6].wait()
    part[...] = mm(latent[...], dpx_out[...], TN)
    rows = width // (2 * keep.shape[0])
    blank = jnp.zeros((8, 128 - rows), F32)
    for chip in range(keep.shape[0]):
        pair = [sums[:, base : base + rows] for base in (2 * chip * rows, (2 * chip + 1) * rows)]
        for out, side in ((keep, core), (give, 1 - core)):
            block = part[pl.ds((2 * chip + side) * rows, rows), :]
            small = jnp.where(side == 0, pair[0], pair[1])
            pieces = [block[:, base : base + 128] for base in range(0, width, 128)]
            whole = jnp.concatenate([*pieces, jnp.concatenate([small, blank], 1)], 0)
            out[chip] = whole.astype(out.dtype)


def pair_kernel(keep, given, out):
    out[...] = (keep[...] + given[...].astype(F32)).astype(BF)


def grid_kernel(dpx, weight_any, cot_any, out, weight, cotangent, sems):
    copies = fetch((weight_any, cot_any), (weight, cotangent), sems)
    for copy in copies:
        copy.wait()
    out[...] = (cotangent[...].astype(F32) + mm(dpx[...], weight[...], NT)).astype(BF)


def final_kernel(feats, arrived, out, enc_out, dec_out):
    total = jnp.sum(arrived[...].astype(F32), 0)
    rows, width = out.shape
    for part in range(width // 128):
        out[:, part * 128 : (part + 1) * 128] = total[part * rows : (part + 1) * rows]
    base = rows * (width // 128)
    enc_out[...] = total[base : base + feats, :rows]
    dec_out[...] = total[base + feats : base + 2 * feats, :rows]


def weight_kernel(
    cap, mesh_rows, place, first, second, first_back, second_back, keys, node_any, dec_any,
    mesh_out, dec_out, node_out, node_w, dec_w, sems,
):
    copies = fetch((node_any, dec_any), (node_w, dec_w), sems)
    width = node_w.shape[0]
    chips = first.shape[0]
    owners = 2 * chips
    slots = owners * cap
    span = chips * slots
    me = place[0]
    core = lax.rem(me, 2)
    block = width // owners
    forward = jnp.concatenate([slot_rows(ref, slots, width) for ref in (first, second)], 0)
    back = jnp.concatenate([slot_rows(ref, slots, width) for ref in (first_back, second_back)], 0)
    tail = slots * (width // 128)
    columns = [ref[chip, tail:, :] for ref in (first_back, second_back) for chip in range(chips)]
    step = columns[0].shape[0]
    columns = jnp.concatenate(columns, 0)
    key = jnp.concatenate([keys[0:1, :], keys[1:2, :]], 1)
    down = jnp.broadcast_to(key, (128, 2 * span)).T
    same = jnp.concatenate([hot(down == key[:, base : base + 128]) for base in range(0, 2 * span, 128)], 1)
    agg = mm(same, forward)
    act = (agg * sigmoid(agg)).astype(BF)
    shape = (width, 128)
    mine = hot((iota(shape, 0) == block * me + iota(shape, 1)) & (iota(shape, 1) < block))
    for copy in copies:
        copy.wait()
    node_cols = mm(node_w[...], mine).astype(BF)
    both = mm(act, jnp.concatenate([node_cols, mine], 1))
    pieces = [gathered_slots(piece, chips, core, cap, (span, 1), 0) for piece in range(2)]
    band, owner, turn = [jnp.concatenate([a, b], 0) for a, b in zip(*pieces)]
    source = jnp.where(lax.rem(owner, 2) == core, 0, chips) + lax.div(owner, 2)
    number = cap * band + turn
    at = lax.div(number, step) * (owners * step) + source * step + lax.rem(number, step)
    shape = (128, 128)
    folded = []
    for base in range(0, 128, 2 * block):
        fold = hot((iota(shape, 0) == base + block * core + iota(shape, 1)) & (iota(shape, 1) < block))
        folded.append(mm(columns, fold).astype(BF))
    latent = mm(hot(iota((2 * span, 2 * span), 1) == at), jnp.concatenate(folded, 0))
    hmesh = (both[:, :128] + latent).astype(BF)
    left = jnp.concatenate([hmesh, both[:, 128:].astype(BF)], 1)
    sums = mm(left, back, TN)
    dec_out[...] = sums[:block]
    lead = sums[128 : 128 + block]
    high = lead.astype(BF)
    low = (lead - high.astype(F32)).astype(BF)
    node_out[...] = mm(high, dec_w[...], NT) + mm(low, dec_w[...], NT)
    mesh = mesh_out.shape[0]
    shape = (mesh, 2 * span)
    own = (me * mesh_rows + iota(shape, 0)).astype(F32)
    dproj = mm(hot(own == key), back)
    high = dproj.astype(BF)
    low = (dproj - high.astype(F32)).astype(BF)
    mesh_out[...] = (mm(high, dec_w[...], NT) + mm(low, dec_w[...], NT)).astype(BF)


SMEM = pl.BlockSpec(memory_space=pltpu.SMEM)
VMEM = pl.BlockSpec(memory_space=pltpu.VMEM)
FAR = pl.BlockSpec(memory_space=pltpu.HBM)


def kernel_call(body, name, scalars, near, far, outs, scratch, flops, limit, out_specs=None):
    shapes = [jax.ShapeDtypeStruct(shape, dtype) for shape, dtype in outs]
    moved = sum(a.size * a.dtype.itemsize for a in (*near, *far)) + sum(s.size * s.dtype.itemsize for s in shapes)
    buffers = [pltpu.VMEM(a.shape, a.dtype) for a in far]
    if far:
        buffers.append(pltpu.SemaphoreType.DMA((len(far),)))
    return pl.pallas_call(
        body,
        name=name,
        out_shape=shapes,
        in_specs=[SMEM] * len(scalars) + [VMEM] * len(near) + [FAR] * len(far),
        out_specs=out_specs or [VMEM] * len(shapes),
        scratch_shapes=[*scratch, *buffers],
        compiler_params=pltpu.CompilerParams(vmem_limit_bytes=limit * MIB),
        cost_estimate=pl.CostEstimate(flops=flops, bytes_accessed=moved, transcendentals=0),
    )(*scalars, *near, *far)


def gather_plan(
    grid_latent,
    mesh_latent,
    grid_cotangent,
    enc_sender,
    enc_receiver,
    enc_feat,
    enc_count,
    dec_sender,
    dec_feat,
    serve_rows,
    enc_proj,
    node_proj,
    dec_proj,
    enc_feat_w,
    dec_feat_w,
):
    owners = lax.axis_size("lat")
    chips = owners // 2
    cap = serve_rows.shape[2]
    slots = owners * cap
    mesh_rows, width = mesh_latent.shape
    grid_rows = grid_latent.shape[0]
    edges = enc_sender.shape[0]
    feats = enc_feat.shape[0]
    block = width // owners
    span = chips * slots
    parts = width // 128
    share = width // chips
    groups = [[core + 2 * chip for chip in range(chips)] for core in range(2)]
    swap = [(index, index ^ 1) for index in range(owners)]
    place = lax.axis_index("lat").astype(jnp.int32).reshape(1)

    def gather(message):
        first = lax.all_to_all(message, "lat", 0, 0, tiled=True, axis_index_groups=groups)
        return first, lax.ppermute(first, "lat", swap)

    send = enc_sender.reshape(1, edges)
    receive = enc_receiver.reshape(1, edges)
    message, slope, served = kernel_call(
        lambda *refs: encoder_kernel(cap, *refs),
        "encoder",
        [enc_count],
        [],
        [grid_latent, enc_proj, mesh_latent, send, receive, enc_feat, enc_feat_w.T, serve_rows[0].T],
        [((chips, parts * (slots + 8) + 8, 128), BF), ((edges, width), BF), ((slots, width), BF)],
        [
            pltpu.VMEM((grid_rows, width), BF),
            pltpu.VMEM((edges, grid_rows), BF),
            pltpu.VMEM((edges, width), BF),
            pltpu.SemaphoreType.DMA((edges // math.gcd(edges, 512),)),
        ],
        2 * edges * grid_rows * width,
        60,
        [VMEM, FAR, VMEM],
    )
    first, second = gather(message)
    message, keys, same, agg_slope, dec_grad = kernel_call(
        lambda *refs: decoder_kernel(cap, mesh_rows, *refs),
        "decoder",
        [place],
        [first, second, served],
        [node_proj, dec_proj, dec_sender, dec_feat, dec_feat_w.T, grid_cotangent],
        [
            ((chips, parts * slots + slots * share // 128, 128), BF),
            ((2, span), F32),
            ((2, slots, span), BF),
            ((slots, width), F32),
            ((8, width), F32),
        ],
        [],
        24 * grid_rows * 128 * width,
        20,
    )
    first_back, second_back = gather(message)
    term_rows = -(-6 * feats // 16) * 16
    dpx, keep, give = kernel_call(
        backward_kernel,
        "backward",
        [place, enc_count],
        [first_back, second_back, same, agg_slope, dec_grad],
        [node_proj, dec_proj, send, receive, enc_feat, grid_latent, slope],
        [((grid_rows, width), BF), ((chips, parts * block + 8, 128), F32), ((chips, parts * block + 8, 128), BF)],
        [
            pltpu.VMEM((grid_rows + term_rows, edges), BF),
            pltpu.VMEM((edges, width), BF),
            pltpu.VMEM((width, width), F32),
        ],
        2 * edges * grid_rows * width,
        24,
    )
    given = lax.ppermute(give, "lat", swap)
    (grid_grad,) = kernel_call(
        grid_kernel,
        "grid",
        [],
        [dpx],
        [enc_proj, grid_cotangent],
        [((grid_rows, width), BF)],
        [],
        2 * grid_rows * width * width,
        16,
    )
    given, grid_grad = lax.optimization_barrier((given, grid_grad))
    (pair,) = kernel_call(pair_kernel, "pair", [], [keep, given], [], [(give.shape, BF)], [], keep.size, 8)
    pair, keys = lax.optimization_barrier((pair, keys))
    arrived = lax.all_to_all(pair, "lat", 0, 0, tiled=True, axis_index_groups=groups)
    mesh_grad, dec_proj_grad, node_proj_grad = kernel_call(
        lambda *refs: weight_kernel(cap, mesh_rows, *refs),
        "weights",
        [place],
        [first, second, first_back, second_back, keys],
        [node_proj, dec_proj],
        [((mesh_rows, width), BF), ((block, width), F32), ((block, width), F32)],
        [],
        2 * (2 * span) * (2 * span) * width,
        24,
    )
    enc_proj_grad, enc_feat_grad, dec_feat_grad = kernel_call(
        lambda *refs: final_kernel(feats, *refs),
        "final",
        [],
        [arrived],
        [],
        [((block, width), F32), ((feats, block), F32), ((feats, block), F32)],
        [],
        arrived.size,
        8,
    )
    return (
        grid_grad,
        mesh_grad,
        enc_proj_grad,
        node_proj_grad,
        dec_proj_grad,
        enc_feat_grad.T,
        dec_feat_grad.T,
    )


def gather_fits(args):
    mesh_latent, serve_rows = args[1], args[9]
    owners, cap = serve_rows.shape[1], serve_rows.shape[2]
    width = mesh_latent.shape[1]
    chips = owners // 2
    return (
        owners % 2 == 0
        and 2 * cap == 8
        and owners * cap <= 64
        and width % 128 == 0
        and width % (8 * owners) == 0
        and 128 % (width // chips) == 0
        and owners * cap * (width // chips) % 2048 == 0
        and mesh_latent.shape[0] <= 65536
        and mesh_latent.shape[0] * owners < 1 << 24
        and args[0].shape[0] % 128 == 0
        and args[3].shape[0] % 128 == 0
        and args[5].shape[0] == 4
    )


def per_device(*args):
    return gather_plan(*args) if gather_fits(args) else owner_plan(*args)


def solution(mesh):
    placed = (
        P(("member", "lat"), None),
        P(("member", "lat"), None),
        P(("member", "lat"), None),
        P(("member", "lat")),
        P(("member", "lat")),
        P(None, ("member", "lat")),
        P(("member", "lat")),
        P(None, ("member", "lat")),
        P(None, None, ("member", "lat")),
        P(("member", "lat"), None, None),
        P(),
        P(),
        P(),
        P(),
        P(),
    )
    return jax.shard_map(
        per_device,
        mesh=mesh,
        in_specs=placed,
        out_specs=(
            P(("member", "lat"), None),
            P(("member", "lat"), None),
            P(("member", "lat"), None),
            P(("member", "lat"), None),
            P(("member", "lat"), None),
            P(("member", "lat"), None),
            P(("member", "lat"), None),
        ),
        check_vma=False,
    )
```

```python
import math

import jax
import jax.numpy as jnp
from jax import lax
from jax.experimental import pallas as pl
from jax.experimental.pallas import tpu as pltpu
from jax.sharding import PartitionSpec as P

BF = jnp.bfloat16
F32 = jnp.float32
HI = lax.Precision.HIGHEST
MIB = 1 << 20
NN = (((1,), (0,)), ((), ()))
NT = (((1,), (1,)), ((), ()))
TN = (((0,), (0,)), ((), ()))


def silu_grad(value):
    sig = jax.nn.sigmoid(value)
    return sig * (1.0 + value * (1.0 - sig))


def owner_plan(
    grid_latent,
    mesh_latent,
    grid_cotangent,
    enc_sender,
    enc_receiver,
    enc_feat,
    enc_count,
    dec_sender,
    dec_feat,
    serve_rows,
    enc_proj,
    node_proj,
    dec_proj,
    enc_feat_w,
    dec_feat_w,
):
    highest = lax.Precision.HIGHEST
    owners_count = lax.axis_size("lat")
    serve_flat = serve_rows.reshape(-1)
    slot_total = serve_flat.shape[0]
    per_owner = slot_total // owners_count
    mesh_rows = mesh_latent.shape[0]
    grid_rows = grid_latent.shape[0]
    width = grid_latent.shape[1]
    edge_slots = enc_sender.shape[0]
    edge_block = math.gcd(edge_slots, 512)
    grid_block = math.gcd(grid_rows, 512)
    live_count = enc_count[0]
    slot_ids = lax.iota(jnp.int32, slot_total)[:, None]
    row_ids = lax.iota(jnp.int32, grid_rows)[:, None]

    def to_window(rows):
        outgoing = jnp.take(rows, serve_flat, axis=0).reshape(owners_count, per_owner, width)
        arrived = lax.all_to_all(outgoing, "lat", split_axis=0, concat_axis=0, tiled=True)
        return arrived.reshape(slot_total, width)

    def to_owners(partial_value):
        arrived = lax.all_to_all(
            partial_value.reshape(owners_count, per_owner, width),
            "lat",
            split_axis=0,
            concat_axis=0,
            tiled=True,
        )
        return jax.ops.segment_sum(
            arrived.reshape(slot_total, width), serve_flat, num_segments=mesh_rows
        )

    px = jnp.dot(grid_latent, enc_proj, preferred_element_type=jnp.float32).astype(jnp.bfloat16)

    def enc_block(start):
        senders = lax.dynamic_slice_in_dim(enc_sender, start, edge_block)
        receivers = lax.dynamic_slice_in_dim(enc_receiver, start, edge_block)
        feats = lax.dynamic_slice_in_dim(enc_feat, start, edge_block, 1)
        pre = jnp.take(px, senders, axis=0).astype(jnp.float32) + jnp.einsum(
            "fb,lf->bl", feats, enc_feat_w, precision=highest
        )
        live = (lax.iota(jnp.int32, edge_block) + start < live_count)[:, None]
        onehot = (receivers[None, :] == slot_ids).astype(jnp.bfloat16)
        return (pre, live, onehot, senders, feats)

    block_steps = edge_slots // edge_block

    def enc_forward(index, partial_value):
        pre, live, onehot, senders, feats = enc_block(index * edge_block)
        message = jnp.where(live, jax.nn.silu(pre), 0.0).astype(jnp.bfloat16)
        return partial_value + jnp.dot(onehot, message, preferred_element_type=jnp.float32)

    enc_partial = lax.fori_loop(
        0, block_steps, enc_forward, jnp.zeros((slot_total, width), jnp.float32)
    )
    agg = to_owners(enc_partial)
    act = jax.nn.silu(agg).astype(jnp.bfloat16)
    hmesh = (
        mesh_latent.astype(jnp.float32)
        + jnp.dot(act, node_proj, preferred_element_type=jnp.float32)
    ).astype(jnp.bfloat16)
    proj_window = to_window(
        jnp.dot(hmesh, dec_proj, preferred_element_type=jnp.float32).astype(jnp.bfloat16)
    )

    def dec_backward(index, carry):
        dproj, dfw = carry
        start = index * grid_block
        cot = lax.dynamic_slice_in_dim(grid_cotangent, start, grid_block).astype(jnp.float32)
        for k in range(3):
            senders = lax.dynamic_slice_in_dim(dec_sender[k], start, grid_block)
            feats = lax.dynamic_slice_in_dim(dec_feat[k], start, grid_block, 1)
            pre = jnp.take(proj_window, senders, axis=0).astype(jnp.float32) + jnp.einsum(
                "fg,lf->gl", feats, dec_feat_w, precision=highest
            )
            grad_half = (cot * silu_grad(pre)).astype(jnp.bfloat16)
            slot_hot = (senders[None, :] == slot_ids).astype(jnp.bfloat16)
            dproj = dproj + jnp.dot(slot_hot, grad_half, preferred_element_type=jnp.float32)
            dfw = dfw + jnp.einsum(
                "gl,fg->lf", grad_half.astype(jnp.float32), feats, precision=highest
            )
        return (dproj, dfw)

    start_carry = (
        jnp.zeros((slot_total, width), jnp.float32),
        jnp.zeros((width, dec_feat_w.shape[1]), jnp.float32),
    )
    dproj_window, dec_fw_part = lax.fori_loop(0, grid_rows // grid_block, dec_backward, start_carry)
    dec_weight = dec_proj.astype(jnp.float32)
    dproj = to_owners(dproj_window)
    dhmesh = jnp.dot(dproj, dec_weight.T, precision=highest)
    dec_proj_part = jnp.dot(hmesh.astype(jnp.float32).T, dproj, precision=highest)
    mesh_grad = dhmesh.astype(jnp.bfloat16)
    node_proj_part = jnp.dot(act.T, mesh_grad, preferred_element_type=jnp.float32)
    dagg = (
        jnp.dot(mesh_grad, node_proj.T, preferred_element_type=jnp.float32) * silu_grad(agg)
    ).astype(jnp.bfloat16)
    dagg_window = to_window(dagg)

    def enc_backward(index, carry):
        dpx, dew = carry
        pre, live, onehot, senders, feats = enc_block(index * edge_block)
        upstream = jnp.einsum("wb,wl->bl", onehot, dagg_window, preferred_element_type=jnp.float32)
        grad_half = jnp.where(live, upstream * silu_grad(pre), 0.0).astype(jnp.bfloat16)
        row_hot = (senders[None, :] == row_ids).astype(jnp.bfloat16)
        dpx = dpx + jnp.dot(row_hot, grad_half, preferred_element_type=jnp.float32)
        dew = dew + jnp.einsum("bl,fb->lf", grad_half.astype(jnp.float32), feats, precision=highest)
        return (dpx, dew)

    start_back = (
        jnp.zeros((grid_rows, width), jnp.float32),
        jnp.zeros((width, enc_feat_w.shape[1]), jnp.float32),
    )
    dpx_sum, enc_fw_part = lax.fori_loop(0, block_steps, enc_backward, start_back)
    dpx = dpx_sum.astype(jnp.bfloat16)
    enc_proj_part = jnp.dot(grid_latent.T, dpx, preferred_element_type=jnp.float32)
    grid_grad = (
        grid_cotangent.astype(jnp.float32)
        + jnp.dot(dpx, enc_proj.T, preferred_element_type=jnp.float32)
    ).astype(jnp.bfloat16)
    enc_proj_grad, node_proj_grad, dec_proj_grad, enc_feat_w_grad, dec_feat_w_grad = (
        lax.psum_scatter(enc_proj_part, "lat", scatter_dimension=0, tiled=True),
        lax.psum_scatter(node_proj_part, "lat", scatter_dimension=0, tiled=True),
        lax.psum_scatter(dec_proj_part, "lat", scatter_dimension=0, tiled=True),
        lax.psum_scatter(enc_fw_part, "lat", scatter_dimension=0, tiled=True),
        lax.psum_scatter(dec_fw_part, "lat", scatter_dimension=0, tiled=True),
    )
    return (
        grid_grad,
        mesh_grad,
        enc_proj_grad,
        node_proj_grad,
        dec_proj_grad,
        enc_feat_w_grad,
        dec_feat_w_grad,
    )


def mm(a, b, dims=NN, precision=None):
    return lax.dot_general(a, b, dims, precision=precision, preferred_element_type=F32)


def iota(shape, dim):
    return lax.broadcasted_iota(jnp.int32, shape, dim)


def halves(value):
    turn = jnp.tanh(value)
    up = 1.0 + turn
    silu = value * up
    return silu, up + silu * (1.0 - turn)


def hot(mask):
    return jnp.where(mask, 1.0, 0.0).astype(BF)


def split3(value):
    high = value.astype(BF).astype(F32)
    rest = value - high
    middle = rest.astype(BF).astype(F32)
    return high, middle, rest - middle


def stack_rows(feats):
    return -(-6 * feats // 16) * 16


def stack_terms(value, order):
    parts = split3(value)
    rows = len(order) * value.shape[0]
    blank = jnp.zeros((stack_rows(value.shape[0]) - rows, value.shape[1]), F32)
    return jnp.concatenate([*(parts[which] for which in order), blank], 0)


FEAT_ORDER = (0, 0, 1, 1, 2, 0)
WEIGHT_ORDER = (0, 1, 0, 1, 0, 2)


def fetch(sources, targets, sems):
    copies = [pltpu.make_async_copy(src, dst, sems.at[i]) for i, (src, dst) in enumerate(zip(sources, targets))]
    for copy in copies:
        copy.start()
    return copies


def feature_grad(terms, feats):
    total = terms[: 2 * feats] + terms[2 * feats : 4 * feats] + terms[4 * feats : 6 * feats]
    return jnp.where(iota(total.shape, 0) < feats, total, 0.0)


def encoder_kernel(
    cap, count, latent_any, weight_any, mesh_any, send_any, receive_any, feat_any, feat_w_any, serve_any,
    message, slope_far, served_out, px, picks, slope, slope_sems,
    latent, weight, mesh, send, receive, feat, feat_w, serve, sems, latent_sems,
):
    sources = (send_any, feat_any, weight_any, feat_w_any, receive_any, mesh_any, serve_any)
    targets = (send, feat, weight, feat_w, receive, mesh, serve)
    copies = fetch(sources[:3], targets[:3], sems)
    edges = send.shape[1]
    grid_rows, width = latent.shape
    chips = message.shape[0]
    slots = served_out.shape[0]
    step = math.gcd(grid_rows, 256)
    cuts = [slice(start, start + step) for start in range(0, grid_rows, step)]
    chunks = fetch([latent_any.at[cut, :] for cut in cuts], [latent.at[cut, :] for cut in cuts], latent_sems)
    copies += fetch(sources[3:], targets[3:], sems.at[pl.ds(3, 4)])
    block = math.gcd(edges, 512)
    copies[0].wait()
    copies[1].wait()

    def build(start):
        part = slice(start, start + block)
        ids = jnp.broadcast_to(send[:, part].astype(F32), (128, block)).T
        for base in range(0, grid_rows, 128):
            lane = (iota((block, 128), 1) + base).astype(F32)
            picks[part, base : base + 128] = hot(ids == lane)

    for start in range(0, edges // 2, block):
        build(start)
    copies[2].wait()
    for cut, chunk in zip(cuts, chunks):
        chunk.wait()
    px[:grid_rows, :] = (0.5 * mm(latent[...], weight[...]).astype(BF).astype(F32)).astype(BF)
    for copy in copies[3:5]:
        copy.wait()
    terms = stack_terms(0.5 * feat_w[...], WEIGHT_ORDER)
    px[grid_rows:, :] = jnp.concatenate([terms, jnp.zeros((128 - terms.shape[0], width), F32)], 0).astype(BF)
    total = jnp.zeros((slots, width), F32)
    stores = []
    for start in range(0, edges, block):
        part = slice(start, start + block)
        if start >= edges // 2:
            build(start)
        pre = mm(picks[part, :grid_rows], px[:grid_rows, :])
        pre = pre + mm(stack_terms(feat[:, part], FEAT_ORDER).astype(BF), px[grid_rows : grid_rows + 32, :], TN)
        silu, double = halves(pre)
        slope[part, :] = double.astype(BF)
        out = pltpu.make_async_copy(slope.at[part, :], slope_far.at[part, :], slope_sems.at[len(stores)])
        out.start()
        stores.append(out)
        live = iota((1, block), 1) + start < count[0]
        slot = jnp.where(live, receive[:, part], -1)
        to_slot = hot(iota((slots, block), 0) == slot)
        total = total + mm(to_slot, silu.astype(BF))
    copies[5].wait()
    copies[6].wait()
    owners = slots // cap
    ids = serve[...]
    spread = hot(iota((owners, slots), 0) == lax.div(iota((owners, slots), 1), cap))
    turn = iota((cap, slots), 0) == iota((cap, slots), 1) % cap
    digits = []
    for value in (lax.shift_right_logical(ids, 8), ids & 255):
        wide = mm(value.astype(F32).astype(BF), spread)
        digits.append(jnp.sum(jnp.where(turn, wide, 0.0), 0, keepdims=True))
    id_row = (digits[0] * 256.0 + digits[1]).astype(jnp.int32)
    served = mm(hot(iota((mesh.shape[0], slots), 0) == id_row), mesh[...], TN)
    served_out[...] = served.astype(BF)
    lane = iota((slots, 128), 1)
    back = iota((slots, 128), 0)
    wide = mm(digits[0].astype(BF), hot(lane == back)) + mm(digits[1].astype(BF), hot(lane == back + slots))
    id_rows = jnp.where(iota((8, 128), 0) == 0, wide, 0.0)
    half = total.astype(BF)
    for chip in range(chips):
        write_slots(message, chip, half)
        rows = served[2 * cap * chip : 2 * cap * (chip + 1)]
        tail = [rows[:, base : base + 128] for base in range(0, width, 128)]
        message[chip, slots * (width // 128) :, :] = jnp.concatenate([*tail, id_rows], 0).astype(BF)
    for out in stores:
        out.wait()


def write_slots(message, chip, value):
    slots = value.shape[0]
    for part in range(value.shape[1] // 128):
        message[chip, part * slots : (part + 1) * slots, :] = value[:, part * 128 : (part + 1) * 128]


def slot_rows(ref, slots, width):
    parts = [
        jnp.concatenate([ref[chip, base : base + slots, :] for chip in range(ref.shape[0])], 0)
        for base in range(0, slots * (width // 128), slots)
    ]
    return jnp.concatenate(parts, 1)


def gathered_slots(piece, chips, core, cap, shape, dim):
    slots = 2 * chips * cap
    index = iota(shape, dim)
    chip = lax.div(index, slots)
    slot = index - chip * slots
    band = 2 * chip + jnp.where(piece == 0, core, 1 - core)
    return band, lax.div(slot, cap), lax.rem(slot, cap)


def holder_of(shape, dim, chips, core):
    index = iota(shape, dim)
    return jnp.where(index < chips, 2 * index + core, 2 * (index - chips) + 1 - core)


def slot_matches(first, second, me, cap, mesh_rows, width):
    chips = first.shape[0]
    owners = 2 * chips
    slots = owners * cap
    span = chips * slots
    parts = width // 128
    core = lax.rem(me, 2)
    table = jnp.zeros((owners, 128), F32)
    latent = jnp.zeros((slots, width), F32)
    for piece, ref in enumerate((first, second)):
        ids, rows = [], []
        for chip in range(chips):
            tail = ref[chip, slots * parts :, :].astype(F32)
            ids.append(tail[8 * parts :])
            rows.append(jnp.concatenate([tail[8 * part : 8 * part + 8] for part in range(parts)], 1))
        ids = jnp.concatenate(ids, 0).astype(BF)
        rows = jnp.concatenate(rows, 0).astype(BF)
        shape = (owners, 8 * chips)
        table = table + mm(hot(iota(shape, 1) == (iota(shape, 0) - piece * chips) * 8), ids)
        shape = (slots, 8 * chips)
        window = iota(shape, 0)
        owner = lax.div(window, cap)
        held = lax.rem(owner, 2) == (core if piece == 0 else 1 - core)
        at = lax.div(owner, 2) * 8 + cap * core + lax.rem(window, cap)
        latent = latent + mm(hot(held & (iota(shape, 1) == at)), rows)
    digits = table.astype(BF)
    shape = (slots, owners)
    mine = mm(hot(holder_of(shape, 1, chips, core) == lax.div(iota(shape, 0), cap)), digits)
    lane = iota((slots, 128), 1) - cap * me - lax.rem(iota((slots, 128), 0), cap)
    scaled = jnp.where(lane == 0, 256.0 * mine, jnp.where(lane == slots, mine, 0.0))
    own_key = jnp.sum(scaled, 1, keepdims=True)
    own_key = own_key + (lax.div(iota((slots, 1), 0), cap) * mesh_rows).astype(F32)
    keys, same = [], []
    for piece in range(2):
        band, owner, place = gathered_slots(piece, chips, core, cap, (1, span), 1)
        at = iota((128, span), 0) - cap * band - place
        weight = jnp.where(at == 0, 256.0, jnp.where(at == slots, 1.0, 0.0)).astype(BF)
        value = jnp.where(holder_of((owners, 1), 0, chips, core) == owner, mm(digits, weight), 0.0)
        key = jnp.sum(value, 0, keepdims=True) + (owner * mesh_rows).astype(F32)
        keys.append(key)
        same.append(hot(key == own_key))
    return keys, same, latent


def decoder_picks(
    after, send_any, feat_any, node_any, dec_any, feat_w_any, cot_any,
    pick, pick_turned, node_w, dec_w, feat_w, cotangent, send, feat, sems,
):
    sources = (send_any, feat_any, node_any, dec_any, feat_w_any, cot_any)
    copies = fetch(sources, (send, feat, node_w, dec_w, feat_w, cotangent), sems)
    slots = after.shape[0]
    grid_rows = send.shape[1]
    copies[0].wait()
    copies[1].wait()
    block = math.gcd(grid_rows, 512)
    for k in range(3):
        for start in range(0, grid_rows, block):
            part = slice(start, start + block)
            to = slice(k * grid_rows + start, k * grid_rows + start + block)
            to_slot = jnp.where(iota((slots, block), 0) == send[k : k + 1, part], 1.0, 0.0)
            rows = jnp.concatenate([to_slot, stack_terms(feat[k, :, part], FEAT_ORDER)], 0)
            pick[:, to] = rows.astype(BF)
            rows = jnp.concatenate([rows, jnp.zeros((128 - rows.shape[0], block), F32)], 0)
            pick_turned[to, :] = rows.T.astype(BF)
    for copy in copies[2:]:
        copy.wait()


def encoder_picks(
    count, receive_any, latent_any, dec_any, node_any, send_any, feat_any, slope_any,
    to_edge, latent_turned, dec_turned, node_turned, send, feat, slope, receive, latent, dec_w, node_w, sems,
):
    sources = (receive_any, dec_any, node_any, latent_any, send_any, feat_any, slope_any)
    copies = fetch(sources, (receive, dec_w, node_w, latent, send, feat, slope), sems)
    edges = receive.shape[1]
    copies[0].wait()
    block = math.gcd(edges, 512)
    for start in range(0, edges, block):
        part = slice(start, start + block)
        live = iota((1, block), 1) + start < count[0]
        slot = jnp.where(live, receive[:, part], -1)
        to_edge[part, :] = jnp.where(iota((128, block), 0) == slot, 1.0, 0.0).T.astype(BF)
    for copy in copies[1:4]:
        copy.wait()
    dec_turned[...] = dec_w[...].T
    node_turned[...] = node_w[...].T
    latent_turned[...] = latent[...].T
    for copy in copies[4:]:
        copy.wait()


def decoder_kernel(
    cap, mesh_rows, place, first, second, extra, pick, pick_turned, node_w, dec_w, feat_w, cotangent,
    message, keys_out, same_out, slope_out, grad_out,
):
    slots, width = extra.shape
    keys, same, latent = slot_matches(first, second, place[0], cap, mesh_rows, width)
    agg = jnp.zeros((slots, width), F32)
    for piece, ref in enumerate((first, second)):
        keys_out[piece : piece + 1, :] = keys[piece]
        same_out[piece] = same[piece]
        agg = agg + mm(same[piece], slot_rows(ref, slots, width))
    silu, double = halves(0.5 * agg)
    slope_out[...] = 0.25 * double
    hmesh = (latent + mm(silu.astype(BF), node_w[...])).astype(BF)
    proj = mm(hmesh, dec_w[...]).astype(BF)
    rows = pick.shape[0]
    blank = jnp.zeros((128 - rows, width), F32)
    terms = jnp.concatenate([stack_terms(0.5 * feat_w[...], WEIGHT_ORDER), blank], 0).astype(BF)
    table = jnp.concatenate([(0.5 * proj.astype(F32)).astype(BF), terms], 0)
    grid_rows = cotangent.shape[0]
    block = math.gcd(grid_rows, 512)
    total = jnp.zeros((rows, width), F32)
    for start in range(0, grid_rows, block):
        cot = cotangent[start : start + block, :].astype(F32)
        for base in range(start, 3 * grid_rows, grid_rows):
            part = slice(base, base + block)
            double = halves(mm(pick_turned[part, :], table))[1]
            total = total + mm(pick[:, part], (cot * double).astype(BF))
    total = 0.5 * total
    half = total[:slots].astype(BF)
    grad_out[...] = feature_grad(total[slots:], feat_w.shape[0])
    chips = message.shape[0]
    share = width // chips
    step = slots * share // 128
    for chip in range(chips):
        write_slots(message, chip, half)
        columns = extra[:, chip * share : (chip + 1) * share].astype(F32)
        columns = jnp.concatenate([columns[base : base + step] for base in range(0, slots, step)], 1)
        message[chip, slots * (width // 128) :, :] = columns.astype(BF)


def backward_kernel(
    place, first, second, same, agg_slope, dec_grad, to_edge, latent_turned, dec_turned, node_turned,
    send, feat, slope, dpx_far, keep, give, grads, part, dpx, dpx_sems,
):
    slots = same.shape[1]
    edges, width = grads.shape
    grid_rows = dpx.shape[0]
    feats = feat.shape[0]
    core = lax.rem(place[0], 2)
    dproj = mm(same[0], slot_rows(first, slots, width)) + mm(same[1], slot_rows(second, slots, width))
    high = dproj.astype(BF)
    low = (dproj - high.astype(F32)).astype(BF)
    dhmesh = mm(jnp.concatenate([high, low], 0), dec_turned[...])
    mesh_grad = (dhmesh[:slots] + dhmesh[slots:]).astype(BF)
    dagg = mm(mesh_grad, node_turned[...]) * agg_slope[...]
    dagg = jnp.concatenate([dagg, jnp.zeros((128 - slots, width), F32)], 0).astype(BF)
    block = math.gcd(edges, 512)
    for start in range(0, edges, block):
        cut = slice(start, start + block)
        grads[cut, :] = (mm(to_edge[cut, :], dagg) * slope[cut, :].astype(F32)).astype(BF)
    step = math.gcd(grid_rows, 256)
    stores = []
    for start in range(0, grid_rows, step):
        cut = slice(start, start + step)
        from_row = hot(iota((step, edges), 0) + start == send[...])
        dpx[cut, :] = mm(from_row, grads[...]).astype(BF)
        out = pltpu.make_async_copy(dpx.at[cut, :], dpx_far.at[cut, :], dpx_sems.at[len(stores)])
        out.start()
        stores.append(out)
    enc_grad = feature_grad(mm(stack_terms(feat[...], FEAT_ORDER).astype(BF), grads[...]), feats)
    sums = jnp.where(iota(enc_grad.shape, 0) < feats, enc_grad, pltpu.roll(dec_grad[...], feats, 0))
    part[...] = mm(latent_turned[...], dpx[...])
    rows = width // (2 * keep.shape[0])
    blank = jnp.zeros((8, 128 - rows), F32)
    for chip in range(keep.shape[0]):
        pair = [sums[:, base : base + rows] for base in (2 * chip * rows, (2 * chip + 1) * rows)]
        for out, side in ((keep, core), (give, 1 - core)):
            block = part[pl.ds((2 * chip + side) * rows, rows), :]
            small = jnp.where(side == 0, pair[0], pair[1])
            pieces = [block[:, base : base + 128] for base in range(0, width, 128)]
            whole = jnp.concatenate([*pieces, jnp.concatenate([small, blank], 1)], 0)
            out[chip] = whole.astype(out.dtype)
    for out in stores:
        out.wait()


def pair_kernel(keep, given, out):
    out[...] = (keep[...] + given[...].astype(F32)).astype(BF)


def grid_kernel(dpx_any, weight_any, cot_any, out, dpx, weight, cotangent, sems):
    copies = fetch((dpx_any, weight_any, cot_any), (dpx, weight, cotangent), sems)
    for copy in copies:
        copy.wait()
    out[...] = (cotangent[...].astype(F32) + mm(dpx[...], weight[...], NT)).astype(BF)


def final_kernel(feats, arrived, out, enc_out, dec_out):
    total = jnp.sum(arrived[...].astype(F32), 0)
    rows, width = out.shape
    for part in range(width // 128):
        out[:, part * 128 : (part + 1) * 128] = total[part * rows : (part + 1) * rows]
    base = rows * (width // 128)
    enc_out[...] = total[base : base + feats, :rows]
    dec_out[...] = total[base + feats : base + 2 * feats, :rows]


def act_kernel(cap, mesh_rows, place, first, second, keys, node_any, both_out, turn_out, own_out, node_w, sems):
    copies = fetch((node_any,), (node_w,), sems)
    width = node_w.shape[0]
    chips = first.shape[0]
    owners = 2 * chips
    slots = owners * cap
    span = chips * slots
    me = place[0]
    core = lax.rem(me, 2)
    block = width // owners
    forward = jnp.concatenate([slot_rows(ref, slots, width) for ref in (first, second)], 0)
    key = jnp.concatenate([keys[0:1, :], keys[1:2, :]], 1)
    down = jnp.broadcast_to(key, (128, 2 * span)).T
    same = jnp.concatenate([hot(down == key[:, base : base + 128]) for base in range(0, 2 * span, 128)], 1)
    agg = mm(same, forward)
    act = halves(0.5 * agg)[0].astype(BF)
    shape = (width, 128)
    mine = hot((iota(shape, 0) == block * me + iota(shape, 1)) & (iota(shape, 1) < block))
    copies[0].wait()
    node_cols = mm(node_w[...], mine).astype(BF)
    both_out[...] = mm(act, jnp.concatenate([node_cols, mine], 1))
    step = slots * 2 * block // 128
    pieces = [gathered_slots(piece, chips, core, cap, (span, 1), 0) for piece in range(2)]
    band, owner, turn = [jnp.concatenate([a, b], 0) for a, b in zip(*pieces)]
    source = jnp.where(lax.rem(owner, 2) == core, 0, chips) + lax.div(owner, 2)
    number = cap * band + turn
    at = lax.div(number, step) * (owners * step) + source * step + lax.rem(number, step)
    turn_out[...] = hot(iota((2 * span, 2 * span), 1) == at)
    own = (me * mesh_rows + iota((own_out.shape[0], 2 * span), 0)).astype(F32)
    own_out[...] = hot(own == key)


def weight_kernel(place, first, second, both, turn, own, dec_turned, mesh_out, dec_out, node_out):
    width = dec_turned.shape[0]
    chips = first.shape[0]
    slots = turn.shape[0] // (2 * chips)
    block = dec_out.shape[0]
    core = lax.rem(place[0], 2)
    back = jnp.concatenate([slot_rows(ref, slots, width) for ref in (first, second)], 0)
    tail = slots * (width // 128)
    columns = jnp.concatenate([ref[chip, tail:, :] for ref in (first, second) for chip in range(chips)], 0)
    shape = (128, 128)
    folded = []
    for base in range(0, 128, 2 * block):
        fold = hot((iota(shape, 0) == base + block * core + iota(shape, 1)) & (iota(shape, 1) < block))
        folded.append(mm(columns, fold).astype(BF))
    latent = mm(turn[...], jnp.concatenate(folded, 0))
    hmesh = (both[:, :128] + latent).astype(BF)
    left = jnp.concatenate([hmesh, both[:, 128:].astype(BF)], 1)
    sums = mm(left, back, TN)
    dec_out[...] = sums[:block]
    lead = sums[128 : 128 + block]
    high = lead.astype(BF)
    low = (lead - high.astype(F32)).astype(BF)
    node_out[...] = mm(high, dec_turned[...]) + mm(low, dec_turned[...])
    dproj = mm(own[...], back)
    high = dproj.astype(BF)
    low = (dproj - high.astype(F32)).astype(BF)
    mesh_out[...] = (mm(high, dec_turned[...]) + mm(low, dec_turned[...])).astype(BF)


SMEM = pl.BlockSpec(memory_space=pltpu.SMEM)
VMEM = pl.BlockSpec(memory_space=pltpu.VMEM)
FAR = pl.BlockSpec(memory_space=pltpu.HBM)


def kernel_call(body, name, scalars, near, far, outs, scratch, flops, limit, out_specs=None, pin=False, last=(), kept=0):
    shapes = [jax.ShapeDtypeStruct(shape, dtype) for shape, dtype in outs]
    out_specs = out_specs or [VMEM] * len(shapes)
    pinned = [pltpu.HBM(s.shape, s.dtype) if spec is FAR else s for s, spec in zip(shapes, out_specs)]
    if pin:
        far = [pltpu.with_memory_space_constraint(a, pltpu.HBM) for a in far]
    moved = sum(a.size * a.dtype.itemsize for a in (*near, *far)) + sum(s.size * s.dtype.itemsize for s in shapes)
    buffers = [pltpu.VMEM(a.shape, a.dtype) for a in far[: len(far) - kept]]
    if far:
        buffers.append(pltpu.SemaphoreType.DMA((len(far),)))
    return pl.pallas_call(
        body,
        name=name,
        out_shape=pinned,
        in_specs=[SMEM] * len(scalars) + [VMEM] * len(near) + [FAR] * len(far),
        out_specs=out_specs,
        scratch_shapes=[*scratch, *buffers, *last],
        compiler_params=pltpu.CompilerParams(vmem_limit_bytes=limit * MIB),
        cost_estimate=pl.CostEstimate(flops=flops, bytes_accessed=moved, transcendentals=0),
    )(*scalars, *near, *far)


def gather_plan(
    grid_latent,
    mesh_latent,
    grid_cotangent,
    enc_sender,
    enc_receiver,
    enc_feat,
    enc_count,
    dec_sender,
    dec_feat,
    serve_rows,
    enc_proj,
    node_proj,
    dec_proj,
    enc_feat_w,
    dec_feat_w,
):
    owners = lax.axis_size("lat")
    chips = owners // 2
    cap = serve_rows.shape[2]
    slots = owners * cap
    mesh_rows, width = mesh_latent.shape
    grid_rows = grid_latent.shape[0]
    edges = enc_sender.shape[0]
    feats = enc_feat.shape[0]
    block = width // owners
    span = chips * slots
    parts = width // 128
    share = width // chips
    groups = [[core + 2 * chip for chip in range(chips)] for core in range(2)]
    swap = [(index, index ^ 1) for index in range(owners)]
    place = lax.axis_index("lat").astype(jnp.int32).reshape(1)

    def gather(message, *later):
        first = lax.all_to_all(message, "lat", 0, 0, tiled=True, axis_index_groups=groups)
        first, *later = lax.optimization_barrier((first, *later))
        return first, lax.ppermute(first, "lat", swap), *later

    send = enc_sender.reshape(1, edges)
    receive = enc_receiver.reshape(1, edges)
    message, slope, served = kernel_call(
        lambda *refs: encoder_kernel(cap, *refs),
        "encoder",
        [enc_count],
        [],
        [grid_latent, enc_proj, mesh_latent, send, receive, enc_feat, enc_feat_w.T, serve_rows[0].T],
        [((chips, parts * (slots + 8) + 8, 128), BF), ((edges, width), BF), ((slots, width), BF)],
        [
            pltpu.VMEM((grid_rows + 128, width), BF),
            pltpu.VMEM((edges, grid_rows + 128), BF),
            pltpu.VMEM((edges, width), BF),
            pltpu.SemaphoreType.DMA((edges // math.gcd(edges, 512),)),
        ],
        2 * edges * grid_rows * width,
        28,
        [VMEM, FAR, VMEM],
        pin=True,
        last=[pltpu.SemaphoreType.DMA((grid_rows // math.gcd(grid_rows, 256),))],
    )
    term_rows = stack_rows(feats)
    first, second, served = gather(message, served)
    pick, pick_turned, near_node, near_dec, near_feat_w, near_cotangent = kernel_call(
        decoder_picks,
        "decoder_picks",
        [],
        [served],
        [dec_sender, dec_feat, node_proj, dec_proj, dec_feat_w.T, grid_cotangent],
        [
            ((slots + term_rows, 3 * grid_rows), BF),
            ((3 * grid_rows, 128), BF),
            ((width, width), BF),
            ((width, width), BF),
            ((feats, width), F32),
            ((grid_rows, width), BF),
        ],
        [],
        2000 * MIB,
        16,
        pin=True,
        kept=4,
    )
    message, keys, same, agg_slope, dec_grad = kernel_call(
        lambda *refs: decoder_kernel(cap, mesh_rows, *refs),
        "decoder",
        [place],
        [first, second, served, pick, pick_turned, near_node, near_dec, near_feat_w, near_cotangent],
        [],
        [
            ((chips, parts * slots + slots * share // 128, 128), BF),
            ((2, span), F32),
            ((2, slots, span), BF),
            ((slots, width), F32),
            ((2 * feats, width), F32),
        ],
        [],
        24 * grid_rows * 128 * width,
        20,
    )
    first_back, second_back, pick_count = gather(message, enc_count)
    to_edge, latent_turned, dec_turned, node_turned, near_send, near_feat, near_slope = kernel_call(
        encoder_picks,
        "encoder_picks",
        [pick_count],
        [],
        [receive, grid_latent, dec_proj, node_proj, send, enc_feat, slope],
        [
            ((edges, 128), BF),
            ((width, grid_rows), BF),
            ((width, width), BF),
            ((width, width), BF),
            ((1, edges), jnp.int32),
            ((feats, edges), F32),
            ((edges, width), BF),
        ],
        [],
        2000 * MIB,
        16,
        pin=True,
        kept=3,
    )
    dpx, keep, give = kernel_call(
        backward_kernel,
        "backward",
        [place],
        [
            first_back,
            second_back,
            same,
            agg_slope,
            dec_grad,
            to_edge,
            latent_turned,
            dec_turned,
            node_turned,
            near_send,
            near_feat,
            near_slope,
        ],
        [],
        [((grid_rows, width), BF), ((chips, parts * block + 8, 128), F32), ((chips, parts * block + 8, 128), BF)],
        [
            pltpu.VMEM((edges, width), BF),
            pltpu.VMEM((width, width), F32),
            pltpu.VMEM((grid_rows, width), BF),
            pltpu.SemaphoreType.DMA((grid_rows // math.gcd(grid_rows, 256),)),
        ],
        2 * edges * grid_rows * width,
        24,
        [FAR, VMEM, VMEM],
    )
    given = lax.ppermute(give, "lat", swap)
    (pair,) = kernel_call(pair_kernel, "pair", [], [keep, given], [], [(give.shape, BF)], [], keep.size, 8)
    pair, keys, dpx = lax.optimization_barrier((pair, keys, dpx))
    arrived = lax.all_to_all(pair, "lat", 0, 0, tiled=True, axis_index_groups=groups)
    (grid_grad,) = kernel_call(
        grid_kernel,
        "grid",
        [],
        [],
        [dpx, enc_proj, grid_cotangent],
        [((grid_rows, width), BF)],
        [],
        2 * grid_rows * width * width,
        16,
    )
    both, turn, own = kernel_call(
        lambda *refs: act_kernel(cap, mesh_rows, *refs),
        "acts",
        [place],
        [first, second, keys],
        [node_proj],
        [((2 * span, 256), F32), ((2 * span, 2 * span), BF), ((mesh_rows, 2 * span), BF)],
        [],
        2 * (2 * span) * (2 * span) * width,
        20,
    )
    mesh_grad, dec_proj_grad, node_proj_grad = kernel_call(
        weight_kernel,
        "weights",
        [place],
        [first_back, second_back, both, turn, own, dec_turned],
        [],
        [((mesh_rows, width), BF), ((block, width), F32), ((block, width), F32)],
        [],
        8 * (2 * span) * 256 * width,
        20,
    )
    enc_proj_grad, enc_feat_grad, dec_feat_grad = kernel_call(
        lambda *refs: final_kernel(feats, *refs),
        "final",
        [],
        [arrived],
        [],
        [((block, width), F32), ((feats, block), F32), ((feats, block), F32)],
        [],
        arrived.size,
        8,
    )
    return (
        grid_grad,
        mesh_grad,
        enc_proj_grad,
        node_proj_grad,
        dec_proj_grad,
        enc_feat_grad.T,
        dec_feat_grad.T,
    )


def gather_fits(args):
    mesh_latent, serve_rows = args[1], args[9]
    owners, cap = serve_rows.shape[1], serve_rows.shape[2]
    width = mesh_latent.shape[1]
    chips = owners // 2
    return (
        owners % 2 == 0
        and 2 * cap == 8
        and owners * cap <= 64
        and width % 128 == 0
        and width % (8 * owners) == 0
        and 128 % (width // chips) == 0
        and owners * cap * (width // chips) % 2048 == 0
        and mesh_latent.shape[0] <= 65536
        and mesh_latent.shape[0] * owners < 1 << 24
        and args[0].shape[0] % 128 == 0
        and args[3].shape[0] % 128 == 0
        and args[5].shape[0] == 4
    )


def per_device(*args):
    return gather_plan(*args) if gather_fits(args) else owner_plan(*args)


def solution(mesh):
    placed = (
        P(("member", "lat"), None),
        P(("member", "lat"), None),
        P(("member", "lat"), None),
        P(("member", "lat")),
        P(("member", "lat")),
        P(None, ("member", "lat")),
        P(("member", "lat")),
        P(None, ("member", "lat")),
        P(None, None, ("member", "lat")),
        P(("member", "lat"), None, None),
        P(),
        P(),
        P(),
        P(),
        P(),
    )
    return jax.shard_map(
        per_device,
        mesh=mesh,
        in_specs=placed,
        out_specs=(
            P(("member", "lat"), None),
            P(("member", "lat"), None),
            P(("member", "lat"), None),
            P(("member", "lat"), None),
            P(("member", "lat"), None),
            P(("member", "lat"), None),
            P(("member", "lat"), None),
        ),
        check_vma=False,
    )
```

```python
import math

import jax
import jax.numpy as jnp
from jax import lax
from jax.experimental import pallas as pl
from jax.experimental.pallas import tpu as pltpu
from jax.sharding import PartitionSpec as P

BF = jnp.bfloat16
F32 = jnp.float32
HI = lax.Precision.HIGHEST
MIB = 1 << 20
NN = (((1,), (0,)), ((), ()))
NT = (((1,), (1,)), ((), ()))
TN = (((0,), (0,)), ((), ()))


def silu_grad(value):
    sig = jax.nn.sigmoid(value)
    return sig * (1.0 + value * (1.0 - sig))


def owner_plan(
    grid_latent,
    mesh_latent,
    grid_cotangent,
    enc_sender,
    enc_receiver,
    enc_feat,
    enc_count,
    dec_sender,
    dec_feat,
    serve_rows,
    enc_proj,
    node_proj,
    dec_proj,
    enc_feat_w,
    dec_feat_w,
):
    highest = lax.Precision.HIGHEST
    owners_count = lax.axis_size("lat")
    serve_flat = serve_rows.reshape(-1)
    slot_total = serve_flat.shape[0]
    per_owner = slot_total // owners_count
    mesh_rows = mesh_latent.shape[0]
    grid_rows = grid_latent.shape[0]
    width = grid_latent.shape[1]
    edge_slots = enc_sender.shape[0]
    edge_block = math.gcd(edge_slots, 512)
    grid_block = math.gcd(grid_rows, 512)
    live_count = enc_count[0]
    slot_ids = lax.iota(jnp.int32, slot_total)[:, None]
    row_ids = lax.iota(jnp.int32, grid_rows)[:, None]

    def to_window(rows):
        outgoing = jnp.take(rows, serve_flat, axis=0).reshape(owners_count, per_owner, width)
        arrived = lax.all_to_all(outgoing, "lat", split_axis=0, concat_axis=0, tiled=True)
        return arrived.reshape(slot_total, width)

    def to_owners(partial_value):
        arrived = lax.all_to_all(
            partial_value.reshape(owners_count, per_owner, width),
            "lat",
            split_axis=0,
            concat_axis=0,
            tiled=True,
        )
        return jax.ops.segment_sum(
            arrived.reshape(slot_total, width), serve_flat, num_segments=mesh_rows
        )

    px = jnp.dot(grid_latent, enc_proj, preferred_element_type=jnp.float32).astype(jnp.bfloat16)

    def enc_block(start):
        senders = lax.dynamic_slice_in_dim(enc_sender, start, edge_block)
        receivers = lax.dynamic_slice_in_dim(enc_receiver, start, edge_block)
        feats = lax.dynamic_slice_in_dim(enc_feat, start, edge_block, 1)
        pre = jnp.take(px, senders, axis=0).astype(jnp.float32) + jnp.einsum(
            "fb,lf->bl", feats, enc_feat_w, precision=highest
        )
        live = (lax.iota(jnp.int32, edge_block) + start < live_count)[:, None]
        onehot = (receivers[None, :] == slot_ids).astype(jnp.bfloat16)
        return (pre, live, onehot, senders, feats)

    block_steps = edge_slots // edge_block

    def enc_forward(index, partial_value):
        pre, live, onehot, senders, feats = enc_block(index * edge_block)
        message = jnp.where(live, jax.nn.silu(pre), 0.0).astype(jnp.bfloat16)
        return partial_value + jnp.dot(onehot, message, preferred_element_type=jnp.float32)

    enc_partial = lax.fori_loop(
        0, block_steps, enc_forward, jnp.zeros((slot_total, width), jnp.float32)
    )
    agg = to_owners(enc_partial)
    act = jax.nn.silu(agg).astype(jnp.bfloat16)
    hmesh = (
        mesh_latent.astype(jnp.float32)
        + jnp.dot(act, node_proj, preferred_element_type=jnp.float32)
    ).astype(jnp.bfloat16)
    proj_window = to_window(
        jnp.dot(hmesh, dec_proj, preferred_element_type=jnp.float32).astype(jnp.bfloat16)
    )

    def dec_backward(index, carry):
        dproj, dfw = carry
        start = index * grid_block
        cot = lax.dynamic_slice_in_dim(grid_cotangent, start, grid_block).astype(jnp.float32)
        for k in range(3):
            senders = lax.dynamic_slice_in_dim(dec_sender[k], start, grid_block)
            feats = lax.dynamic_slice_in_dim(dec_feat[k], start, grid_block, 1)
            pre = jnp.take(proj_window, senders, axis=0).astype(jnp.float32) + jnp.einsum(
                "fg,lf->gl", feats, dec_feat_w, precision=highest
            )
            grad_half = (cot * silu_grad(pre)).astype(jnp.bfloat16)
            slot_hot = (senders[None, :] == slot_ids).astype(jnp.bfloat16)
            dproj = dproj + jnp.dot(slot_hot, grad_half, preferred_element_type=jnp.float32)
            dfw = dfw + jnp.einsum(
                "gl,fg->lf", grad_half.astype(jnp.float32), feats, precision=highest
            )
        return (dproj, dfw)

    start_carry = (
        jnp.zeros((slot_total, width), jnp.float32),
        jnp.zeros((width, dec_feat_w.shape[1]), jnp.float32),
    )
    dproj_window, dec_fw_part = lax.fori_loop(0, grid_rows // grid_block, dec_backward, start_carry)
    dec_weight = dec_proj.astype(jnp.float32)
    dproj = to_owners(dproj_window)
    dhmesh = jnp.dot(dproj, dec_weight.T, precision=highest)
    dec_proj_part = jnp.dot(hmesh.astype(jnp.float32).T, dproj, precision=highest)
    mesh_grad = dhmesh.astype(jnp.bfloat16)
    node_proj_part = jnp.dot(act.T, mesh_grad, preferred_element_type=jnp.float32)
    dagg = (
        jnp.dot(mesh_grad, node_proj.T, preferred_element_type=jnp.float32) * silu_grad(agg)
    ).astype(jnp.bfloat16)
    dagg_window = to_window(dagg)

    def enc_backward(index, carry):
        dpx, dew = carry
        pre, live, onehot, senders, feats = enc_block(index * edge_block)
        upstream = jnp.einsum("wb,wl->bl", onehot, dagg_window, preferred_element_type=jnp.float32)
        grad_half = jnp.where(live, upstream * silu_grad(pre), 0.0).astype(jnp.bfloat16)
        row_hot = (senders[None, :] == row_ids).astype(jnp.bfloat16)
        dpx = dpx + jnp.dot(row_hot, grad_half, preferred_element_type=jnp.float32)
        dew = dew + jnp.einsum("bl,fb->lf", grad_half.astype(jnp.float32), feats, precision=highest)
        return (dpx, dew)

    start_back = (
        jnp.zeros((grid_rows, width), jnp.float32),
        jnp.zeros((width, enc_feat_w.shape[1]), jnp.float32),
    )
    dpx_sum, enc_fw_part = lax.fori_loop(0, block_steps, enc_backward, start_back)
    dpx = dpx_sum.astype(jnp.bfloat16)
    enc_proj_part = jnp.dot(grid_latent.T, dpx, preferred_element_type=jnp.float32)
    grid_grad = (
        grid_cotangent.astype(jnp.float32)
        + jnp.dot(dpx, enc_proj.T, preferred_element_type=jnp.float32)
    ).astype(jnp.bfloat16)
    enc_proj_grad, node_proj_grad, dec_proj_grad, enc_feat_w_grad, dec_feat_w_grad = (
        lax.psum_scatter(enc_proj_part, "lat", scatter_dimension=0, tiled=True),
        lax.psum_scatter(node_proj_part, "lat", scatter_dimension=0, tiled=True),
        lax.psum_scatter(dec_proj_part, "lat", scatter_dimension=0, tiled=True),
        lax.psum_scatter(enc_fw_part, "lat", scatter_dimension=0, tiled=True),
        lax.psum_scatter(dec_fw_part, "lat", scatter_dimension=0, tiled=True),
    )
    return (
        grid_grad,
        mesh_grad,
        enc_proj_grad,
        node_proj_grad,
        dec_proj_grad,
        enc_feat_w_grad,
        dec_feat_w_grad,
    )


def mm(a, b, dims=NN, precision=None):
    return lax.dot_general(a, b, dims, precision=precision, preferred_element_type=F32)


def iota(shape, dim):
    return lax.broadcasted_iota(jnp.int32, shape, dim)


def halves(value):
    turn = jnp.tanh(value)
    up = 1.0 + turn
    silu = value * up
    return silu, up + silu * (1.0 - turn)


def hot(mask):
    return jnp.where(mask, 1.0, 0.0).astype(BF)


def split3(value):
    high = value.astype(BF).astype(F32)
    rest = value - high
    middle = rest.astype(BF).astype(F32)
    return high, middle, rest - middle


def stack_rows(feats):
    return -(-6 * feats // 16) * 16


def stack_terms(value, order):
    parts = split3(value)
    rows = len(order) * value.shape[0]
    blank = jnp.zeros((stack_rows(value.shape[0]) - rows, value.shape[1]), F32)
    return jnp.concatenate([*(parts[which] for which in order), blank], 0)


FEAT_ORDER = (0, 0, 1, 1, 2, 0)
WEIGHT_ORDER = (0, 1, 0, 1, 0, 2)


def fetch(sources, targets, sems):
    copies = [pltpu.make_async_copy(src, dst, sems.at[i]) for i, (src, dst) in enumerate(zip(sources, targets))]
    for copy in copies:
        copy.start()
    return copies


def feature_grad(terms, feats):
    total = terms[: 2 * feats] + terms[2 * feats : 4 * feats] + terms[4 * feats : 6 * feats]
    return jnp.where(iota(total.shape, 0) < feats, total, 0.0)


def encoder_kernel(
    cap, count, latent_any, weight_any, mesh_any, send_any, receive_any, feat_any, feat_w_any, serve_any,
    message, slope_far, served_out, own_out, px, picks, silus, slope, slope_sems,
    latent, weight, mesh, send, receive, feat, feat_w, serve, sems, latent_sems,
):
    sources = (send_any, feat_any, weight_any, feat_w_any, receive_any, mesh_any, serve_any)
    targets = (send, feat, weight, feat_w, receive, mesh, serve)
    copies = fetch(sources[:3], targets[:3], sems)
    edges = send.shape[1]
    grid_rows, width = latent.shape
    chips = message.shape[0]
    slots = served_out.shape[0]
    step = math.gcd(grid_rows, 256)
    cuts = [slice(start, start + step) for start in range(0, grid_rows, step)]
    chunks = fetch([latent_any.at[cut, :] for cut in cuts], [latent.at[cut, :] for cut in cuts], latent_sems)
    copies += fetch(sources[3:], targets[3:], sems.at[pl.ds(3, 4)])
    block = math.gcd(edges, 512)
    copies[0].wait()
    copies[1].wait()

    def build(start):
        part = slice(start, start + block)
        ids = jnp.broadcast_to(send[:, part].astype(F32), (128, block)).T
        for base in range(0, grid_rows, 128):
            lane = (iota((block, 128), 1) + base).astype(F32)
            picks[part, base : base + 128] = hot(ids == lane)

    for start in range(0, edges // 2, block):
        build(start)
    copies[2].wait()
    for cut, chunk in zip(cuts, chunks):
        chunk.wait()
    px[:grid_rows, :] = (0.5 * mm(latent[...], weight[...]).astype(BF).astype(F32)).astype(BF)
    for copy in copies[3:5]:
        copy.wait()
    terms = stack_terms(0.5 * feat_w[...], WEIGHT_ORDER)
    px[grid_rows:, :] = jnp.concatenate([terms, jnp.zeros((128 - terms.shape[0], width), F32)], 0).astype(BF)
    stores = []
    for start in range(0, edges, block):
        part = slice(start, start + block)
        if start >= edges // 2:
            build(start)
        pre = mm(picks[part, :grid_rows], px[:grid_rows, :])
        pre = pre + mm(stack_terms(feat[:, part], FEAT_ORDER).astype(BF), px[grid_rows : grid_rows + 32, :], TN)
        silu, double = halves(pre)
        slope[part, :] = double.astype(BF)
        out = pltpu.make_async_copy(slope.at[part, :], slope_far.at[part, :], slope_sems.at[len(stores)])
        out.start()
        stores.append(out)
        silus[part, :] = silu.astype(BF)
    live = iota((1, edges), 1) < count[0]
    total = mm(hot(iota((slots, edges), 0) == jnp.where(live, receive[...], -1)), silus[...])
    copies[5].wait()
    copies[6].wait()
    owners = slots // cap
    ids = serve[...]
    spread = hot(iota((owners, slots), 0) == lax.div(iota((owners, slots), 1), cap))
    turn = iota((cap, slots), 0) == iota((cap, slots), 1) % cap
    digits = []
    for value in (lax.shift_right_logical(ids, 8), ids & 255):
        wide = mm(value.astype(F32).astype(BF), spread)
        digits.append(jnp.sum(jnp.where(turn, wide, 0.0), 0, keepdims=True))
    id_row = (digits[0] * 256.0 + digits[1]).astype(jnp.int32)
    served = mm(hot(iota((mesh.shape[0], slots), 0) == id_row), mesh[...], TN)
    served_out[...] = served.astype(BF)
    lane = iota((slots, 128), 1)
    back = iota((slots, 128), 0)
    wide = mm(digits[0].astype(BF), hot(lane == back)) + mm(digits[1].astype(BF), hot(lane == back + slots))
    id_rows = jnp.where(iota((8, 128), 0) == 0, wide, 0.0)
    half = total.astype(BF)
    own_out[...] = (total - half.astype(F32)).astype(BF)
    for chip in range(chips):
        write_slots(message, chip, half)
        rows = served[2 * cap * chip : 2 * cap * (chip + 1)]
        tail = [rows[:, base : base + 128] for base in range(0, width, 128)]
        message[chip, slots * (width // 128) :, :] = jnp.concatenate([*tail, id_rows], 0).astype(BF)
    for out in stores:
        out.wait()


def write_slots(message, chip, value):
    slots = value.shape[0]
    for part in range(value.shape[1] // 128):
        message[chip, part * slots : (part + 1) * slots, :] = value[:, part * 128 : (part + 1) * 128]


def slot_rows(ref, slots, width):
    parts = [
        jnp.concatenate([ref[chip, base : base + slots, :] for chip in range(ref.shape[0])], 0)
        for base in range(0, slots * (width // 128), slots)
    ]
    return jnp.concatenate(parts, 1)


def gathered_slots(piece, chips, core, cap, shape, dim):
    slots = 2 * chips * cap
    index = iota(shape, dim)
    chip = lax.div(index, slots)
    slot = index - chip * slots
    band = 2 * chip + jnp.where(piece == 0, core, 1 - core)
    return band, lax.div(slot, cap), lax.rem(slot, cap)


def holder_of(shape, dim, chips, core):
    index = iota(shape, dim)
    return jnp.where(index < chips, 2 * index + core, 2 * (index - chips) + 1 - core)


def slot_matches(first, second, me, cap, mesh_rows, width):
    chips = first.shape[0]
    owners = 2 * chips
    slots = owners * cap
    span = chips * slots
    parts = width // 128
    core = lax.rem(me, 2)
    table = jnp.zeros((owners, 128), F32)
    latent = jnp.zeros((slots, width), F32)
    for piece, ref in enumerate((first, second)):
        ids, rows = [], []
        for chip in range(chips):
            tail = ref[chip, slots * parts :, :].astype(F32)
            ids.append(tail[8 * parts :])
            rows.append(jnp.concatenate([tail[8 * part : 8 * part + 8] for part in range(parts)], 1))
        ids = jnp.concatenate(ids, 0).astype(BF)
        rows = jnp.concatenate(rows, 0).astype(BF)
        shape = (owners, 8 * chips)
        table = table + mm(hot(iota(shape, 1) == (iota(shape, 0) - piece * chips) * 8), ids)
        shape = (slots, 8 * chips)
        window = iota(shape, 0)
        owner = lax.div(window, cap)
        held = lax.rem(owner, 2) == (core if piece == 0 else 1 - core)
        at = lax.div(owner, 2) * 8 + cap * core + lax.rem(window, cap)
        latent = latent + mm(hot(held & (iota(shape, 1) == at)), rows)
    digits = table.astype(BF)
    shape = (slots, owners)
    mine = mm(hot(holder_of(shape, 1, chips, core) == lax.div(iota(shape, 0), cap)), digits)
    lane = iota((slots, 128), 1) - cap * me - lax.rem(iota((slots, 128), 0), cap)
    scaled = jnp.where(lane == 0, 256.0 * mine, jnp.where(lane == slots, mine, 0.0))
    own_key = jnp.sum(scaled, 1, keepdims=True)
    own_key = own_key + (lax.div(iota((slots, 1), 0), cap) * mesh_rows).astype(F32)
    keys, same = [], []
    for piece in range(2):
        band, owner, place = gathered_slots(piece, chips, core, cap, (1, span), 1)
        at = iota((128, span), 0) - cap * band - place
        weight = jnp.where(at == 0, 256.0, jnp.where(at == slots, 1.0, 0.0)).astype(BF)
        value = jnp.where(holder_of((owners, 1), 0, chips, core) == owner, mm(digits, weight), 0.0)
        key = jnp.sum(value, 0, keepdims=True) + (owner * mesh_rows).astype(F32)
        keys.append(key)
        same.append(hot(key == own_key))
    return keys, same, latent


def decoder_picks(
    after, send_any, feat_any, node_any, dec_any, feat_w_any,
    pick, pick_turned, node_w, dec_w, feat_w, send, feat, sems,
):
    sources = (send_any, feat_any, node_any, dec_any, feat_w_any)
    copies = fetch(sources, (send, feat, node_w, dec_w, feat_w), sems)
    slots = after.shape[0]
    grid_rows = send.shape[1]
    copies[0].wait()
    copies[1].wait()
    block = math.gcd(grid_rows, 512)
    for k in range(3):
        for start in range(0, grid_rows, block):
            part = slice(start, start + block)
            to = slice(k * grid_rows + start, k * grid_rows + start + block)
            to_slot = jnp.where(iota((slots, block), 0) == send[k : k + 1, part], 1.0, 0.0)
            rows = jnp.concatenate([to_slot, stack_terms(feat[k, :, part], FEAT_ORDER)], 0)
            pick[:, to] = rows.astype(BF)
            rows = jnp.concatenate([rows, jnp.zeros((128 - rows.shape[0], block), F32)], 0)
            pick_turned[to, :] = rows.T.astype(BF)
    for copy in copies[2:]:
        copy.wait()


def encoder_picks(
    count, latent, receive_any, dec_any, node_any, send_any, feat_any,
    to_edge, latent_turned, dec_turned, node_turned, send, feat, receive, dec_w, node_w, sems,
):
    sources = (receive_any, dec_any, node_any, send_any, feat_any)
    copies = fetch(sources, (receive, dec_w, node_w, send, feat), sems)
    edges = receive.shape[1]
    copies[0].wait()
    block = math.gcd(edges, 512)
    for start in range(0, edges, block):
        part = slice(start, start + block)
        live = iota((1, block), 1) + start < count[0]
        slot = jnp.where(live, receive[:, part], -1)
        to_edge[part, :] = jnp.where(iota((128, block), 0) == slot, 1.0, 0.0).T.astype(BF)
    for copy in copies[1:3]:
        copy.wait()
    dec_turned[...] = dec_w[...].T
    node_turned[...] = node_w[...].T
    latent_turned[...] = latent[...].T
    for copy in copies[3:]:
        copy.wait()


def decoder_kernel(
    cap, mesh_rows, place, first, second, extra, rest, pick, pick_turned, node_w, dec_w, feat_w, cotangent,
    message, keys_out, same_out, slope_out, grad_out, mine_out, rest_out,
):
    slots, width = extra.shape
    keys, same, latent = slot_matches(first, second, place[0], cap, mesh_rows, width)
    agg = jnp.zeros((slots, width), F32)
    for piece, ref in enumerate((first, second)):
        keys_out[piece : piece + 1, :] = keys[piece]
        same_out[piece] = same[piece]
        agg = agg + mm(same[piece], slot_rows(ref, slots, width))
    shape = (same[0].shape[1], slots)
    chosen = hot(iota(shape, 0) == slots * lax.div(place[0], 2) + iota(shape, 1))
    mine = mm(same[0], chosen).astype(BF)
    mine_out[...] = mine
    agg = agg + mm(mine, rest[...])
    silu, double = halves(0.5 * agg)
    slope_out[...] = 0.25 * double
    hmesh = (latent + mm(silu.astype(BF), node_w[...])).astype(BF)
    proj = mm(hmesh, dec_w[...]).astype(BF)
    rows = pick.shape[0]
    blank = jnp.zeros((128 - rows, width), F32)
    terms = jnp.concatenate([stack_terms(0.5 * feat_w[...], WEIGHT_ORDER), blank], 0).astype(BF)
    table = jnp.concatenate([(0.5 * proj.astype(F32)).astype(BF), terms], 0)
    grid_rows = cotangent.shape[0]
    block = math.gcd(grid_rows, 512)
    total = jnp.zeros((rows, width), F32)
    for start in range(0, grid_rows, block):
        cot = cotangent[start : start + block, :].astype(F32)
        for base in range(start, 3 * grid_rows, grid_rows):
            part = slice(base, base + block)
            double = halves(mm(pick_turned[part, :], table))[1]
            total = total + mm(pick[:, part], (cot * double).astype(BF))
    total = 0.5 * total
    half = total[:slots].astype(BF)
    rest_out[...] = (total[:slots] - half.astype(F32)).astype(BF)
    grad_out[...] = feature_grad(total[slots:], feat_w.shape[0])
    chips = message.shape[0]
    share = width // chips
    step = slots * share // 128
    for chip in range(chips):
        write_slots(message, chip, half)
        columns = extra[:, chip * share : (chip + 1) * share].astype(F32)
        columns = jnp.concatenate([columns[base : base + step] for base in range(0, slots, step)], 1)
        message[chip, slots * (width // 128) :, :] = columns.astype(BF)


def backward_kernel(
    place, first, second, same, mine, rest, agg_slope, dec_grad, to_edge, latent_turned, dec_turned, node_turned,
    send, feat, slope, dpx_far, dpx, give, sums_out, grads, dpx_sems,
):
    slots = same.shape[1]
    edges, width = grads.shape
    grid_rows = dpx.shape[0]
    feats = feat.shape[0]
    core = lax.rem(place[0], 2)
    dproj = mm(same[0], slot_rows(first, slots, width)) + mm(same[1], slot_rows(second, slots, width))
    dproj = dproj + mm(mine[...], rest[...])
    high = dproj.astype(BF)
    low = (dproj - high.astype(F32)).astype(BF)
    dhmesh = mm(jnp.concatenate([high, low], 0), dec_turned[...])
    mesh_grad = (dhmesh[:slots] + dhmesh[slots:]).astype(BF)
    dagg = mm(mesh_grad, node_turned[...]) * agg_slope[...]
    dagg = jnp.concatenate([dagg, jnp.zeros((128 - slots, width), F32)], 0).astype(BF)
    block = math.gcd(edges, 512)
    for start in range(0, edges, block):
        cut = slice(start, start + block)
        grads[cut, :] = (mm(to_edge[cut, :], dagg) * slope[cut, :].astype(F32)).astype(BF)
    step = math.gcd(grid_rows, 256)
    stores = []
    for start in range(0, grid_rows, step):
        cut = slice(start, start + step)
        from_row = hot(iota((step, edges), 0) + start == send[...])
        dpx[cut, :] = mm(from_row, grads[...]).astype(BF)
        out = pltpu.make_async_copy(dpx.at[cut, :], dpx_far.at[cut, :], dpx_sems.at[len(stores)])
        out.start()
        stores.append(out)
    enc_grad = feature_grad(mm(stack_terms(feat[...], FEAT_ORDER).astype(BF), grads[...]), feats)
    sums = jnp.where(iota(enc_grad.shape, 0) < feats, enc_grad, pltpu.roll(dec_grad[...], feats, 0))
    sums_out[...] = sums
    write_shares(give, 1 - core, latent_turned, dpx, sums)
    for out in stores:
        out.wait()


def write_shares(out, side, latent_turned, dpx, sums):
    chips = out.shape[0]
    width = dpx.shape[1]
    rows = width // (2 * chips)
    left = [latent_turned[pl.ds((2 * chip + side) * rows, rows), :] for chip in range(chips)]
    product = mm(jnp.concatenate(left, 0), dpx[...])
    blank = jnp.zeros((8, 128 - rows), F32)
    for chip in range(chips):
        block = product[chip * rows : (chip + 1) * rows]
        pair = [sums[:, base : base + rows] for base in (2 * chip * rows, (2 * chip + 1) * rows)]
        small = jnp.concatenate([jnp.where(side == 0, pair[0], pair[1]), blank], 1)
        pieces = [block[:, base : base + 128] for base in range(0, width, 128)]
        out[chip] = jnp.concatenate([*pieces, small], 0).astype(out.dtype)


def keep_kernel(place, latent_turned, dpx, sums, keep):
    write_shares(keep, lax.rem(place[0], 2), latent_turned, dpx, sums[...])


def pair_kernel(keep, given, out):
    out[...] = (keep[...] + given[...].astype(F32)).astype(BF)


def final_kernel(feats, arrived, out, enc_out, dec_out):
    total = jnp.sum(arrived[...].astype(F32), 0)
    rows, width = out.shape
    for part in range(width // 128):
        out[:, part * 128 : (part + 1) * 128] = total[part * rows : (part + 1) * rows]
    base = rows * (width // 128)
    enc_out[...] = total[base : base + feats, :rows]
    dec_out[...] = total[base + feats : base + 2 * feats, :rows]


def beside_kernel(
    cap, mesh_rows, place, keys, node_any, first_any, second_any, first_back_any, second_back_any, dec_any, dpx_any,
    weight_any, cot_any, mesh_out, dec_out, node_out, grid_out,
    node_w, first, second, first_back, second_back, dec_w, dpx, weight, cotangent, sems,
):
    sources = (
        first_any, second_any, node_any, first_back_any, second_back_any, dec_any, dpx_any, weight_any, cot_any,
    )
    targets = (first, second, node_w, first_back, second_back, dec_w, dpx, weight, cotangent)
    copies = fetch(sources, targets, sems)
    width = node_w.shape[0]
    chips = first.shape[0]
    owners = 2 * chips
    slots = owners * cap
    span = chips * slots
    me = place[0]
    core = lax.rem(me, 2)
    block = width // owners
    key = jnp.concatenate([keys[0:1, :], keys[1:2, :]], 1)
    down = jnp.broadcast_to(key, (128, 2 * span)).T
    same = jnp.concatenate([hot(down == key[:, base : base + 128]) for base in range(0, 2 * span, 128)], 1)
    for copy in copies[:3]:
        copy.wait()
    forward = jnp.concatenate([slot_rows(ref, slots, width) for ref in (first, second)], 0)
    act = halves(0.5 * mm(same, forward))[0].astype(BF)
    shape = (width, 128)
    mine = hot((iota(shape, 0) == block * me + iota(shape, 1)) & (iota(shape, 1) < block))
    node_cols = mm(node_w[...], mine).astype(BF)
    both = mm(act, jnp.concatenate([node_cols, mine], 1))
    step = slots * 2 * block // 128
    pieces = [gathered_slots(piece, chips, core, cap, (span, 1), 0) for piece in range(2)]
    band, owner, turn = [jnp.concatenate([a, b], 0) for a, b in zip(*pieces)]
    source = jnp.where(lax.rem(owner, 2) == core, 0, chips) + lax.div(owner, 2)
    number = cap * band + turn
    at = lax.div(number, step) * (owners * step) + source * step + lax.rem(number, step)
    for copy in copies[3:]:
        copy.wait()
    back = jnp.concatenate([slot_rows(ref, slots, width) for ref in (first_back, second_back)], 0)
    tail = slots * (width // 128)
    columns = [ref[chip, tail:, :] for ref in (first_back, second_back) for chip in range(chips)]
    columns = jnp.concatenate(columns, 0)
    shape = (128, 128)
    folded = []
    for base in range(0, 128, 2 * block):
        fold = hot((iota(shape, 0) == base + block * core + iota(shape, 1)) & (iota(shape, 1) < block))
        folded.append(mm(columns, fold).astype(BF))
    latent = mm(hot(iota((2 * span, 2 * span), 1) == at), jnp.concatenate(folded, 0))
    hmesh = (both[:, :128] + latent).astype(BF)
    left = jnp.concatenate([hmesh, both[:, 128:].astype(BF)], 1)
    sums = mm(left, back, TN)
    dec_out[...] = sums[:block]
    own = (me * mesh_rows + iota((mesh_out.shape[0], 2 * span), 0)).astype(F32)
    dproj = jnp.concatenate([mm(hot(own == key), back), sums[128 : 128 + block]], 0)
    high = dproj.astype(BF)
    low = (dproj - high.astype(F32)).astype(BF)
    turned = mm(high, dec_w[...], NT) + mm(low, dec_w[...], NT)
    mesh = mesh_out.shape[0]
    mesh_out[...] = turned[:mesh].astype(BF)
    node_out[...] = turned[mesh:]
    grid_out[...] = (cotangent[...].astype(F32) + mm(dpx[...], weight[...], NT)).astype(BF)


SMEM = pl.BlockSpec(memory_space=pltpu.SMEM)
VMEM = pl.BlockSpec(memory_space=pltpu.VMEM)
FAR = pl.BlockSpec(memory_space=pltpu.HBM)


def kernel_call(body, name, scalars, near, far, outs, scratch, flops, limit, out_specs=None, pin=False, last=(), kept=0):
    shapes = [jax.ShapeDtypeStruct(shape, dtype) for shape, dtype in outs]
    out_specs = out_specs or [VMEM] * len(shapes)
    pinned = [pltpu.HBM(s.shape, s.dtype) if spec is FAR else s for s, spec in zip(shapes, out_specs)]
    if pin:
        far = [pltpu.with_memory_space_constraint(a, pltpu.HBM) for a in far]
    moved = sum(a.size * a.dtype.itemsize for a in (*near, *far)) + sum(s.size * s.dtype.itemsize for s in shapes)
    buffers = [pltpu.VMEM(a.shape, a.dtype) for a in far[: len(far) - kept]]
    if far:
        buffers.append(pltpu.SemaphoreType.DMA((len(far),)))
    return pl.pallas_call(
        body,
        name=name,
        out_shape=pinned,
        in_specs=[SMEM] * len(scalars) + [VMEM] * len(near) + [FAR] * len(far),
        out_specs=out_specs,
        scratch_shapes=[*scratch, *buffers, *last],
        compiler_params=pltpu.CompilerParams(vmem_limit_bytes=limit * MIB),
        cost_estimate=pl.CostEstimate(flops=flops, bytes_accessed=moved, transcendentals=0),
    )(*scalars, *near, *far)


def gather_plan(
    grid_latent,
    mesh_latent,
    grid_cotangent,
    enc_sender,
    enc_receiver,
    enc_feat,
    enc_count,
    dec_sender,
    dec_feat,
    serve_rows,
    enc_proj,
    node_proj,
    dec_proj,
    enc_feat_w,
    dec_feat_w,
):
    owners = lax.axis_size("lat")
    chips = owners // 2
    cap = serve_rows.shape[2]
    slots = owners * cap
    mesh_rows, width = mesh_latent.shape
    grid_rows = grid_latent.shape[0]
    edges = enc_sender.shape[0]
    feats = enc_feat.shape[0]
    block = width // owners
    span = chips * slots
    parts = width // 128
    share = width // chips
    groups = [[core + 2 * chip for chip in range(chips)] for core in range(2)]
    swap = [(index, index ^ 1) for index in range(owners)]
    place = lax.axis_index("lat").astype(jnp.int32).reshape(1)

    def gather(message, *later):
        first = lax.all_to_all(message, "lat", 0, 0, tiled=True, axis_index_groups=groups)
        first, *later = lax.optimization_barrier((first, *later))
        return first, lax.ppermute(first, "lat", swap), *later

    send = enc_sender.reshape(1, edges)
    receive = enc_receiver.reshape(1, edges)
    message, slope, served, rest = kernel_call(
        lambda *refs: encoder_kernel(cap, *refs),
        "encoder",
        [enc_count],
        [],
        [grid_latent, enc_proj, mesh_latent, send, receive, enc_feat, enc_feat_w.T, serve_rows[0].T],
        [
            ((chips, parts * (slots + 8) + 8, 128), BF),
            ((edges, width), BF),
            ((slots, width), BF),
            ((slots, width), BF),
        ],
        [
            pltpu.VMEM((grid_rows + 128, width), BF),
            pltpu.VMEM((edges, grid_rows), BF),
            pltpu.VMEM((edges, width), BF),
            pltpu.VMEM((edges, width), BF),
            pltpu.SemaphoreType.DMA((edges // math.gcd(edges, 512),)),
        ],
        2 * edges * grid_rows * width,
        28,
        [VMEM, FAR, VMEM, VMEM],
        pin=True,
        last=[pltpu.SemaphoreType.DMA((grid_rows // math.gcd(grid_rows, 256),))],
    )
    term_rows = stack_rows(feats)
    first, second, served = gather(message, served)
    pick, pick_turned, near_node, near_dec, near_feat_w = kernel_call(
        decoder_picks,
        "decoder_picks",
        [],
        [served],
        [dec_sender, dec_feat, node_proj, dec_proj, dec_feat_w.T],
        [
            ((slots + term_rows, 3 * grid_rows), BF),
            ((3 * grid_rows, 128), BF),
            ((width, width), BF),
            ((width, width), BF),
            ((feats, width), F32),
        ],
        [],
        2000 * MIB,
        16,
        pin=True,
        kept=3,
    )
    message, keys, same, agg_slope, dec_grad, mine, rest = kernel_call(
        lambda *refs: decoder_kernel(cap, mesh_rows, *refs),
        "decoder",
        [place],
        [first, second, served, rest, pick, pick_turned, near_node, near_dec, near_feat_w, grid_cotangent],
        [],
        [
            ((chips, parts * slots + slots * share // 128, 128), BF),
            ((2, span), F32),
            ((2, slots, span), BF),
            ((slots, width), F32),
            ((2 * feats, width), F32),
            ((slots, slots), BF),
            ((slots, width), BF),
        ],
        [],
        24 * grid_rows * 128 * width,
        20,
    )
    first_back, second_back, pick_count = gather(message, enc_count)
    to_edge, latent_turned, dec_turned, node_turned, near_send, near_feat = kernel_call(
        encoder_picks,
        "encoder_picks",
        [pick_count],
        [grid_latent],
        [receive, dec_proj, node_proj, send, enc_feat],
        [
            ((edges, 128), BF),
            ((width, grid_rows), BF),
            ((width, width), BF),
            ((width, width), BF),
            ((1, edges), jnp.int32),
            ((feats, edges), F32),
        ],
        [],
        2000 * MIB,
        16,
        pin=True,
        kept=2,
    )
    dpx_far, dpx, give, sums = kernel_call(
        backward_kernel,
        "backward",
        [place],
        [
            first_back,
            second_back,
            same,
            mine,
            rest,
            agg_slope,
            dec_grad,
            to_edge,
            latent_turned,
            dec_turned,
            node_turned,
            near_send,
            near_feat,
            slope,
        ],
        [],
        [
            ((grid_rows, width), BF),
            ((grid_rows, width), BF),
            ((chips, parts * block + 8, 128), BF),
            ((2 * feats, width), F32),
        ],
        [
            pltpu.VMEM((edges, width), BF),
            pltpu.SemaphoreType.DMA((grid_rows // math.gcd(grid_rows, 256),)),
        ],
        2 * edges * grid_rows * width,
        24,
        [FAR, VMEM, VMEM, VMEM],
    )
    (keep,) = kernel_call(
        keep_kernel,
        "keep",
        [place],
        [latent_turned, dpx, sums],
        [],
        [((chips, parts * block + 8, 128), F32)],
        [],
        grid_rows * width * width,
        16,
    )
    given = lax.ppermute(give, "lat", swap)
    (pair,) = kernel_call(pair_kernel, "pair", [], [keep, given], [], [(give.shape, BF)], [], keep.size, 8)
    pair, keys, dpx_far = lax.optimization_barrier((pair, keys, dpx_far))
    arrived = lax.all_to_all(pair, "lat", 0, 0, tiled=True, axis_index_groups=groups)
    mesh_grad, dec_proj_grad, node_proj_grad, grid_grad = kernel_call(
        lambda *refs: beside_kernel(cap, mesh_rows, *refs),
        "beside",
        [place],
        [keys],
        [
            node_proj,
            first,
            second,
            first_back,
            second_back,
            dec_proj,
            dpx_far,
            enc_proj,
            grid_cotangent,
        ],
        [
            ((mesh_rows, width), BF),
            ((block, width), F32),
            ((block, width), F32),
            ((grid_rows, width), BF),
        ],
        [],
        2 * (2 * span) * (2 * span) * width,
        30,
        pin=True,
    )
    enc_proj_grad, enc_feat_grad, dec_feat_grad = kernel_call(
        lambda *refs: final_kernel(feats, *refs),
        "final",
        [],
        [arrived],
        [],
        [((block, width), F32), ((feats, block), F32), ((feats, block), F32)],
        [],
        arrived.size,
        8,
    )
    return (
        grid_grad,
        mesh_grad,
        enc_proj_grad,
        node_proj_grad,
        dec_proj_grad,
        enc_feat_grad.T,
        dec_feat_grad.T,
    )


def gather_fits(args):
    mesh_latent, serve_rows = args[1], args[9]
    owners, cap = serve_rows.shape[1], serve_rows.shape[2]
    width = mesh_latent.shape[1]
    chips = owners // 2
    return (
        owners % 2 == 0
        and 2 * cap == 8
        and owners * cap <= 64
        and width % 128 == 0
        and width % (8 * owners) == 0
        and 128 % (width // chips) == 0
        and owners * cap * (width // chips) % 2048 == 0
        and mesh_latent.shape[0] <= 65536
        and mesh_latent.shape[0] * owners < 1 << 24
        and args[0].shape[0] % 128 == 0
        and args[3].shape[0] % 128 == 0
        and args[5].shape[0] == 4
    )


def per_device(*args):
    return gather_plan(*args) if gather_fits(args) else owner_plan(*args)


def solution(mesh):
    placed = (
        P(("member", "lat"), None),
        P(("member", "lat"), None),
        P(("member", "lat"), None),
        P(("member", "lat")),
        P(("member", "lat")),
        P(None, ("member", "lat")),
        P(("member", "lat")),
        P(None, ("member", "lat")),
        P(None, None, ("member", "lat")),
        P(("member", "lat"), None, None),
        P(),
        P(),
        P(),
        P(),
        P(),
    )
    return jax.shard_map(
        per_device,
        mesh=mesh,
        in_specs=placed,
        out_specs=(
            P(("member", "lat"), None),
            P(("member", "lat"), None),
            P(("member", "lat"), None),
            P(("member", "lat"), None),
            P(("member", "lat"), None),
            P(("member", "lat"), None),
            P(("member", "lat"), None),
        ),
        check_vma=False,
    )
```

```python
import math

import jax
import jax.numpy as jnp
from jax import lax
from jax.experimental import pallas as pl
from jax.experimental.pallas import tpu as pltpu
from jax.sharding import PartitionSpec as P

BF = jnp.bfloat16
F32 = jnp.float32
HI = lax.Precision.HIGHEST
MIB = 1 << 20
NN = (((1,), (0,)), ((), ()))
NT = (((1,), (1,)), ((), ()))
TN = (((0,), (0,)), ((), ()))


def silu_grad(value):
    sig = jax.nn.sigmoid(value)
    return sig * (1.0 + value * (1.0 - sig))


def owner_plan(
    grid_latent,
    mesh_latent,
    grid_cotangent,
    enc_sender,
    enc_receiver,
    enc_feat,
    enc_count,
    dec_sender,
    dec_feat,
    serve_rows,
    enc_proj,
    node_proj,
    dec_proj,
    enc_feat_w,
    dec_feat_w,
):
    highest = lax.Precision.HIGHEST
    owners_count = lax.axis_size("lat")
    serve_flat = serve_rows.reshape(-1)
    slot_total = serve_flat.shape[0]
    per_owner = slot_total // owners_count
    mesh_rows = mesh_latent.shape[0]
    grid_rows = grid_latent.shape[0]
    width = grid_latent.shape[1]
    edge_slots = enc_sender.shape[0]
    edge_block = math.gcd(edge_slots, 512)
    grid_block = math.gcd(grid_rows, 512)
    live_count = enc_count[0]
    slot_ids = lax.iota(jnp.int32, slot_total)[:, None]
    row_ids = lax.iota(jnp.int32, grid_rows)[:, None]

    def to_window(rows):
        outgoing = jnp.take(rows, serve_flat, axis=0).reshape(owners_count, per_owner, width)
        arrived = lax.all_to_all(outgoing, "lat", split_axis=0, concat_axis=0, tiled=True)
        return arrived.reshape(slot_total, width)

    def to_owners(partial_value):
        arrived = lax.all_to_all(
            partial_value.reshape(owners_count, per_owner, width),
            "lat",
            split_axis=0,
            concat_axis=0,
            tiled=True,
        )
        return jax.ops.segment_sum(
            arrived.reshape(slot_total, width), serve_flat, num_segments=mesh_rows
        )

    px = jnp.dot(grid_latent, enc_proj, preferred_element_type=jnp.float32).astype(jnp.bfloat16)

    def enc_block(start):
        senders = lax.dynamic_slice_in_dim(enc_sender, start, edge_block)
        receivers = lax.dynamic_slice_in_dim(enc_receiver, start, edge_block)
        feats = lax.dynamic_slice_in_dim(enc_feat, start, edge_block, 1)
        pre = jnp.take(px, senders, axis=0).astype(jnp.float32) + jnp.einsum(
            "fb,lf->bl", feats, enc_feat_w, precision=highest
        )
        live = (lax.iota(jnp.int32, edge_block) + start < live_count)[:, None]
        onehot = (receivers[None, :] == slot_ids).astype(jnp.bfloat16)
        return (pre, live, onehot, senders, feats)

    block_steps = edge_slots // edge_block

    def enc_forward(index, partial_value):
        pre, live, onehot, senders, feats = enc_block(index * edge_block)
        message = jnp.where(live, jax.nn.silu(pre), 0.0).astype(jnp.bfloat16)
        return partial_value + jnp.dot(onehot, message, preferred_element_type=jnp.float32)

    enc_partial = lax.fori_loop(
        0, block_steps, enc_forward, jnp.zeros((slot_total, width), jnp.float32)
    )
    agg = to_owners(enc_partial)
    act = jax.nn.silu(agg).astype(jnp.bfloat16)
    hmesh = (
        mesh_latent.astype(jnp.float32)
        + jnp.dot(act, node_proj, preferred_element_type=jnp.float32)
    ).astype(jnp.bfloat16)
    proj_window = to_window(
        jnp.dot(hmesh, dec_proj, preferred_element_type=jnp.float32).astype(jnp.bfloat16)
    )

    def dec_backward(index, carry):
        dproj, dfw = carry
        start = index * grid_block
        cot = lax.dynamic_slice_in_dim(grid_cotangent, start, grid_block).astype(jnp.float32)
        for k in range(3):
            senders = lax.dynamic_slice_in_dim(dec_sender[k], start, grid_block)
            feats = lax.dynamic_slice_in_dim(dec_feat[k], start, grid_block, 1)
            pre = jnp.take(proj_window, senders, axis=0).astype(jnp.float32) + jnp.einsum(
                "fg,lf->gl", feats, dec_feat_w, precision=highest
            )
            grad_half = (cot * silu_grad(pre)).astype(jnp.bfloat16)
            slot_hot = (senders[None, :] == slot_ids).astype(jnp.bfloat16)
            dproj = dproj + jnp.dot(slot_hot, grad_half, preferred_element_type=jnp.float32)
            dfw = dfw + jnp.einsum(
                "gl,fg->lf", grad_half.astype(jnp.float32), feats, precision=highest
            )
        return (dproj, dfw)

    start_carry = (
        jnp.zeros((slot_total, width), jnp.float32),
        jnp.zeros((width, dec_feat_w.shape[1]), jnp.float32),
    )
    dproj_window, dec_fw_part = lax.fori_loop(0, grid_rows // grid_block, dec_backward, start_carry)
    dec_weight = dec_proj.astype(jnp.float32)
    dproj = to_owners(dproj_window)
    dhmesh = jnp.dot(dproj, dec_weight.T, precision=highest)
    dec_proj_part = jnp.dot(hmesh.astype(jnp.float32).T, dproj, precision=highest)
    mesh_grad = dhmesh.astype(jnp.bfloat16)
    node_proj_part = jnp.dot(act.T, mesh_grad, preferred_element_type=jnp.float32)
    dagg = (
        jnp.dot(mesh_grad, node_proj.T, preferred_element_type=jnp.float32) * silu_grad(agg)
    ).astype(jnp.bfloat16)
    dagg_window = to_window(dagg)

    def enc_backward(index, carry):
        dpx, dew = carry
        pre, live, onehot, senders, feats = enc_block(index * edge_block)
        upstream = jnp.einsum("wb,wl->bl", onehot, dagg_window, preferred_element_type=jnp.float32)
        grad_half = jnp.where(live, upstream * silu_grad(pre), 0.0).astype(jnp.bfloat16)
        row_hot = (senders[None, :] == row_ids).astype(jnp.bfloat16)
        dpx = dpx + jnp.dot(row_hot, grad_half, preferred_element_type=jnp.float32)
        dew = dew + jnp.einsum("bl,fb->lf", grad_half.astype(jnp.float32), feats, precision=highest)
        return (dpx, dew)

    start_back = (
        jnp.zeros((grid_rows, width), jnp.float32),
        jnp.zeros((width, enc_feat_w.shape[1]), jnp.float32),
    )
    dpx_sum, enc_fw_part = lax.fori_loop(0, block_steps, enc_backward, start_back)
    dpx = dpx_sum.astype(jnp.bfloat16)
    enc_proj_part = jnp.dot(grid_latent.T, dpx, preferred_element_type=jnp.float32)
    grid_grad = (
        grid_cotangent.astype(jnp.float32)
        + jnp.dot(dpx, enc_proj.T, preferred_element_type=jnp.float32)
    ).astype(jnp.bfloat16)
    enc_proj_grad, node_proj_grad, dec_proj_grad, enc_feat_w_grad, dec_feat_w_grad = (
        lax.psum_scatter(enc_proj_part, "lat", scatter_dimension=0, tiled=True),
        lax.psum_scatter(node_proj_part, "lat", scatter_dimension=0, tiled=True),
        lax.psum_scatter(dec_proj_part, "lat", scatter_dimension=0, tiled=True),
        lax.psum_scatter(enc_fw_part, "lat", scatter_dimension=0, tiled=True),
        lax.psum_scatter(dec_fw_part, "lat", scatter_dimension=0, tiled=True),
    )
    return (
        grid_grad,
        mesh_grad,
        enc_proj_grad,
        node_proj_grad,
        dec_proj_grad,
        enc_feat_w_grad,
        dec_feat_w_grad,
    )


def mm(a, b, dims=NN, precision=None):
    return lax.dot_general(a, b, dims, precision=precision, preferred_element_type=F32)


def iota(shape, dim):
    return lax.broadcasted_iota(jnp.int32, shape, dim)


def halves(value):
    turn = jnp.tanh(value)
    up = 1.0 + turn
    silu = value * up
    return silu, up + silu * (1.0 - turn)


def hot(mask):
    return jnp.where(mask, 1.0, 0.0).astype(BF)


def split3(value):
    high = value.astype(BF).astype(F32)
    rest = value - high
    middle = rest.astype(BF).astype(F32)
    return high, middle, rest - middle


def stack_rows(feats):
    return -(-6 * feats // 16) * 16


def stack_terms(value, order):
    parts = split3(value)
    rows = len(order) * value.shape[0]
    blank = jnp.zeros((stack_rows(value.shape[0]) - rows, value.shape[1]), F32)
    return jnp.concatenate([*(parts[which] for which in order), blank], 0)


FEAT_ORDER = (0, 0, 1, 1, 2, 0)
WEIGHT_ORDER = (0, 1, 0, 1, 0, 2)


def fetch(sources, targets, sems):
    copies = [pltpu.make_async_copy(src, dst, sems.at[i]) for i, (src, dst) in enumerate(zip(sources, targets))]
    for copy in copies:
        copy.start()
    return copies


def feature_grad(terms, feats):
    total = terms[: 2 * feats] + terms[2 * feats : 4 * feats] + terms[4 * feats : 6 * feats]
    return jnp.where(iota(total.shape, 0) < feats, total, 0.0)


def encoder_kernel(
    cap, count, latent_any, weight_any, mesh_any, send_any, receive_any, feat_any, feat_w_any, serve_any,
    message, slope_far, served_out, own_out, px, picks, silus, slope, slope_sems,
    latent, weight, mesh, send, receive, feat, feat_w, serve, sems, latent_sems,
):
    sources = (send_any, feat_any, weight_any, feat_w_any, receive_any, mesh_any, serve_any)
    targets = (send, feat, weight, feat_w, receive, mesh, serve)
    copies = fetch(sources[:3], targets[:3], sems)
    edges = send.shape[1]
    grid_rows, width = latent.shape
    chips = message.shape[0]
    slots = served_out.shape[0]
    step = math.gcd(grid_rows, 256)
    cuts = [slice(start, start + step) for start in range(0, grid_rows, step)]
    chunks = fetch([latent_any.at[cut, :] for cut in cuts], [latent.at[cut, :] for cut in cuts], latent_sems)
    copies += fetch(sources[3:], targets[3:], sems.at[pl.ds(3, 4)])
    block = math.gcd(edges, 512)
    copies[0].wait()
    copies[1].wait()
    for start in range(0, edges, block):
        part = slice(start, start + block)
        ids = jnp.broadcast_to(send[:, part].astype(F32), (128, block)).T
        for base in range(0, grid_rows, 128):
            lane = (iota((block, 128), 1) + base).astype(F32)
            picks[part, base : base + 128] = hot(ids == lane)
    copies[2].wait()
    for cut, chunk in zip(cuts, chunks):
        chunk.wait()
    px[:grid_rows, :] = (0.5 * mm(latent[...], weight[...]).astype(BF).astype(F32)).astype(BF)
    for copy in copies[3:5]:
        copy.wait()
    terms = stack_terms(0.5 * feat_w[...], WEIGHT_ORDER)
    px[grid_rows:, :] = jnp.concatenate([terms, jnp.zeros((128 - terms.shape[0], width), F32)], 0).astype(BF)
    stores = []
    for start in range(0, edges, block):
        part = slice(start, start + block)
        pre = mm(picks[part, :grid_rows], px[:grid_rows, :])
        pre = pre + mm(stack_terms(feat[:, part], FEAT_ORDER).astype(BF), px[grid_rows : grid_rows + 32, :], TN)
        silu, double = halves(pre)
        slope[part, :] = double.astype(BF)
        out = pltpu.make_async_copy(slope.at[part, :], slope_far.at[part, :], slope_sems.at[len(stores)])
        out.start()
        stores.append(out)
        silus[part, :] = silu.astype(BF)
    live = iota((1, edges), 1) < count[0]
    total = mm(hot(iota((slots, edges), 0) == jnp.where(live, receive[...], -1)), silus[...])
    copies[5].wait()
    copies[6].wait()
    owners = slots // cap
    ids = serve[...]
    spread = hot(iota((owners, slots), 0) == lax.div(iota((owners, slots), 1), cap))
    turn = iota((cap, slots), 0) == iota((cap, slots), 1) % cap
    digits = []
    for value in (lax.shift_right_logical(ids, 8), ids & 255):
        wide = mm(value.astype(F32).astype(BF), spread)
        digits.append(jnp.sum(jnp.where(turn, wide, 0.0), 0, keepdims=True))
    id_row = (digits[0] * 256.0 + digits[1]).astype(jnp.int32)
    served = mm(hot(iota((mesh.shape[0], slots), 0) == id_row), mesh[...], TN)
    served_out[...] = served.astype(BF)
    lane = iota((slots, 128), 1)
    back = iota((slots, 128), 0)
    wide = mm(digits[0].astype(BF), hot(lane == back)) + mm(digits[1].astype(BF), hot(lane == back + slots))
    id_rows = jnp.where(iota((8, 128), 0) == 0, wide, 0.0)
    half = total.astype(BF)
    own_out[...] = (total - half.astype(F32)).astype(BF)
    for chip in range(chips):
        write_slots(message, chip, half)
        rows = served[2 * cap * chip : 2 * cap * (chip + 1)]
        tail = [rows[:, base : base + 128] for base in range(0, width, 128)]
        message[chip, slots * (width // 128) :, :] = jnp.concatenate([*tail, id_rows], 0).astype(BF)
    for out in stores:
        out.wait()


def write_slots(message, chip, value):
    slots = value.shape[0]
    for part in range(value.shape[1] // 128):
        message[chip, part * slots : (part + 1) * slots, :] = value[:, part * 128 : (part + 1) * 128]


def slot_rows(ref, slots, width):
    parts = [
        jnp.concatenate([ref[chip, base : base + slots, :] for chip in range(ref.shape[0])], 0)
        for base in range(0, slots * (width // 128), slots)
    ]
    return jnp.concatenate(parts, 1)


def gathered_slots(piece, chips, core, cap, shape, dim):
    slots = 2 * chips * cap
    index = iota(shape, dim)
    chip = lax.div(index, slots)
    slot = index - chip * slots
    band = 2 * chip + jnp.where(piece == 0, core, 1 - core)
    return band, lax.div(slot, cap), lax.rem(slot, cap)


def holder_of(shape, dim, chips, core):
    index = iota(shape, dim)
    return jnp.where(index < chips, 2 * index + core, 2 * (index - chips) + 1 - core)


def slot_matches(first, second, me, cap, mesh_rows, width):
    chips = first.shape[0]
    owners = 2 * chips
    slots = owners * cap
    span = chips * slots
    parts = width // 128
    core = lax.rem(me, 2)
    table = jnp.zeros((owners, 128), F32)
    latent = jnp.zeros((slots, width), F32)
    for piece, ref in enumerate((first, second)):
        ids, rows = [], []
        for chip in range(chips):
            tail = ref[chip, slots * parts :, :].astype(F32)
            ids.append(tail[8 * parts :])
            rows.append(jnp.concatenate([tail[8 * part : 8 * part + 8] for part in range(parts)], 1))
        ids = jnp.concatenate(ids, 0).astype(BF)
        rows = jnp.concatenate(rows, 0).astype(BF)
        shape = (owners, 8 * chips)
        table = table + mm(hot(iota(shape, 1) == (iota(shape, 0) - piece * chips) * 8), ids)
        shape = (slots, 8 * chips)
        window = iota(shape, 0)
        owner = lax.div(window, cap)
        held = lax.rem(owner, 2) == (core if piece == 0 else 1 - core)
        at = lax.div(owner, 2) * 8 + cap * core + lax.rem(window, cap)
        latent = latent + mm(hot(held & (iota(shape, 1) == at)), rows)
    digits = table.astype(BF)
    shape = (slots, owners)
    mine = mm(hot(holder_of(shape, 1, chips, core) == lax.div(iota(shape, 0), cap)), digits)
    lane = iota((slots, 128), 1) - cap * me - lax.rem(iota((slots, 128), 0), cap)
    scaled = jnp.where(lane == 0, 256.0 * mine, jnp.where(lane == slots, mine, 0.0))
    own_key = jnp.sum(scaled, 1, keepdims=True)
    own_key = own_key + (lax.div(iota((slots, 1), 0), cap) * mesh_rows).astype(F32)
    keys, same = [], []
    for piece in range(2):
        band, owner, place = gathered_slots(piece, chips, core, cap, (1, span), 1)
        at = iota((128, span), 0) - cap * band - place
        weight = jnp.where(at == 0, 256.0, jnp.where(at == slots, 1.0, 0.0)).astype(BF)
        value = jnp.where(holder_of((owners, 1), 0, chips, core) == owner, mm(digits, weight), 0.0)
        key = jnp.sum(value, 0, keepdims=True) + (owner * mesh_rows).astype(F32)
        keys.append(key)
        same.append(hot(key == own_key))
    return keys, same, latent


def decoder_picks(
    after, send_any, feat_any, node_any, dec_any, feat_w_any,
    pick, pick_turned, node_w, dec_w, feat_w, send, feat, sems,
):
    sources = (send_any, feat_any, node_any, dec_any, feat_w_any)
    copies = fetch(sources, (send, feat, node_w, dec_w, feat_w), sems)
    slots = after.shape[0]
    grid_rows = send.shape[1]
    copies[0].wait()
    copies[1].wait()
    block = math.gcd(grid_rows, 512)
    for k in range(3):
        for start in range(0, grid_rows, block):
            part = slice(start, start + block)
            to = slice(k * grid_rows + start, k * grid_rows + start + block)
            to_slot = jnp.where(iota((slots, block), 0) == send[k : k + 1, part], 1.0, 0.0)
            rows = jnp.concatenate([to_slot, stack_terms(feat[k, :, part], FEAT_ORDER)], 0)
            pick[:, to] = rows.astype(BF)
            rows = jnp.concatenate([rows, jnp.zeros((128 - rows.shape[0], block), F32)], 0)
            pick_turned[to, :] = rows.T.astype(BF)
    for copy in copies[2:]:
        copy.wait()


def encoder_picks(
    count, latent, receive_any, dec_any, node_any, send_any, feat_any,
    to_edge, latent_turned, dec_turned, node_turned, send, feat, receive, dec_w, node_w, sems,
):
    sources = (receive_any, dec_any, node_any, send_any, feat_any)
    copies = fetch(sources, (receive, dec_w, node_w, send, feat), sems)
    edges = receive.shape[1]
    copies[0].wait()
    block = math.gcd(edges, 512)
    for start in range(0, edges, block):
        part = slice(start, start + block)
        live = iota((1, block), 1) + start < count[0]
        slot = jnp.where(live, receive[:, part], -1)
        to_edge[part, :] = jnp.where(iota((128, block), 0) == slot, 1.0, 0.0).T.astype(BF)
    for copy in copies[1:3]:
        copy.wait()
    dec_turned[...] = dec_w[...].T
    node_turned[...] = node_w[...].T
    latent_turned[...] = latent[...].T
    for copy in copies[3:]:
        copy.wait()


def decoder_kernel(
    cap, mesh_rows, place, first, second, extra, rest, pick, pick_turned, node_w, dec_w, feat_w, cotangent,
    message, keys_out, same_out, slope_out, grad_out, mine_out, rest_out,
):
    slots, width = extra.shape
    keys, same, latent = slot_matches(first, second, place[0], cap, mesh_rows, width)
    agg = jnp.zeros((slots, width), F32)
    for piece, ref in enumerate((first, second)):
        keys_out[piece : piece + 1, :] = keys[piece]
        same_out[piece] = same[piece]
        agg = agg + mm(same[piece], slot_rows(ref, slots, width))
    shape = (same[0].shape[1], slots)
    chosen = hot(iota(shape, 0) == slots * lax.div(place[0], 2) + iota(shape, 1))
    mine = mm(same[0], chosen).astype(BF)
    mine_out[...] = mine
    agg = agg + mm(mine, rest[...])
    silu, double = halves(0.5 * agg)
    slope_out[...] = 0.25 * double
    hmesh = (latent + mm(silu.astype(BF), node_w[...])).astype(BF)
    proj = mm(hmesh, dec_w[...]).astype(BF)
    rows = pick.shape[0]
    blank = jnp.zeros((128 - rows, width), F32)
    terms = jnp.concatenate([stack_terms(0.5 * feat_w[...], WEIGHT_ORDER), blank], 0).astype(BF)
    table = jnp.concatenate([(0.5 * proj.astype(F32)).astype(BF), terms], 0)
    grid_rows = cotangent.shape[0]
    block = math.gcd(grid_rows, 1024)
    total = jnp.zeros((rows, width), F32)
    for start in range(0, grid_rows, block):
        cot = cotangent[start : start + block, :].astype(F32)
        for base in range(start, 3 * grid_rows, grid_rows):
            part = slice(base, base + block)
            double = halves(mm(pick_turned[part, :], table))[1]
            total = total + mm(pick[:, part], (cot * double).astype(BF))
    total = 0.5 * total
    half = total[:slots].astype(BF)
    rest_out[...] = (total[:slots] - half.astype(F32)).astype(BF)
    grad_out[...] = feature_grad(total[slots:], feat_w.shape[0])
    chips = message.shape[0]
    share = width // chips
    step = slots * share // 128
    for chip in range(chips):
        write_slots(message, chip, half)
        columns = extra[:, chip * share : (chip + 1) * share].astype(F32)
        columns = jnp.concatenate([columns[base : base + step] for base in range(0, slots, step)], 1)
        message[chip, slots * (width // 128) :, :] = columns.astype(BF)


def backward_kernel(
    place, first, second, same, mine, rest, agg_slope, dec_grad, to_edge, latent_turned, dec_turned, node_turned,
    send, feat, slope, dpx_far, dpx, give, sums_out, grads, dpx_sems,
):
    slots = same.shape[1]
    edges, width = grads.shape
    grid_rows = dpx.shape[0]
    feats = feat.shape[0]
    core = lax.rem(place[0], 2)
    dproj = mm(same[0], slot_rows(first, slots, width)) + mm(same[1], slot_rows(second, slots, width))
    dproj = dproj + mm(mine[...], rest[...])
    high = dproj.astype(BF)
    low = (dproj - high.astype(F32)).astype(BF)
    dhmesh = mm(jnp.concatenate([high, low], 0), dec_turned[...])
    mesh_grad = (dhmesh[:slots] + dhmesh[slots:]).astype(BF)
    dagg = mm(mesh_grad, node_turned[...]) * agg_slope[...]
    dagg = jnp.concatenate([dagg, jnp.zeros((128 - slots, width), F32)], 0).astype(BF)
    block = math.gcd(edges, 1024)
    for start in range(0, edges, block):
        cut = slice(start, start + block)
        grads[cut, :] = (mm(to_edge[cut, :], dagg) * slope[cut, :].astype(F32)).astype(BF)
    step = math.gcd(grid_rows, 512)
    stores = []
    terms = stack_terms(feat[...], FEAT_ORDER).astype(BF)
    for start in range(0, grid_rows, step):
        cut = slice(start, start + step)
        left = hot(iota((step, edges), 0) + start == send[...])
        if start == 0:
            left = jnp.concatenate([left, terms], 0)
        product = mm(left, grads[...])
        if start == 0:
            enc_grad = feature_grad(product[step:], feats)
        dpx[cut, :] = product[:step].astype(BF)
        out = pltpu.make_async_copy(dpx.at[cut, :], dpx_far.at[cut, :], dpx_sems.at[len(stores)])
        out.start()
        stores.append(out)
    sums = jnp.where(iota(enc_grad.shape, 0) < feats, enc_grad, pltpu.roll(dec_grad[...], feats, 0))
    sums_out[...] = sums
    write_shares(give, 1 - core, latent_turned, dpx, sums)
    for out in stores:
        out.wait()


def write_shares(out, side, latent_turned, dpx, sums):
    chips = out.shape[0]
    width = dpx.shape[1]
    rows = width // (2 * chips)
    left = [latent_turned[pl.ds((2 * chip + side) * rows, rows), :] for chip in range(chips)]
    product = mm(jnp.concatenate(left, 0), dpx[...])
    blank = jnp.zeros((8, 128 - rows), F32)
    for chip in range(chips):
        block = product[chip * rows : (chip + 1) * rows]
        pair = [sums[:, base : base + rows] for base in (2 * chip * rows, (2 * chip + 1) * rows)]
        small = jnp.concatenate([jnp.where(side == 0, pair[0], pair[1]), blank], 1)
        pieces = [block[:, base : base + 128] for base in range(0, width, 128)]
        out[chip] = jnp.concatenate([*pieces, small], 0).astype(out.dtype)


def keep_kernel(place, latent_turned, dpx, sums, keep):
    write_shares(keep, lax.rem(place[0], 2), latent_turned, dpx, sums[...])


def pair_kernel(keep, given, out):
    out[...] = (keep[...] + given[...].astype(F32)).astype(BF)


def final_kernel(feats, arrived, out, enc_out, dec_out):
    total = jnp.sum(arrived[...].astype(F32), 0)
    rows, width = out.shape
    for part in range(width // 128):
        out[:, part * 128 : (part + 1) * 128] = total[part * rows : (part + 1) * rows]
    base = rows * (width // 128)
    enc_out[...] = total[base : base + feats, :rows]
    dec_out[...] = total[base + feats : base + 2 * feats, :rows]


def beside_kernel(
    cap, mesh_rows, place, keys, node_any, first_any, second_any, first_back_any, second_back_any, dec_any, dpx_any,
    weight_any, cot_any, mesh_out, dec_out, node_out, grid_out,
    node_w, first, second, first_back, second_back, dec_w, dpx, weight, cotangent, sems,
):
    sources = (
        first_any, second_any, node_any, first_back_any, second_back_any, dec_any, dpx_any, weight_any, cot_any,
    )
    targets = (first, second, node_w, first_back, second_back, dec_w, dpx, weight, cotangent)
    copies = fetch(sources, targets, sems)
    width = node_w.shape[0]
    chips = first.shape[0]
    owners = 2 * chips
    slots = owners * cap
    span = chips * slots
    me = place[0]
    core = lax.rem(me, 2)
    block = width // owners
    key = jnp.concatenate([keys[0:1, :], keys[1:2, :]], 1)
    down = jnp.broadcast_to(key, (128, 2 * span)).T
    same = jnp.concatenate([hot(down == key[:, base : base + 128]) for base in range(0, 2 * span, 128)], 1)
    for copy in copies[:3]:
        copy.wait()
    forward = jnp.concatenate([slot_rows(ref, slots, width) for ref in (first, second)], 0)
    act = halves(0.5 * mm(same, forward))[0].astype(BF)
    shape = (width, 128)
    mine = hot((iota(shape, 0) == block * me + iota(shape, 1)) & (iota(shape, 1) < block))
    node_cols = mm(node_w[...], mine).astype(BF)
    both = mm(act, jnp.concatenate([node_cols, mine], 1))
    step = slots * 2 * block // 128
    pieces = [gathered_slots(piece, chips, core, cap, (span, 1), 0) for piece in range(2)]
    band, owner, turn = [jnp.concatenate([a, b], 0) for a, b in zip(*pieces)]
    source = jnp.where(lax.rem(owner, 2) == core, 0, chips) + lax.div(owner, 2)
    number = cap * band + turn
    at = lax.div(number, step) * (owners * step) + source * step + lax.rem(number, step)
    for copy in copies[3:]:
        copy.wait()
    back = jnp.concatenate([slot_rows(ref, slots, width) for ref in (first_back, second_back)], 0)
    tail = slots * (width // 128)
    columns = [ref[chip, tail:, :] for ref in (first_back, second_back) for chip in range(chips)]
    columns = jnp.concatenate(columns, 0)
    shape = (128, 128)
    folded = []
    for base in range(0, 128, 2 * block):
        fold = hot((iota(shape, 0) == base + block * core + iota(shape, 1)) & (iota(shape, 1) < block))
        folded.append(mm(columns, fold).astype(BF))
    latent = mm(hot(iota((2 * span, 2 * span), 1) == at), jnp.concatenate(folded, 0))
    hmesh = (both[:, :128] + latent).astype(BF)
    left = jnp.concatenate([hmesh, both[:, 128:].astype(BF)], 1)
    sums = mm(left, back, TN)
    dec_out[...] = sums[:block]
    own = (me * mesh_rows + iota((mesh_out.shape[0], 2 * span), 0)).astype(F32)
    dproj = jnp.concatenate([mm(hot(own == key), back), sums[128 : 128 + block]], 0)
    high = dproj.astype(BF)
    low = (dproj - high.astype(F32)).astype(BF)
    turned = mm(high, dec_w[...], NT) + mm(low, dec_w[...], NT)
    mesh = mesh_out.shape[0]
    mesh_out[...] = turned[:mesh].astype(BF)
    node_out[...] = turned[mesh:]
    grid_out[...] = (cotangent[...].astype(F32) + mm(dpx[...], weight[...], NT)).astype(BF)


SMEM = pl.BlockSpec(memory_space=pltpu.SMEM)
VMEM = pl.BlockSpec(memory_space=pltpu.VMEM)
FAR = pl.BlockSpec(memory_space=pltpu.HBM)


def kernel_call(body, name, scalars, near, far, outs, scratch, flops, limit, out_specs=None, pin=False, last=(), kept=0):
    shapes = [jax.ShapeDtypeStruct(shape, dtype) for shape, dtype in outs]
    out_specs = out_specs or [VMEM] * len(shapes)
    pinned = [pltpu.HBM(s.shape, s.dtype) if spec is FAR else s for s, spec in zip(shapes, out_specs)]
    if pin:
        far = [pltpu.with_memory_space_constraint(a, pltpu.HBM) for a in far]
    moved = sum(a.size * a.dtype.itemsize for a in (*near, *far)) + sum(s.size * s.dtype.itemsize for s in shapes)
    buffers = [pltpu.VMEM(a.shape, a.dtype) for a in far[: len(far) - kept]]
    if far:
        buffers.append(pltpu.SemaphoreType.DMA((len(far),)))
    return pl.pallas_call(
        body,
        name=name,
        out_shape=pinned,
        in_specs=[SMEM] * len(scalars) + [VMEM] * len(near) + [FAR] * len(far),
        out_specs=out_specs,
        scratch_shapes=[*scratch, *buffers, *last],
        compiler_params=pltpu.CompilerParams(vmem_limit_bytes=limit * MIB),
        cost_estimate=pl.CostEstimate(flops=flops, bytes_accessed=moved, transcendentals=0),
    )(*scalars, *near, *far)


def gather_plan(
    grid_latent,
    mesh_latent,
    grid_cotangent,
    enc_sender,
    enc_receiver,
    enc_feat,
    enc_count,
    dec_sender,
    dec_feat,
    serve_rows,
    enc_proj,
    node_proj,
    dec_proj,
    enc_feat_w,
    dec_feat_w,
):
    owners = lax.axis_size("lat")
    chips = owners // 2
    cap = serve_rows.shape[2]
    slots = owners * cap
    mesh_rows, width = mesh_latent.shape
    grid_rows = grid_latent.shape[0]
    edges = enc_sender.shape[0]
    feats = enc_feat.shape[0]
    block = width // owners
    span = chips * slots
    parts = width // 128
    share = width // chips
    groups = [[core + 2 * chip for chip in range(chips)] for core in range(2)]
    swap = [(index, index ^ 1) for index in range(owners)]
    place = lax.axis_index("lat").astype(jnp.int32).reshape(1)

    def gather(message, *later):
        first = lax.all_to_all(message, "lat", 0, 0, tiled=True, axis_index_groups=groups)
        first, *later = lax.optimization_barrier((first, *later))
        return first, lax.ppermute(first, "lat", swap), *later

    send = enc_sender.reshape(1, edges)
    receive = enc_receiver.reshape(1, edges)
    message, slope, served, rest = kernel_call(
        lambda *refs: encoder_kernel(cap, *refs),
        "encoder",
        [enc_count],
        [],
        [grid_latent, enc_proj, mesh_latent, send, receive, enc_feat, enc_feat_w.T, serve_rows[0].T],
        [
            ((chips, parts * (slots + 8) + 8, 128), BF),
            ((edges, width), BF),
            ((slots, width), BF),
            ((slots, width), BF),
        ],
        [
            pltpu.VMEM((grid_rows + 128, width), BF),
            pltpu.VMEM((edges, grid_rows), BF),
            pltpu.VMEM((edges, width), BF),
            pltpu.VMEM((edges, width), BF),
            pltpu.SemaphoreType.DMA((edges // math.gcd(edges, 512),)),
        ],
        2 * edges * grid_rows * width,
        28,
        [VMEM, FAR, VMEM, VMEM],
        pin=True,
        last=[pltpu.SemaphoreType.DMA((grid_rows // math.gcd(grid_rows, 256),))],
    )
    term_rows = stack_rows(feats)
    first, second, served = gather(message, served)
    pick, pick_turned, near_node, near_dec, near_feat_w = kernel_call(
        decoder_picks,
        "decoder_picks",
        [],
        [served],
        [dec_sender, dec_feat, node_proj, dec_proj, dec_feat_w.T],
        [
            ((slots + term_rows, 3 * grid_rows), BF),
            ((3 * grid_rows, 128), BF),
            ((width, width), BF),
            ((width, width), BF),
            ((feats, width), F32),
        ],
        [],
        2000 * MIB,
        16,
        pin=True,
        kept=3,
    )
    message, keys, same, agg_slope, dec_grad, mine, rest = kernel_call(
        lambda *refs: decoder_kernel(cap, mesh_rows, *refs),
        "decoder",
        [place],
        [first, second, served, rest, pick, pick_turned, near_node, near_dec, near_feat_w, grid_cotangent],
        [],
        [
            ((chips, parts * slots + slots * share // 128, 128), BF),
            ((2, span), F32),
            ((2, slots, span), BF),
            ((slots, width), F32),
            ((2 * feats, width), F32),
            ((slots, slots), BF),
            ((slots, width), BF),
        ],
        [],
        24 * grid_rows * 128 * width,
        20,
    )
    first_back, second_back, pick_count = gather(message, enc_count)
    to_edge, latent_turned, dec_turned, node_turned, near_send, near_feat = kernel_call(
        encoder_picks,
        "encoder_picks",
        [pick_count],
        [grid_latent],
        [receive, dec_proj, node_proj, send, enc_feat],
        [
            ((edges, 128), BF),
            ((width, grid_rows), BF),
            ((width, width), BF),
            ((width, width), BF),
            ((1, edges), jnp.int32),
            ((feats, edges), F32),
        ],
        [],
        2000 * MIB,
        16,
        pin=True,
        kept=2,
    )
    dpx_far, dpx, give, sums = kernel_call(
        backward_kernel,
        "backward",
        [place],
        [
            first_back,
            second_back,
            same,
            mine,
            rest,
            agg_slope,
            dec_grad,
            to_edge,
            latent_turned,
            dec_turned,
            node_turned,
            near_send,
            near_feat,
            slope,
        ],
        [],
        [
            ((grid_rows, width), BF),
            ((grid_rows, width), BF),
            ((chips, parts * block + 8, 128), BF),
            ((2 * feats, width), F32),
        ],
        [
            pltpu.VMEM((edges, width), BF),
            pltpu.SemaphoreType.DMA((grid_rows // math.gcd(grid_rows, 256),)),
        ],
        2 * edges * grid_rows * width,
        24,
        [FAR, VMEM, VMEM, VMEM],
    )
    (keep,) = kernel_call(
        keep_kernel,
        "keep",
        [place],
        [latent_turned, dpx, sums],
        [],
        [((chips, parts * block + 8, 128), F32)],
        [],
        grid_rows * width * width,
        16,
    )
    given = lax.ppermute(give, "lat", swap)
    (pair,) = kernel_call(pair_kernel, "pair", [], [keep, given], [], [(give.shape, BF)], [], keep.size, 8)
    pair, keys, dpx_far = lax.optimization_barrier((pair, keys, dpx_far))
    arrived = lax.all_to_all(pair, "lat", 0, 0, tiled=True, axis_index_groups=groups)
    mesh_grad, dec_proj_grad, node_proj_grad, grid_grad = kernel_call(
        lambda *refs: beside_kernel(cap, mesh_rows, *refs),
        "beside",
        [place],
        [keys],
        [
            node_proj,
            first,
            second,
            first_back,
            second_back,
            dec_proj,
            dpx_far,
            enc_proj,
            grid_cotangent,
        ],
        [
            ((mesh_rows, width), BF),
            ((block, width), F32),
            ((block, width), F32),
            ((grid_rows, width), BF),
        ],
        [],
        2 * (2 * span) * (2 * span) * width,
        30,
        pin=True,
    )
    enc_proj_grad, enc_feat_grad, dec_feat_grad = kernel_call(
        lambda *refs: final_kernel(feats, *refs),
        "final",
        [],
        [arrived],
        [],
        [((block, width), F32), ((feats, block), F32), ((feats, block), F32)],
        [],
        arrived.size,
        8,
    )
    return (
        grid_grad,
        mesh_grad,
        enc_proj_grad,
        node_proj_grad,
        dec_proj_grad,
        enc_feat_grad.T,
        dec_feat_grad.T,
    )


def gather_fits(args):
    mesh_latent, serve_rows = args[1], args[9]
    owners, cap = serve_rows.shape[1], serve_rows.shape[2]
    width = mesh_latent.shape[1]
    chips = owners // 2
    return (
        owners % 2 == 0
        and 2 * cap == 8
        and owners * cap <= 64
        and width % 128 == 0
        and width % (8 * owners) == 0
        and 128 % (width // chips) == 0
        and owners * cap * (width // chips) % 2048 == 0
        and mesh_latent.shape[0] <= 65536
        and mesh_latent.shape[0] * owners < 1 << 24
        and args[0].shape[0] % 128 == 0
        and args[3].shape[0] % 128 == 0
        and args[5].shape[0] == 4
    )


def per_device(*args):
    return gather_plan(*args) if gather_fits(args) else owner_plan(*args)


def solution(mesh):
    placed = (
        P(("member", "lat"), None),
        P(("member", "lat"), None),
        P(("member", "lat"), None),
        P(("member", "lat")),
        P(("member", "lat")),
        P(None, ("member", "lat")),
        P(("member", "lat")),
        P(None, ("member", "lat")),
        P(None, None, ("member", "lat")),
        P(("member", "lat"), None, None),
        P(),
        P(),
        P(),
        P(),
        P(),
    )
    return jax.shard_map(
        per_device,
        mesh=mesh,
        in_specs=placed,
        out_specs=(
            P(("member", "lat"), None),
            P(("member", "lat"), None),
            P(("member", "lat"), None),
            P(("member", "lat"), None),
            P(("member", "lat"), None),
            P(("member", "lat"), None),
            P(("member", "lat"), None),
        ),
        check_vma=False,
    )
```

```python
import math

import jax
import jax.numpy as jnp
from jax import lax
from jax.experimental import pallas as pl
from jax.experimental.pallas import tpu as pltpu
from jax.sharding import PartitionSpec as P

BF = jnp.bfloat16
F32 = jnp.float32
HI = lax.Precision.HIGHEST
MIB = 1 << 20
NN = (((1,), (0,)), ((), ()))
NT = (((1,), (1,)), ((), ()))
TN = (((0,), (0,)), ((), ()))


def silu_grad(value):
    sig = jax.nn.sigmoid(value)
    return sig * (1.0 + value * (1.0 - sig))


def owner_plan(
    grid_latent,
    mesh_latent,
    grid_cotangent,
    enc_sender,
    enc_receiver,
    enc_feat,
    enc_count,
    dec_sender,
    dec_feat,
    serve_rows,
    enc_proj,
    node_proj,
    dec_proj,
    enc_feat_w,
    dec_feat_w,
):
    highest = lax.Precision.HIGHEST
    owners_count = lax.axis_size("lat")
    serve_flat = serve_rows.reshape(-1)
    slot_total = serve_flat.shape[0]
    per_owner = slot_total // owners_count
    mesh_rows = mesh_latent.shape[0]
    grid_rows = grid_latent.shape[0]
    width = grid_latent.shape[1]
    edge_slots = enc_sender.shape[0]
    edge_block = math.gcd(edge_slots, 512)
    grid_block = math.gcd(grid_rows, 512)
    live_count = enc_count[0]
    slot_ids = lax.iota(jnp.int32, slot_total)[:, None]
    row_ids = lax.iota(jnp.int32, grid_rows)[:, None]

    def to_window(rows):
        outgoing = jnp.take(rows, serve_flat, axis=0).reshape(owners_count, per_owner, width)
        arrived = lax.all_to_all(outgoing, "lat", split_axis=0, concat_axis=0, tiled=True)
        return arrived.reshape(slot_total, width)

    def to_owners(partial_value):
        arrived = lax.all_to_all(
            partial_value.reshape(owners_count, per_owner, width),
            "lat",
            split_axis=0,
            concat_axis=0,
            tiled=True,
        )
        return jax.ops.segment_sum(
            arrived.reshape(slot_total, width), serve_flat, num_segments=mesh_rows
        )

    px = jnp.dot(grid_latent, enc_proj, preferred_element_type=jnp.float32).astype(jnp.bfloat16)

    def enc_block(start):
        senders = lax.dynamic_slice_in_dim(enc_sender, start, edge_block)
        receivers = lax.dynamic_slice_in_dim(enc_receiver, start, edge_block)
        feats = lax.dynamic_slice_in_dim(enc_feat, start, edge_block, 1)
        pre = jnp.take(px, senders, axis=0).astype(jnp.float32) + jnp.einsum(
            "fb,lf->bl", feats, enc_feat_w, precision=highest
        )
        live = (lax.iota(jnp.int32, edge_block) + start < live_count)[:, None]
        onehot = (receivers[None, :] == slot_ids).astype(jnp.bfloat16)
        return (pre, live, onehot, senders, feats)

    block_steps = edge_slots // edge_block

    def enc_forward(index, partial_value):
        pre, live, onehot, senders, feats = enc_block(index * edge_block)
        message = jnp.where(live, jax.nn.silu(pre), 0.0).astype(jnp.bfloat16)
        return partial_value + jnp.dot(onehot, message, preferred_element_type=jnp.float32)

    enc_partial = lax.fori_loop(
        0, block_steps, enc_forward, jnp.zeros((slot_total, width), jnp.float32)
    )
    agg = to_owners(enc_partial)
    act = jax.nn.silu(agg).astype(jnp.bfloat16)
    hmesh = (
        mesh_latent.astype(jnp.float32)
        + jnp.dot(act, node_proj, preferred_element_type=jnp.float32)
    ).astype(jnp.bfloat16)
    proj_window = to_window(
        jnp.dot(hmesh, dec_proj, preferred_element_type=jnp.float32).astype(jnp.bfloat16)
    )

    def dec_backward(index, carry):
        dproj, dfw = carry
        start = index * grid_block
        cot = lax.dynamic_slice_in_dim(grid_cotangent, start, grid_block).astype(jnp.float32)
        for k in range(3):
            senders = lax.dynamic_slice_in_dim(dec_sender[k], start, grid_block)
            feats = lax.dynamic_slice_in_dim(dec_feat[k], start, grid_block, 1)
            pre = jnp.take(proj_window, senders, axis=0).astype(jnp.float32) + jnp.einsum(
                "fg,lf->gl", feats, dec_feat_w, precision=highest
            )
            grad_half = (cot * silu_grad(pre)).astype(jnp.bfloat16)
            slot_hot = (senders[None, :] == slot_ids).astype(jnp.bfloat16)
            dproj = dproj + jnp.dot(slot_hot, grad_half, preferred_element_type=jnp.float32)
            dfw = dfw + jnp.einsum(
                "gl,fg->lf", grad_half.astype(jnp.float32), feats, precision=highest
            )
        return (dproj, dfw)

    start_carry = (
        jnp.zeros((slot_total, width), jnp.float32),
        jnp.zeros((width, dec_feat_w.shape[1]), jnp.float32),
    )
    dproj_window, dec_fw_part = lax.fori_loop(0, grid_rows // grid_block, dec_backward, start_carry)
    dec_weight = dec_proj.astype(jnp.float32)
    dproj = to_owners(dproj_window)
    dhmesh = jnp.dot(dproj, dec_weight.T, precision=highest)
    dec_proj_part = jnp.dot(hmesh.astype(jnp.float32).T, dproj, precision=highest)
    mesh_grad = dhmesh.astype(jnp.bfloat16)
    node_proj_part = jnp.dot(act.T, mesh_grad, preferred_element_type=jnp.float32)
    dagg = (
        jnp.dot(mesh_grad, node_proj.T, preferred_element_type=jnp.float32) * silu_grad(agg)
    ).astype(jnp.bfloat16)
    dagg_window = to_window(dagg)

    def enc_backward(index, carry):
        dpx, dew = carry
        pre, live, onehot, senders, feats = enc_block(index * edge_block)
        upstream = jnp.einsum("wb,wl->bl", onehot, dagg_window, preferred_element_type=jnp.float32)
        grad_half = jnp.where(live, upstream * silu_grad(pre), 0.0).astype(jnp.bfloat16)
        row_hot = (senders[None, :] == row_ids).astype(jnp.bfloat16)
        dpx = dpx + jnp.dot(row_hot, grad_half, preferred_element_type=jnp.float32)
        dew = dew + jnp.einsum("bl,fb->lf", grad_half.astype(jnp.float32), feats, precision=highest)
        return (dpx, dew)

    start_back = (
        jnp.zeros((grid_rows, width), jnp.float32),
        jnp.zeros((width, enc_feat_w.shape[1]), jnp.float32),
    )
    dpx_sum, enc_fw_part = lax.fori_loop(0, block_steps, enc_backward, start_back)
    dpx = dpx_sum.astype(jnp.bfloat16)
    enc_proj_part = jnp.dot(grid_latent.T, dpx, preferred_element_type=jnp.float32)
    grid_grad = (
        grid_cotangent.astype(jnp.float32)
        + jnp.dot(dpx, enc_proj.T, preferred_element_type=jnp.float32)
    ).astype(jnp.bfloat16)
    enc_proj_grad, node_proj_grad, dec_proj_grad, enc_feat_w_grad, dec_feat_w_grad = (
        lax.psum_scatter(enc_proj_part, "lat", scatter_dimension=0, tiled=True),
        lax.psum_scatter(node_proj_part, "lat", scatter_dimension=0, tiled=True),
        lax.psum_scatter(dec_proj_part, "lat", scatter_dimension=0, tiled=True),
        lax.psum_scatter(enc_fw_part, "lat", scatter_dimension=0, tiled=True),
        lax.psum_scatter(dec_fw_part, "lat", scatter_dimension=0, tiled=True),
    )
    return (
        grid_grad,
        mesh_grad,
        enc_proj_grad,
        node_proj_grad,
        dec_proj_grad,
        enc_feat_w_grad,
        dec_feat_w_grad,
    )


def mm(a, b, dims=NN, precision=None):
    return lax.dot_general(a, b, dims, precision=precision, preferred_element_type=F32)


def iota(shape, dim):
    return lax.broadcasted_iota(jnp.int32, shape, dim)


def halves(value):
    turn = jnp.tanh(value)
    up = 1.0 + turn
    silu = value * up
    return silu, up + silu * (1.0 - turn)


def hot(mask):
    return jnp.where(mask, 1.0, 0.0).astype(BF)


def split3(value):
    high = value.astype(BF).astype(F32)
    rest = value - high
    middle = rest.astype(BF).astype(F32)
    return high, middle, rest - middle


def stack_rows(feats):
    return -(-6 * feats // 16) * 16


def stack_terms(value, order):
    parts = split3(value)
    rows = len(order) * value.shape[0]
    blank = jnp.zeros((stack_rows(value.shape[0]) - rows, value.shape[1]), F32)
    return jnp.concatenate([*(parts[which] for which in order), blank], 0)


FEAT_ORDER = (0, 0, 1, 1, 2, 0)
WEIGHT_ORDER = (0, 1, 0, 1, 0, 2)


def fetch(sources, targets, sems):
    copies = [pltpu.make_async_copy(src, dst, sems.at[i]) for i, (src, dst) in enumerate(zip(sources, targets))]
    for copy in copies:
        copy.start()
    return copies


def feature_grad(terms, feats):
    total = terms[: 2 * feats] + terms[2 * feats : 4 * feats] + terms[4 * feats : 6 * feats]
    return jnp.where(iota(total.shape, 0) < feats, total, 0.0)


def encoder_kernel(
    cap, count, latent_any, weight_any, mesh_any, send_any, receive_any, feat_any, feat_w_any, serve_any,
    message, slope_far, served_out, own_out, px, picks, silus, slope, slope_sems,
    latent, weight, mesh, send, receive, feat, feat_w, serve, sems, latent_sems,
):
    sources = (send_any, feat_any, weight_any, feat_w_any, receive_any, mesh_any, serve_any)
    targets = (send, feat, weight, feat_w, receive, mesh, serve)
    copies = fetch(sources[:3], targets[:3], sems)
    edges = send.shape[1]
    grid_rows, width = latent.shape
    chips = message.shape[0]
    slots = served_out.shape[0]
    step = math.gcd(grid_rows, 256)
    cuts = [slice(start, start + step) for start in range(0, grid_rows, step)]
    chunks = fetch([latent_any.at[cut, :] for cut in cuts], [latent.at[cut, :] for cut in cuts], latent_sems)
    copies += fetch(sources[3:], targets[3:], sems.at[pl.ds(3, 4)])
    block = math.gcd(edges, 512)
    copies[0].wait()
    copies[1].wait()
    for start in range(0, edges, block):
        part = slice(start, start + block)
        ids = jnp.broadcast_to(send[:, part].astype(F32), (128, block)).T
        for base in range(0, grid_rows, 128):
            lane = (iota((block, 128), 1) + base).astype(F32)
            picks[part, base : base + 128] = hot(ids == lane)
    copies[2].wait()
    for cut, chunk in zip(cuts, chunks):
        chunk.wait()
    px[:grid_rows, :] = (0.5 * mm(latent[...], weight[...]).astype(BF).astype(F32)).astype(BF)
    for copy in copies[3:5]:
        copy.wait()
    terms = stack_terms(0.5 * feat_w[...], WEIGHT_ORDER)
    px[grid_rows:, :] = jnp.concatenate([terms, jnp.zeros((128 - terms.shape[0], width), F32)], 0).astype(BF)
    stores = []
    for start in range(0, edges, block):
        part = slice(start, start + block)
        pre = mm(picks[part, :grid_rows], px[:grid_rows, :])
        pre = pre + mm(stack_terms(feat[:, part], FEAT_ORDER).astype(BF), px[grid_rows : grid_rows + 32, :], TN)
        silu, double = halves(pre)
        slope[part, :] = double.astype(BF)
        out = pltpu.make_async_copy(slope.at[part, :], slope_far.at[part, :], slope_sems.at[len(stores)])
        out.start()
        stores.append(out)
        silus[part, :] = silu.astype(BF)
    live = iota((1, edges), 1) < count[0]
    total = mm(hot(iota((slots, edges), 0) == jnp.where(live, receive[...], -1)), silus[...])
    copies[5].wait()
    copies[6].wait()
    owners = slots // cap
    ids = serve[...]
    spread = hot(iota((owners, slots), 0) == lax.div(iota((owners, slots), 1), cap))
    turn = iota((cap, slots), 0) == iota((cap, slots), 1) % cap
    digits = []
    for value in (lax.shift_right_logical(ids, 8), ids & 255):
        wide = mm(value.astype(F32).astype(BF), spread)
        digits.append(jnp.sum(jnp.where(turn, wide, 0.0), 0, keepdims=True))
    id_row = (digits[0] * 256.0 + digits[1]).astype(jnp.int32)
    served = mm(hot(iota((mesh.shape[0], slots), 0) == id_row), mesh[...], TN)
    served_out[...] = served.astype(BF)
    code = scale_codes(jnp.max(jnp.abs(total), 1, keepdims=True))
    fixed = to_fixed(total * scale_values(code, -1))
    own_out[...] = (total - fixed.astype(F32) * scale_values(code, 1)).astype(BF)
    half = fixed.astype(jnp.int16)
    latents = to_fixed(served * (1.0 / LATENT_STEP))
    code_row = jnp.broadcast_to(code.astype(F32), (slots, 128)).T[:1, :]
    lane = iota((slots, 128), 1)
    back = iota((slots, 128), 0)
    wide = 256.0 * mm(digits[0].astype(BF), hot(lane == back)) + mm(digits[1].astype(BF), hot(lane == back))
    wide = wide + mm(code_row.astype(BF), hot(lane == back + slots))
    id_rows = jnp.where(iota((8, 128), 0) == 0, wide, 0.0).astype(jnp.int32)
    for chip in range(chips):
        write_slots(message, chip, half)
        rows = latents[2 * cap * chip : 2 * cap * (chip + 1)]
        tail = [rows[:, base : base + 128] for base in range(0, width, 128)]
        message[chip, slots * (width // 128) :, :] = jnp.concatenate([*tail, id_rows], 0).astype(jnp.int16)
    for out in stores:
        out.wait()


POWERS = range(-40, 24)
LATENT_STEP = 6.0 / 32000.0


def scale_codes(peak):
    code = jnp.zeros(peak.shape, jnp.int32)
    for power in POWERS[:-1]:
        code = code + jnp.where(peak > 32000.0 * 2.0**power, 1, 0)
    return code


def scale_values(code, sign):
    value = jnp.zeros(code.shape, F32)
    for index, power in enumerate(POWERS):
        value = jnp.where(code == index, 2.0 ** (sign * power), value)
    return value


def to_fixed(value):
    return jnp.floor(value + 0.5).astype(jnp.int32)


def fixed_rows(ref, slots, width):
    parts = [
        jnp.concatenate([ref[chip, base : base + slots, :].astype(jnp.int32) for chip in range(ref.shape[0])], 0)
        for base in range(0, slots * (width // 128), slots)
    ]
    value = jnp.concatenate(parts, 1)
    return lax.shift_right_arithmetic(value, 8).astype(F32).astype(BF), (value & 255).astype(F32).astype(BF)


def write_slots(message, chip, value):
    slots = value.shape[0]
    for part in range(value.shape[1] // 128):
        message[chip, part * slots : (part + 1) * slots, :] = value[:, part * 128 : (part + 1) * 128]


def slot_rows(ref, slots, width):
    parts = [
        jnp.concatenate([ref[chip, base : base + slots, :] for chip in range(ref.shape[0])], 0)
        for base in range(0, slots * (width // 128), slots)
    ]
    return jnp.concatenate(parts, 1)


def gathered_slots(piece, chips, core, cap, shape, dim):
    slots = 2 * chips * cap
    index = iota(shape, dim)
    chip = lax.div(index, slots)
    slot = index - chip * slots
    band = 2 * chip + jnp.where(piece == 0, core, 1 - core)
    return band, lax.div(slot, cap), lax.rem(slot, cap)


def holder_of(shape, dim, chips, core):
    index = iota(shape, dim)
    return jnp.where(index < chips, 2 * index + core, 2 * (index - chips) + 1 - core)


def slot_matches(first, second, me, cap, mesh_rows, width):
    chips = first.shape[0]
    owners = 2 * chips
    slots = owners * cap
    span = chips * slots
    parts = width // 128
    core = lax.rem(me, 2)
    tables = [jnp.zeros((owners, 128), F32)] * 2
    latent = jnp.zeros((slots, width), F32)
    for piece, ref in enumerate((first, second)):
        ids, rows = [], []
        for chip in range(chips):
            tail = ref[chip, slots * parts :, :].astype(jnp.int32)
            ids.append(tail[8 * parts :])
            rows.append(jnp.concatenate([tail[8 * part : 8 * part + 8] for part in range(parts)], 1))
        ids = jnp.concatenate(ids, 0)
        rows = jnp.concatenate(rows, 0)
        shape = (owners, 8 * chips)
        take = hot(iota(shape, 1) == (iota(shape, 0) - piece * chips) * 8)
        for index, digit in enumerate((lax.shift_right_arithmetic(ids, 8), ids & 255)):
            tables[index] = tables[index] + mm(take, digit.astype(F32).astype(BF))
        shape = (slots, 8 * chips)
        window = iota(shape, 0)
        owner = lax.div(window, cap)
        held = lax.rem(owner, 2) == (core if piece == 0 else 1 - core)
        at = lax.div(owner, 2) * 8 + cap * core + lax.rem(window, cap)
        pick = hot(held & (iota(shape, 1) == at))
        high = lax.shift_right_arithmetic(rows, 8).astype(F32).astype(BF)
        latent = latent + 256.0 * mm(pick, high) + mm(pick, (rows & 255).astype(F32).astype(BF))
    latent = (latent * LATENT_STEP).astype(BF).astype(F32)
    digits = jnp.concatenate(tables, 0).astype(BF)
    shape = (slots, 2 * owners)
    half = lax.rem(iota(shape, 1), owners)
    holder = jnp.where(half < chips, 2 * half + core, 2 * (half - chips) + 1 - core)
    wanted = jnp.where(holder == lax.div(iota(shape, 0), cap), 1.0, 0.0)
    mine = mm((wanted * jnp.where(iota(shape, 1) < owners, 256.0, 1.0)).astype(BF), digits)
    lane = iota((slots, 128), 1) - cap * me - lax.rem(iota((slots, 128), 0), cap)
    own_key = jnp.sum(jnp.where(lane == 0, mine, 0.0), 1, keepdims=True)
    own_key = own_key + (lax.div(iota((slots, 1), 0), cap) * mesh_rows).astype(F32)
    keys, same, scales = [], [], []
    for piece in range(2):
        band, owner, place = gathered_slots(piece, chips, core, cap, (1, span), 1)
        spread = mm(digits, hot(iota((128, span), 0) == cap * band + place))
        value = 256.0 * spread[:owners] + spread[owners:]
        value = jnp.where(holder_of((owners, 1), 0, chips, core) == owner, value, 0.0)
        key = jnp.sum(value, 0, keepdims=True) + (owner * mesh_rows).astype(F32)
        keys.append(key)
        same.append(hot(key == own_key))
        index = iota((1, span), 1)
        spread = mm(digits[owners:], hot(iota((128, span), 0) == slots + lax.rem(index, slots)))
        source = iota((owners, 1), 0) - piece * chips == lax.div(index, slots)
        code = jnp.sum(jnp.where(source, spread, 0.0), 0, keepdims=True)
        scales.append(scale_values(code.astype(jnp.int32), 1))
    return keys, same, scales, latent


def decoder_picks(
    after, send_any, feat_any, node_any, dec_any, feat_w_any,
    pick, pick_turned, node_w, dec_w, feat_w, send, feat, sems,
):
    sources = (send_any, feat_any, node_any, dec_any, feat_w_any)
    copies = fetch(sources, (send, feat, node_w, dec_w, feat_w), sems)
    slots = after.shape[0]
    grid_rows = send.shape[1]
    copies[0].wait()
    copies[1].wait()
    block = math.gcd(grid_rows, 512)
    for k in range(3):
        for start in range(0, grid_rows, block):
            part = slice(start, start + block)
            to = slice(k * grid_rows + start, k * grid_rows + start + block)
            to_slot = jnp.where(iota((slots, block), 0) == send[k : k + 1, part], 1.0, 0.0)
            rows = jnp.concatenate([to_slot, stack_terms(feat[k, :, part], FEAT_ORDER)], 0)
            pick[:, to] = rows.astype(BF)
            rows = jnp.concatenate([rows, jnp.zeros((128 - rows.shape[0], block), F32)], 0)
            pick_turned[to, :] = rows.T.astype(BF)
    for copy in copies[2:]:
        copy.wait()


def encoder_picks(
    count, latent, receive_any, dec_any, node_any, send_any, feat_any,
    to_edge, latent_turned, chain, send, feat, receive, dec_w, node_w, sems,
):
    sources = (receive_any, dec_any, node_any, send_any, feat_any)
    copies = fetch(sources, (receive, dec_w, node_w, send, feat), sems)
    edges = receive.shape[1]
    copies[0].wait()
    block = math.gcd(edges, 512)
    for start in range(0, edges, block):
        part = slice(start, start + block)
        live = iota((1, block), 1) + start < count[0]
        slot = jnp.where(live, receive[:, part], -1)
        to_edge[part, :] = jnp.where(iota((128, block), 0) == slot, 1.0, 0.0).T.astype(BF)
    for copy in copies[1:3]:
        copy.wait()
    chain[...] = mm(node_w[...], dec_w[...]).T.astype(BF)
    latent_turned[...] = latent[...].T
    for copy in copies[3:]:
        copy.wait()


def decoder_kernel(
    cap, mesh_rows, place, first, second, extra, rest, pick, pick_turned, node_w, dec_w, feat_w, cotangent,
    message, keys_out, same_out, slope_out, grad_out, mine_out, rest_out,
):
    slots, width = extra.shape
    keys, same, scales, latent = slot_matches(first, second, place[0], cap, mesh_rows, width)
    agg = jnp.zeros((slots, width), F32)
    for piece, ref in enumerate((first, second)):
        keys_out[piece : piece + 1, :] = keys[piece]
        same_out[piece] = same[piece]
        keys_out[2 + piece : 3 + piece, :] = scales[piece]
        weight = (same[piece].astype(F32) * scales[piece]).astype(BF)
        high, low = fixed_rows(ref, slots, width)
        agg = agg + 256.0 * mm(weight, high) + mm(weight, low)
    shape = (same[0].shape[1], slots)
    chosen = hot(iota(shape, 0) == slots * lax.div(place[0], 2) + iota(shape, 1))
    mine = mm(same[0], chosen).astype(BF)
    mine_out[...] = mine
    agg = agg + mm(mine, rest[...])
    silu, double = halves(0.5 * agg)
    slope_out[...] = 0.25 * double
    hmesh = (latent + mm(silu.astype(BF), node_w[...])).astype(BF)
    proj = mm(hmesh, dec_w[...]).astype(BF)
    rows = pick.shape[0]
    blank = jnp.zeros((128 - rows, width), F32)
    terms = jnp.concatenate([stack_terms(0.5 * feat_w[...], WEIGHT_ORDER), blank], 0).astype(BF)
    table = jnp.concatenate([(0.5 * proj.astype(F32)).astype(BF), terms], 0)
    grid_rows = cotangent.shape[0]
    block = math.gcd(grid_rows, 1024)
    total = jnp.zeros((rows, width), F32)
    for start in range(0, grid_rows, block):
        cot = cotangent[start : start + block, :].astype(F32)
        for base in range(start, 3 * grid_rows, grid_rows):
            part = slice(base, base + block)
            double = halves(mm(pick_turned[part, :], table))[1]
            total = total + mm(pick[:, part], (cot * double).astype(BF))
    total = 0.5 * total
    half = total[:slots].astype(BF)
    rest_out[...] = (total[:slots] - half.astype(F32)).astype(BF)
    grad_out[...] = feature_grad(total[slots:], feat_w.shape[0])
    chips = message.shape[0]
    share = width // chips
    step = slots * share // 128
    for chip in range(chips):
        write_slots(message, chip, half)
        columns = extra[:, chip * share : (chip + 1) * share].astype(F32)
        columns = jnp.concatenate([columns[base : base + step] for base in range(0, slots, step)], 1)
        message[chip, slots * (width // 128) :, :] = columns.astype(BF)


def backward_kernel(
    place, first, second, same, mine, rest, agg_slope, dec_grad, to_edge, latent_turned, chain,
    send, feat, slope, dpx_far, dpx, give, sums_out, grads, dpx_sems,
):
    slots = same.shape[1]
    edges, width = grads.shape
    grid_rows = dpx.shape[0]
    feats = feat.shape[0]
    core = lax.rem(place[0], 2)
    dproj = mm(same[0], slot_rows(first, slots, width)) + mm(same[1], slot_rows(second, slots, width))
    dproj = dproj + mm(mine[...], rest[...])
    high = dproj.astype(BF)
    low = (dproj - high.astype(F32)).astype(BF)
    dact = mm(jnp.concatenate([high, low], 0), chain[...])
    dagg = (dact[:slots] + dact[slots:]) * agg_slope[...]
    dagg = jnp.concatenate([dagg, jnp.zeros((128 - slots, width), F32)], 0).astype(BF)
    block = math.gcd(edges, 1024)
    for start in range(0, edges, block):
        cut = slice(start, start + block)
        grads[cut, :] = (mm(to_edge[cut, :], dagg) * slope[cut, :].astype(F32)).astype(BF)
    step = math.gcd(grid_rows, 512)
    stores = []
    terms = stack_terms(feat[...], FEAT_ORDER).astype(BF)
    for start in range(0, grid_rows, step):
        cut = slice(start, start + step)
        left = hot(iota((step, edges), 0) + start == send[...])
        if start == 0:
            left = jnp.concatenate([left, terms], 0)
        product = mm(left, grads[...])
        if start == 0:
            enc_grad = feature_grad(product[step:], feats)
        dpx[cut, :] = product[:step].astype(BF)
        out = pltpu.make_async_copy(dpx.at[cut, :], dpx_far.at[cut, :], dpx_sems.at[len(stores)])
        out.start()
        stores.append(out)
    sums = jnp.where(iota(enc_grad.shape, 0) < feats, enc_grad, pltpu.roll(dec_grad[...], feats, 0))
    sums_out[...] = sums
    write_shares(give, 1 - core, latent_turned, dpx, sums)
    for out in stores:
        out.wait()


def write_shares(out, side, latent_turned, dpx, sums):
    chips = out.shape[0]
    width = dpx.shape[1]
    rows = width // (2 * chips)
    left = [latent_turned[pl.ds((2 * chip + side) * rows, rows), :] for chip in range(chips)]
    product = mm(jnp.concatenate(left, 0), dpx[...])
    blank = jnp.zeros((8, 128 - rows), F32)
    for chip in range(chips):
        block = product[chip * rows : (chip + 1) * rows]
        pair = [sums[:, base : base + rows] for base in (2 * chip * rows, (2 * chip + 1) * rows)]
        small = jnp.concatenate([jnp.where(side == 0, pair[0], pair[1]), blank], 1)
        pieces = [block[:, base : base + 128] for base in range(0, width, 128)]
        out[chip] = jnp.concatenate([*pieces, small], 0).astype(out.dtype)


def keep_kernel(place, latent_turned, dpx, sums, keep):
    write_shares(keep, lax.rem(place[0], 2), latent_turned, dpx, sums[...])


def pair_kernel(keep, given, out):
    out[...] = (keep[...] + given[...].astype(F32)).astype(BF)


def final_kernel(feats, arrived, out, enc_out, dec_out):
    total = jnp.sum(arrived[...].astype(F32), 0)
    rows, width = out.shape
    for part in range(width // 128):
        out[:, part * 128 : (part + 1) * 128] = total[part * rows : (part + 1) * rows]
    base = rows * (width // 128)
    enc_out[...] = total[base : base + feats, :rows]
    dec_out[...] = total[base + feats : base + 2 * feats, :rows]


def beside_kernel(
    cap, mesh_rows, place, keys, node_any, first_any, second_any, first_back_any, second_back_any, dec_any, dpx_any,
    weight_any, cot_any, mesh_out, dec_out, node_out, grid_out,
    node_w, first, second, first_back, second_back, dec_w, dpx, weight, cotangent, sems,
):
    sources = (
        first_any, second_any, node_any, first_back_any, second_back_any, dec_any, dpx_any, weight_any, cot_any,
    )
    targets = (first, second, node_w, first_back, second_back, dec_w, dpx, weight, cotangent)
    copies = fetch(sources, targets, sems)
    width = node_w.shape[0]
    chips = first.shape[0]
    owners = 2 * chips
    slots = owners * cap
    span = chips * slots
    me = place[0]
    core = lax.rem(me, 2)
    block = width // owners
    key = jnp.concatenate([keys[0:1, :], keys[1:2, :]], 1)
    down = jnp.broadcast_to(key, (128, 2 * span)).T
    scale = jnp.concatenate([keys[2:3, :], keys[3:4, :]], 1)
    same = [
        jnp.where(down == key[:, base : base + 128], scale[:, base : base + 128], 0.0).astype(BF)
        for base in range(0, 2 * span, 128)
    ]
    same = jnp.concatenate(same, 1)
    for copy in copies[:3]:
        copy.wait()
    fixed = [fixed_rows(ref, slots, width) for ref in (first, second)]
    high, low = [jnp.concatenate([a, b], 0) for a, b in zip(*fixed)]
    act = halves(0.5 * (256.0 * mm(same, high) + mm(same, low)))[0].astype(BF)
    shape = (width, 128)
    mine = hot((iota(shape, 0) == block * me + iota(shape, 1)) & (iota(shape, 1) < block))
    node_cols = mm(node_w[...], mine).astype(BF)
    both = mm(act, jnp.concatenate([node_cols, mine], 1))
    step = slots * 2 * block // 128
    pieces = [gathered_slots(piece, chips, core, cap, (span, 1), 0) for piece in range(2)]
    band, owner, turn = [jnp.concatenate([a, b], 0) for a, b in zip(*pieces)]
    source = jnp.where(lax.rem(owner, 2) == core, 0, chips) + lax.div(owner, 2)
    number = cap * band + turn
    at = lax.div(number, step) * (owners * step) + source * step + lax.rem(number, step)
    for copy in copies[3:]:
        copy.wait()
    back = jnp.concatenate([slot_rows(ref, slots, width) for ref in (first_back, second_back)], 0)
    tail = slots * (width // 128)
    columns = [ref[chip, tail:, :] for ref in (first_back, second_back) for chip in range(chips)]
    columns = jnp.concatenate(columns, 0)
    shape = (128, 128)
    folded = []
    for base in range(0, 128, 2 * block):
        fold = hot((iota(shape, 0) == base + block * core + iota(shape, 1)) & (iota(shape, 1) < block))
        folded.append(mm(columns, fold).astype(BF))
    latent = mm(hot(iota((2 * span, 2 * span), 1) == at), jnp.concatenate(folded, 0))
    hmesh = (both[:, :128] + latent).astype(BF)
    left = jnp.concatenate([hmesh, both[:, 128:].astype(BF)], 1)
    sums = mm(left, back, TN)
    dec_out[...] = sums[:block]
    own = (me * mesh_rows + iota((mesh_out.shape[0], 2 * span), 0)).astype(F32)
    dproj = jnp.concatenate([mm(hot(own == key), back), sums[128 : 128 + block]], 0)
    high = dproj.astype(BF)
    low = (dproj - high.astype(F32)).astype(BF)
    turned = mm(high, dec_w[...], NT) + mm(low, dec_w[...], NT)
    mesh = mesh_out.shape[0]
    mesh_out[...] = turned[:mesh].astype(BF)
    node_out[...] = turned[mesh:]
    grid_out[...] = (cotangent[...].astype(F32) + mm(dpx[...], weight[...], NT)).astype(BF)


SMEM = pl.BlockSpec(memory_space=pltpu.SMEM)
VMEM = pl.BlockSpec(memory_space=pltpu.VMEM)
FAR = pl.BlockSpec(memory_space=pltpu.HBM)


def kernel_call(body, name, scalars, near, far, outs, scratch, flops, limit, out_specs=None, pin=False, last=(), kept=0):
    shapes = [jax.ShapeDtypeStruct(shape, dtype) for shape, dtype in outs]
    out_specs = out_specs or [VMEM] * len(shapes)
    pinned = [pltpu.HBM(s.shape, s.dtype) if spec is FAR else s for s, spec in zip(shapes, out_specs)]
    if pin:
        far = [pltpu.with_memory_space_constraint(a, pltpu.HBM) for a in far]
    moved = sum(a.size * a.dtype.itemsize for a in (*near, *far)) + sum(s.size * s.dtype.itemsize for s in shapes)
    buffers = [pltpu.VMEM(a.shape, a.dtype) for a in far[: len(far) - kept]]
    if far:
        buffers.append(pltpu.SemaphoreType.DMA((len(far),)))
    return pl.pallas_call(
        body,
        name=name,
        out_shape=pinned,
        in_specs=[SMEM] * len(scalars) + [VMEM] * len(near) + [FAR] * len(far),
        out_specs=out_specs,
        scratch_shapes=[*scratch, *buffers, *last],
        compiler_params=pltpu.CompilerParams(vmem_limit_bytes=limit * MIB),
        cost_estimate=pl.CostEstimate(flops=flops, bytes_accessed=moved, transcendentals=0),
    )(*scalars, *near, *far)


def gather_plan(
    grid_latent,
    mesh_latent,
    grid_cotangent,
    enc_sender,
    enc_receiver,
    enc_feat,
    enc_count,
    dec_sender,
    dec_feat,
    serve_rows,
    enc_proj,
    node_proj,
    dec_proj,
    enc_feat_w,
    dec_feat_w,
):
    owners = lax.axis_size("lat")
    chips = owners // 2
    cap = serve_rows.shape[2]
    slots = owners * cap
    mesh_rows, width = mesh_latent.shape
    grid_rows = grid_latent.shape[0]
    edges = enc_sender.shape[0]
    feats = enc_feat.shape[0]
    block = width // owners
    span = chips * slots
    parts = width // 128
    share = width // chips
    groups = [[core + 2 * chip for chip in range(chips)] for core in range(2)]
    swap = [(index, index ^ 1) for index in range(owners)]
    place = lax.axis_index("lat").astype(jnp.int32).reshape(1)

    def gather(message, *later):
        first = lax.all_to_all(message, "lat", 0, 0, tiled=True, axis_index_groups=groups)
        first, *later = lax.optimization_barrier((first, *later))
        return first, lax.ppermute(first, "lat", swap), *later

    send = enc_sender.reshape(1, edges)
    receive = enc_receiver.reshape(1, edges)
    message, slope, served, rest = kernel_call(
        lambda *refs: encoder_kernel(cap, *refs),
        "encoder",
        [enc_count],
        [],
        [grid_latent, enc_proj, mesh_latent, send, receive, enc_feat, enc_feat_w.T, serve_rows[0].T],
        [
            ((chips, parts * (slots + 8) + 8, 128), jnp.int16),
            ((edges, width), BF),
            ((slots, width), BF),
            ((slots, width), BF),
        ],
        [
            pltpu.VMEM((grid_rows + 128, width), BF),
            pltpu.VMEM((edges, grid_rows), BF),
            pltpu.VMEM((edges, width), BF),
            pltpu.VMEM((edges, width), BF),
            pltpu.SemaphoreType.DMA((edges // math.gcd(edges, 512),)),
        ],
        2 * edges * grid_rows * width,
        28,
        [VMEM, FAR, VMEM, VMEM],
        pin=True,
        last=[pltpu.SemaphoreType.DMA((grid_rows // math.gcd(grid_rows, 256),))],
    )
    term_rows = stack_rows(feats)
    first, second, served = gather(message, served)
    pick, pick_turned, near_node, near_dec, near_feat_w = kernel_call(
        decoder_picks,
        "decoder_picks",
        [],
        [served],
        [dec_sender, dec_feat, node_proj, dec_proj, dec_feat_w.T],
        [
            ((slots + term_rows, 3 * grid_rows), BF),
            ((3 * grid_rows, 128), BF),
            ((width, width), BF),
            ((width, width), BF),
            ((feats, width), F32),
        ],
        [],
        2000 * MIB,
        16,
        pin=True,
        kept=3,
    )
    message, keys, same, agg_slope, dec_grad, mine, rest = kernel_call(
        lambda *refs: decoder_kernel(cap, mesh_rows, *refs),
        "decoder",
        [place],
        [first, second, served, rest, pick, pick_turned, near_node, near_dec, near_feat_w, grid_cotangent],
        [],
        [
            ((chips, parts * slots + slots * share // 128, 128), BF),
            ((4, span), F32),
            ((2, slots, span), BF),
            ((slots, width), F32),
            ((2 * feats, width), F32),
            ((slots, slots), BF),
            ((slots, width), BF),
        ],
        [],
        24 * grid_rows * 128 * width,
        20,
    )
    first_back, second_back, pick_count = gather(message, enc_count)
    to_edge, latent_turned, chain, near_send, near_feat = kernel_call(
        encoder_picks,
        "encoder_picks",
        [pick_count],
        [grid_latent],
        [receive, dec_proj, node_proj, send, enc_feat],
        [
            ((edges, 128), BF),
            ((width, grid_rows), BF),
            ((width, width), BF),
            ((1, edges), jnp.int32),
            ((feats, edges), F32),
        ],
        [],
        2000 * MIB,
        16,
        pin=True,
        kept=2,
    )
    dpx_far, dpx, give, sums = kernel_call(
        backward_kernel,
        "backward",
        [place],
        [
            first_back,
            second_back,
            same,
            mine,
            rest,
            agg_slope,
            dec_grad,
            to_edge,
            latent_turned,
            chain,
            near_send,
            near_feat,
            slope,
        ],
        [],
        [
            ((grid_rows, width), BF),
            ((grid_rows, width), BF),
            ((chips, parts * block + 8, 128), BF),
            ((2 * feats, width), F32),
        ],
        [
            pltpu.VMEM((edges, width), BF),
            pltpu.SemaphoreType.DMA((grid_rows // math.gcd(grid_rows, 256),)),
        ],
        2 * edges * grid_rows * width,
        24,
        [FAR, VMEM, VMEM, VMEM],
    )
    (keep,) = kernel_call(
        keep_kernel,
        "keep",
        [place],
        [latent_turned, dpx, sums],
        [],
        [((chips, parts * block + 8, 128), F32)],
        [],
        grid_rows * width * width,
        16,
    )
    given = lax.ppermute(give, "lat", swap)
    (pair,) = kernel_call(pair_kernel, "pair", [], [keep, given], [], [(give.shape, BF)], [], keep.size, 8)
    pair, keys, dpx_far = lax.optimization_barrier((pair, keys, dpx_far))
    arrived = lax.all_to_all(pair, "lat", 0, 0, tiled=True, axis_index_groups=groups)
    mesh_grad, dec_proj_grad, node_proj_grad, grid_grad = kernel_call(
        lambda *refs: beside_kernel(cap, mesh_rows, *refs),
        "beside",
        [place],
        [keys],
        [
            node_proj,
            first,
            second,
            first_back,
            second_back,
            dec_proj,
            dpx_far,
            enc_proj,
            grid_cotangent,
        ],
        [
            ((mesh_rows, width), BF),
            ((block, width), F32),
            ((block, width), F32),
            ((grid_rows, width), BF),
        ],
        [],
        2 * (2 * span) * (2 * span) * width,
        30,
        pin=True,
    )
    enc_proj_grad, enc_feat_grad, dec_feat_grad = kernel_call(
        lambda *refs: final_kernel(feats, *refs),
        "final",
        [],
        [arrived],
        [],
        [((block, width), F32), ((feats, block), F32), ((feats, block), F32)],
        [],
        arrived.size,
        8,
    )
    return (
        grid_grad,
        mesh_grad,
        enc_proj_grad,
        node_proj_grad,
        dec_proj_grad,
        enc_feat_grad.T,
        dec_feat_grad.T,
    )


def gather_fits(args):
    mesh_latent, serve_rows = args[1], args[9]
    owners, cap = serve_rows.shape[1], serve_rows.shape[2]
    width = mesh_latent.shape[1]
    chips = owners // 2
    return (
        owners % 2 == 0
        and 2 * cap == 8
        and owners * cap <= 64
        and width % 128 == 0
        and width % (8 * owners) == 0
        and 128 % (width // chips) == 0
        and owners * cap * (width // chips) % 2048 == 0
        and mesh_latent.shape[0] <= 32768
        and mesh_latent.shape[0] * owners < 1 << 24
        and args[0].shape[0] % 128 == 0
        and args[3].shape[0] % 128 == 0
        and args[5].shape[0] == 4
    )


def per_device(*args):
    return gather_plan(*args) if gather_fits(args) else owner_plan(*args)


def solution(mesh):
    placed = (
        P(("member", "lat"), None),
        P(("member", "lat"), None),
        P(("member", "lat"), None),
        P(("member", "lat")),
        P(("member", "lat")),
        P(None, ("member", "lat")),
        P(("member", "lat")),
        P(None, ("member", "lat")),
        P(None, None, ("member", "lat")),
        P(("member", "lat"), None, None),
        P(),
        P(),
        P(),
        P(),
        P(),
    )
    return jax.shard_map(
        per_device,
        mesh=mesh,
        in_specs=placed,
        out_specs=(
            P(("member", "lat"), None),
            P(("member", "lat"), None),
            P(("member", "lat"), None),
            P(("member", "lat"), None),
            P(("member", "lat"), None),
            P(("member", "lat"), None),
            P(("member", "lat"), None),
        ),
        check_vma=False,
    )
```

```python
import math

import jax
import jax.numpy as jnp
from jax import lax
from jax.experimental import pallas as pl
from jax.experimental.pallas import tpu as pltpu
from jax.sharding import PartitionSpec as P

BF = jnp.bfloat16
F32 = jnp.float32
HI = lax.Precision.HIGHEST
MIB = 1 << 20
NN = (((1,), (0,)), ((), ()))
NT = (((1,), (1,)), ((), ()))
TN = (((0,), (0,)), ((), ()))


def silu_grad(value):
    sig = jax.nn.sigmoid(value)
    return sig * (1.0 + value * (1.0 - sig))


def owner_plan(
    grid_latent,
    mesh_latent,
    grid_cotangent,
    enc_sender,
    enc_receiver,
    enc_feat,
    enc_count,
    dec_sender,
    dec_feat,
    serve_rows,
    enc_proj,
    node_proj,
    dec_proj,
    enc_feat_w,
    dec_feat_w,
):
    highest = lax.Precision.HIGHEST
    owners_count = lax.axis_size("lat")
    serve_flat = serve_rows.reshape(-1)
    slot_total = serve_flat.shape[0]
    per_owner = slot_total // owners_count
    mesh_rows = mesh_latent.shape[0]
    grid_rows = grid_latent.shape[0]
    width = grid_latent.shape[1]
    edge_slots = enc_sender.shape[0]
    edge_block = math.gcd(edge_slots, 512)
    grid_block = math.gcd(grid_rows, 512)
    live_count = enc_count[0]
    slot_ids = lax.iota(jnp.int32, slot_total)[:, None]
    row_ids = lax.iota(jnp.int32, grid_rows)[:, None]

    def to_window(rows):
        outgoing = jnp.take(rows, serve_flat, axis=0).reshape(owners_count, per_owner, width)
        arrived = lax.all_to_all(outgoing, "lat", split_axis=0, concat_axis=0, tiled=True)
        return arrived.reshape(slot_total, width)

    def to_owners(partial_value):
        arrived = lax.all_to_all(
            partial_value.reshape(owners_count, per_owner, width),
            "lat",
            split_axis=0,
            concat_axis=0,
            tiled=True,
        )
        return jax.ops.segment_sum(
            arrived.reshape(slot_total, width), serve_flat, num_segments=mesh_rows
        )

    px = jnp.dot(grid_latent, enc_proj, preferred_element_type=jnp.float32).astype(jnp.bfloat16)

    def enc_block(start):
        senders = lax.dynamic_slice_in_dim(enc_sender, start, edge_block)
        receivers = lax.dynamic_slice_in_dim(enc_receiver, start, edge_block)
        feats = lax.dynamic_slice_in_dim(enc_feat, start, edge_block, 1)
        pre = jnp.take(px, senders, axis=0).astype(jnp.float32) + jnp.einsum(
            "fb,lf->bl", feats, enc_feat_w, precision=highest
        )
        live = (lax.iota(jnp.int32, edge_block) + start < live_count)[:, None]
        onehot = (receivers[None, :] == slot_ids).astype(jnp.bfloat16)
        return (pre, live, onehot, senders, feats)

    block_steps = edge_slots // edge_block

    def enc_forward(index, partial_value):
        pre, live, onehot, senders, feats = enc_block(index * edge_block)
        message = jnp.where(live, jax.nn.silu(pre), 0.0).astype(jnp.bfloat16)
        return partial_value + jnp.dot(onehot, message, preferred_element_type=jnp.float32)

    enc_partial = lax.fori_loop(
        0, block_steps, enc_forward, jnp.zeros((slot_total, width), jnp.float32)
    )
    agg = to_owners(enc_partial)
    act = jax.nn.silu(agg).astype(jnp.bfloat16)
    hmesh = (
        mesh_latent.astype(jnp.float32)
        + jnp.dot(act, node_proj, preferred_element_type=jnp.float32)
    ).astype(jnp.bfloat16)
    proj_window = to_window(
        jnp.dot(hmesh, dec_proj, preferred_element_type=jnp.float32).astype(jnp.bfloat16)
    )

    def dec_backward(index, carry):
        dproj, dfw = carry
        start = index * grid_block
        cot = lax.dynamic_slice_in_dim(grid_cotangent, start, grid_block).astype(jnp.float32)
        for k in range(3):
            senders = lax.dynamic_slice_in_dim(dec_sender[k], start, grid_block)
            feats = lax.dynamic_slice_in_dim(dec_feat[k], start, grid_block, 1)
            pre = jnp.take(proj_window, senders, axis=0).astype(jnp.float32) + jnp.einsum(
                "fg,lf->gl", feats, dec_feat_w, precision=highest
            )
            grad_half = (cot * silu_grad(pre)).astype(jnp.bfloat16)
            slot_hot = (senders[None, :] == slot_ids).astype(jnp.bfloat16)
            dproj = dproj + jnp.dot(slot_hot, grad_half, preferred_element_type=jnp.float32)
            dfw = dfw + jnp.einsum(
                "gl,fg->lf", grad_half.astype(jnp.float32), feats, precision=highest
            )
        return (dproj, dfw)

    start_carry = (
        jnp.zeros((slot_total, width), jnp.float32),
        jnp.zeros((width, dec_feat_w.shape[1]), jnp.float32),
    )
    dproj_window, dec_fw_part = lax.fori_loop(0, grid_rows // grid_block, dec_backward, start_carry)
    dec_weight = dec_proj.astype(jnp.float32)
    dproj = to_owners(dproj_window)
    dhmesh = jnp.dot(dproj, dec_weight.T, precision=highest)
    dec_proj_part = jnp.dot(hmesh.astype(jnp.float32).T, dproj, precision=highest)
    mesh_grad = dhmesh.astype(jnp.bfloat16)
    node_proj_part = jnp.dot(act.T, mesh_grad, preferred_element_type=jnp.float32)
    dagg = (
        jnp.dot(mesh_grad, node_proj.T, preferred_element_type=jnp.float32) * silu_grad(agg)
    ).astype(jnp.bfloat16)
    dagg_window = to_window(dagg)

    def enc_backward(index, carry):
        dpx, dew = carry
        pre, live, onehot, senders, feats = enc_block(index * edge_block)
        upstream = jnp.einsum("wb,wl->bl", onehot, dagg_window, preferred_element_type=jnp.float32)
        grad_half = jnp.where(live, upstream * silu_grad(pre), 0.0).astype(jnp.bfloat16)
        row_hot = (senders[None, :] == row_ids).astype(jnp.bfloat16)
        dpx = dpx + jnp.dot(row_hot, grad_half, preferred_element_type=jnp.float32)
        dew = dew + jnp.einsum("bl,fb->lf", grad_half.astype(jnp.float32), feats, precision=highest)
        return (dpx, dew)

    start_back = (
        jnp.zeros((grid_rows, width), jnp.float32),
        jnp.zeros((width, enc_feat_w.shape[1]), jnp.float32),
    )
    dpx_sum, enc_fw_part = lax.fori_loop(0, block_steps, enc_backward, start_back)
    dpx = dpx_sum.astype(jnp.bfloat16)
    enc_proj_part = jnp.dot(grid_latent.T, dpx, preferred_element_type=jnp.float32)
    grid_grad = (
        grid_cotangent.astype(jnp.float32)
        + jnp.dot(dpx, enc_proj.T, preferred_element_type=jnp.float32)
    ).astype(jnp.bfloat16)
    enc_proj_grad, node_proj_grad, dec_proj_grad, enc_feat_w_grad, dec_feat_w_grad = (
        lax.psum_scatter(enc_proj_part, "lat", scatter_dimension=0, tiled=True),
        lax.psum_scatter(node_proj_part, "lat", scatter_dimension=0, tiled=True),
        lax.psum_scatter(dec_proj_part, "lat", scatter_dimension=0, tiled=True),
        lax.psum_scatter(enc_fw_part, "lat", scatter_dimension=0, tiled=True),
        lax.psum_scatter(dec_fw_part, "lat", scatter_dimension=0, tiled=True),
    )
    return (
        grid_grad,
        mesh_grad,
        enc_proj_grad,
        node_proj_grad,
        dec_proj_grad,
        enc_feat_w_grad,
        dec_feat_w_grad,
    )


def mm(a, b, dims=NN, precision=None):
    return lax.dot_general(a, b, dims, precision=precision, preferred_element_type=F32)


def iota(shape, dim):
    return lax.broadcasted_iota(jnp.int32, shape, dim)


def halves(value):
    turn = jnp.tanh(value)
    up = 1.0 + turn
    silu = value * up
    return silu, up + silu * (1.0 - turn)


def hot(mask):
    return jnp.where(mask, 1.0, 0.0).astype(BF)


def split3(value):
    high = value.astype(BF).astype(F32)
    rest = value - high
    middle = rest.astype(BF).astype(F32)
    return high, middle, rest - middle


def stack_rows(feats):
    return -(-6 * feats // 16) * 16


def stack_terms(value, order):
    parts = split3(value)
    rows = len(order) * value.shape[0]
    blank = jnp.zeros((stack_rows(value.shape[0]) - rows, value.shape[1]), F32)
    return jnp.concatenate([*(parts[which] for which in order), blank], 0)


FEAT_ORDER = (0, 0, 1, 1, 2, 0)
WEIGHT_ORDER = (0, 1, 0, 1, 0, 2)


def fetch(sources, targets, sems):
    copies = [pltpu.make_async_copy(src, dst, sems.at[i]) for i, (src, dst) in enumerate(zip(sources, targets))]
    for copy in copies:
        copy.start()
    return copies


def feature_grad(terms, feats):
    total = terms[: 2 * feats] + terms[2 * feats : 4 * feats] + terms[4 * feats : 6 * feats]
    return jnp.where(iota(total.shape, 0) < feats, total, 0.0)


def encoder_kernel(
    cap, count, latent_any, weight_any, mesh_any, send_any, receive_any, feat_any, feat_w_any, serve_any,
    message, slope_far, served_out, own_out, px, picks, silus, slope, slope_sems,
    latent, weight, mesh, send, receive, feat, feat_w, serve, sems, latent_sems,
):
    sources = (send_any, feat_any, weight_any, feat_w_any, receive_any, mesh_any, serve_any)
    targets = (send, feat, weight, feat_w, receive, mesh, serve)
    copies = fetch(sources[:3], targets[:3], sems)
    edges = send.shape[1]
    grid_rows, width = latent.shape
    chips = message.shape[0]
    slots = served_out.shape[0]
    step = math.gcd(grid_rows, 256)
    cuts = [slice(start, start + step) for start in range(0, grid_rows, step)]
    chunks = fetch([latent_any.at[cut, :] for cut in cuts], [latent.at[cut, :] for cut in cuts], latent_sems)
    copies += fetch(sources[3:], targets[3:], sems.at[pl.ds(3, 4)])
    block = math.gcd(edges, 512)
    copies[0].wait()
    copies[1].wait()
    for start in range(0, edges, block):
        part = slice(start, start + block)
        ids = jnp.broadcast_to(send[:, part].astype(F32), (128, block)).T
        for base in range(0, grid_rows, 128):
            lane = (iota((block, 128), 1) + base).astype(F32)
            picks[part, base : base + 128] = hot(ids == lane)
    copies[2].wait()
    for cut, chunk in zip(cuts, chunks):
        chunk.wait()
    px[:grid_rows, :] = (0.5 * mm(latent[...], weight[...]).astype(BF).astype(F32)).astype(BF)
    for copy in copies[3:5]:
        copy.wait()
    terms = stack_terms(0.5 * feat_w[...], WEIGHT_ORDER)
    px[grid_rows:, :] = jnp.concatenate([terms, jnp.zeros((128 - terms.shape[0], width), F32)], 0).astype(BF)
    stores = []
    for start in range(0, edges, block):
        part = slice(start, start + block)
        pre = mm(picks[part, :grid_rows], px[:grid_rows, :])
        pre = pre + mm(stack_terms(feat[:, part], FEAT_ORDER).astype(BF), px[grid_rows : grid_rows + 32, :], TN)
        silu, double = halves(pre)
        slope[part, :] = double.astype(BF)
        out = pltpu.make_async_copy(slope.at[part, :], slope_far.at[part, :], slope_sems.at[len(stores)])
        out.start()
        stores.append(out)
        silus[part, :] = silu.astype(BF)
    live = iota((1, edges), 1) < count[0]
    total = mm(hot(iota((slots, edges), 0) == jnp.where(live, receive[...], -1)), silus[...])
    copies[5].wait()
    copies[6].wait()
    owners = slots // cap
    ids = serve[...]
    spread = hot(iota((owners, slots), 0) == lax.div(iota((owners, slots), 1), cap))
    turn = iota((cap, slots), 0) == iota((cap, slots), 1) % cap
    digits = []
    for value in (lax.shift_right_logical(ids, 8), ids & 255):
        wide = mm(value.astype(F32).astype(BF), spread)
        digits.append(jnp.sum(jnp.where(turn, wide, 0.0), 0, keepdims=True))
    id_row = (digits[0] * 256.0 + digits[1]).astype(jnp.int32)
    served = mm(hot(iota((mesh.shape[0], slots), 0) == id_row), mesh[...], TN)
    served_out[...] = served.astype(BF)
    code, scale, inverse = scale_codes(jnp.max(jnp.abs(total), 1, keepdims=True))
    fixed = to_fixed(total * inverse)
    own_out[...] = (total - fixed.astype(F32) * scale).astype(BF)
    half = fixed.astype(jnp.int16)
    latents = to_fixed(served * (1.0 / LATENT_STEP))
    code_row = jnp.broadcast_to(code.astype(F32), (slots, 128)).T[:1, :]
    lane = iota((slots, 128), 1)
    back = iota((slots, 128), 0)
    wide = 256.0 * mm(digits[0].astype(BF), hot(lane == back)) + mm(digits[1].astype(BF), hot(lane == back))
    wide = wide + mm(code_row.astype(BF), hot(lane == back + slots))
    id_rows = jnp.where(iota((8, 128), 0) == 0, wide, 0.0).astype(jnp.int32)
    for chip in range(chips):
        write_slots(message, chip, half)
        rows = latents[2 * cap * chip : 2 * cap * (chip + 1)]
        tail = [rows[:, base : base + 128] for base in range(0, width, 128)]
        message[chip, slots * (width // 128) :, :] = jnp.concatenate([*tail, id_rows], 0).astype(jnp.int16)
    for out in stores:
        out.wait()


LEAST_POWER = -40
LATENT_STEP = 6.0 / 32000.0


def scale_codes(peak):
    code = jnp.zeros(peak.shape, jnp.int32)
    scale = jnp.full(peak.shape, 2.0**LEAST_POWER, F32)
    inverse = jnp.full(peak.shape, 2.0**-LEAST_POWER, F32)
    for bit in (32, 16, 8, 4, 2, 1):
        more = peak > 32000.0 * (scale * 2.0 ** (bit - 1))
        code = code + jnp.where(more, bit, 0)
        scale = scale * jnp.where(more, 2.0**bit, 1.0)
        inverse = inverse * jnp.where(more, 2.0**-bit, 1.0)
    return code, scale, inverse


def scale_values(code):
    value = jnp.full(code.shape, 2.0**LEAST_POWER, F32)
    for bit in range(6):
        value = value * jnp.where((lax.shift_right_logical(code, bit) & 1) == 1, 2.0 ** (1 << bit), 1.0)
    return value


def to_fixed(value):
    return jnp.floor(value + 0.5).astype(jnp.int32)


def fixed_rows(ref, slots, width):
    parts = [
        jnp.concatenate([ref[chip, base : base + slots, :].astype(jnp.int32) for chip in range(ref.shape[0])], 0)
        for base in range(0, slots * (width // 128), slots)
    ]
    value = jnp.concatenate(parts, 1)
    return lax.shift_right_arithmetic(value, 8).astype(F32).astype(BF), (value & 255).astype(F32).astype(BF)


def write_slots(message, chip, value):
    slots = value.shape[0]
    for part in range(value.shape[1] // 128):
        message[chip, part * slots : (part + 1) * slots, :] = value[:, part * 128 : (part + 1) * 128]


def slot_rows(ref, slots, width):
    parts = [
        jnp.concatenate([ref[chip, base : base + slots, :] for chip in range(ref.shape[0])], 0)
        for base in range(0, slots * (width // 128), slots)
    ]
    return jnp.concatenate(parts, 1)


def gathered_slots(piece, chips, core, cap, shape, dim):
    slots = 2 * chips * cap
    index = iota(shape, dim)
    chip = lax.div(index, slots)
    slot = index - chip * slots
    band = 2 * chip + jnp.where(piece == 0, core, 1 - core)
    return band, lax.div(slot, cap), lax.rem(slot, cap)


def holder_of(shape, dim, chips, core):
    index = iota(shape, dim)
    return jnp.where(index < chips, 2 * index + core, 2 * (index - chips) + 1 - core)


def slot_matches(first, second, me, cap, mesh_rows, width):
    chips = first.shape[0]
    owners = 2 * chips
    slots = owners * cap
    span = chips * slots
    parts = width // 128
    core = lax.rem(me, 2)
    tables = [jnp.zeros((owners, 128), F32)] * 2
    latent = jnp.zeros((slots, width), F32)
    for piece, ref in enumerate((first, second)):
        ids, rows = [], []
        for chip in range(chips):
            tail = ref[chip, slots * parts :, :].astype(jnp.int32)
            ids.append(tail[8 * parts :])
            rows.append(jnp.concatenate([tail[8 * part : 8 * part + 8] for part in range(parts)], 1))
        ids = jnp.concatenate(ids, 0)
        rows = jnp.concatenate(rows, 0)
        shape = (owners, 8 * chips)
        take = hot(iota(shape, 1) == (iota(shape, 0) - piece * chips) * 8)
        for index, digit in enumerate((lax.shift_right_arithmetic(ids, 8), ids & 255)):
            tables[index] = tables[index] + mm(take, digit.astype(F32).astype(BF))
        shape = (slots, 8 * chips)
        window = iota(shape, 0)
        owner = lax.div(window, cap)
        held = lax.rem(owner, 2) == (core if piece == 0 else 1 - core)
        at = lax.div(owner, 2) * 8 + cap * core + lax.rem(window, cap)
        pick = hot(held & (iota(shape, 1) == at))
        high = lax.shift_right_arithmetic(rows, 8).astype(F32).astype(BF)
        latent = latent + 256.0 * mm(pick, high) + mm(pick, (rows & 255).astype(F32).astype(BF))
    latent = (latent * LATENT_STEP).astype(BF).astype(F32)
    digits = jnp.concatenate(tables, 0).astype(BF)
    shape = (slots, 2 * owners)
    half = lax.rem(iota(shape, 1), owners)
    holder = jnp.where(half < chips, 2 * half + core, 2 * (half - chips) + 1 - core)
    wanted = jnp.where(holder == lax.div(iota(shape, 0), cap), 1.0, 0.0)
    mine = mm((wanted * jnp.where(iota(shape, 1) < owners, 256.0, 1.0)).astype(BF), digits)
    lane = iota((slots, 128), 1) - cap * me - lax.rem(iota((slots, 128), 0), cap)
    own_key = jnp.sum(jnp.where(lane == 0, mine, 0.0), 1, keepdims=True)
    own_key = own_key + (lax.div(iota((slots, 1), 0), cap) * mesh_rows).astype(F32)
    keys, same, scales = [], [], []
    for piece in range(2):
        band, owner, place = gathered_slots(piece, chips, core, cap, (1, span), 1)
        spread = mm(digits, hot(iota((128, span), 0) == cap * band + place))
        value = 256.0 * spread[:owners] + spread[owners:]
        value = jnp.where(holder_of((owners, 1), 0, chips, core) == owner, value, 0.0)
        key = jnp.sum(value, 0, keepdims=True) + (owner * mesh_rows).astype(F32)
        keys.append(key)
        same.append(hot(key == own_key))
        index = iota((1, span), 1)
        spread = mm(digits[owners:], hot(iota((128, span), 0) == slots + lax.rem(index, slots)))
        source = iota((owners, 1), 0) - piece * chips == lax.div(index, slots)
        code = jnp.sum(jnp.where(source, spread, 0.0), 0, keepdims=True)
        scales.append(scale_values(code.astype(jnp.int32)))
    return keys, same, scales, latent


def decoder_picks(
    after, send_any, feat_any, node_any, dec_any, feat_w_any,
    pick, pick_turned, node_w, dec_w, feat_w, send, feat, sems,
):
    sources = (send_any, feat_any, node_any, dec_any, feat_w_any)
    copies = fetch(sources, (send, feat, node_w, dec_w, feat_w), sems)
    slots = after.shape[0]
    grid_rows = send.shape[1]
    copies[0].wait()
    copies[1].wait()
    block = math.gcd(grid_rows, 512)
    for k in range(3):
        for start in range(0, grid_rows, block):
            part = slice(start, start + block)
            to = slice(k * grid_rows + start, k * grid_rows + start + block)
            to_slot = jnp.where(iota((slots, block), 0) == send[k : k + 1, part], 1.0, 0.0)
            rows = jnp.concatenate([to_slot, stack_terms(feat[k, :, part], FEAT_ORDER)], 0)
            pick[:, to] = rows.astype(BF)
            rows = jnp.concatenate([rows, jnp.zeros((128 - rows.shape[0], block), F32)], 0)
            pick_turned[to, :] = rows.T.astype(BF)
    for copy in copies[2:]:
        copy.wait()


def encoder_picks(
    count, latent, receive_any, dec_any, node_any, send_any, feat_any,
    to_edge, latent_turned, chain, send, feat, receive, dec_w, node_w, sems,
):
    sources = (receive_any, dec_any, node_any, send_any, feat_any)
    copies = fetch(sources, (receive, dec_w, node_w, send, feat), sems)
    edges = receive.shape[1]
    copies[0].wait()
    block = math.gcd(edges, 512)
    for start in range(0, edges, block):
        part = slice(start, start + block)
        live = iota((1, block), 1) + start < count[0]
        slot = jnp.where(live, receive[:, part], -1)
        to_edge[part, :] = jnp.where(iota((128, block), 0) == slot, 1.0, 0.0).T.astype(BF)
    for copy in copies[1:3]:
        copy.wait()
    chain[...] = mm(node_w[...], dec_w[...]).T.astype(BF)
    latent_turned[...] = latent[...].T
    for copy in copies[3:]:
        copy.wait()


def decoder_kernel(
    cap, mesh_rows, place, first, second, extra, rest, pick, pick_turned, node_w, dec_w, feat_w, cotangent,
    message, keys_out, same_out, slope_out, grad_out, mine_out, rest_out,
):
    slots, width = extra.shape
    keys, same, scales, latent = slot_matches(first, second, place[0], cap, mesh_rows, width)
    agg = jnp.zeros((slots, width), F32)
    for piece, ref in enumerate((first, second)):
        keys_out[piece : piece + 1, :] = keys[piece]
        same_out[piece] = same[piece]
        keys_out[2 + piece : 3 + piece, :] = scales[piece]
        weight = (same[piece].astype(F32) * scales[piece]).astype(BF)
        high, low = fixed_rows(ref, slots, width)
        agg = agg + 256.0 * mm(weight, high) + mm(weight, low)
    shape = (same[0].shape[1], slots)
    chosen = hot(iota(shape, 0) == slots * lax.div(place[0], 2) + iota(shape, 1))
    mine = mm(same[0], chosen).astype(BF)
    mine_out[...] = mine
    agg = agg + mm(mine, rest[...])
    silu, double = halves(0.5 * agg)
    slope_out[...] = 0.25 * double
    hmesh = (latent + mm(silu.astype(BF), node_w[...])).astype(BF)
    proj = mm(hmesh, dec_w[...]).astype(BF)
    rows = pick.shape[0]
    blank = jnp.zeros((128 - rows, width), F32)
    terms = jnp.concatenate([stack_terms(0.5 * feat_w[...], WEIGHT_ORDER), blank], 0).astype(BF)
    table = jnp.concatenate([(0.5 * proj.astype(F32)).astype(BF), terms], 0)
    grid_rows = cotangent.shape[0]
    block = math.gcd(grid_rows, 1024)
    total = jnp.zeros((rows, width), F32)
    for start in range(0, grid_rows, block):
        cot = cotangent[start : start + block, :].astype(F32)
        for base in range(start, 3 * grid_rows, grid_rows):
            part = slice(base, base + block)
            double = halves(mm(pick_turned[part, :], table))[1]
            total = total + mm(pick[:, part], (cot * double).astype(BF))
    total = 0.5 * total
    half = total[:slots].astype(BF)
    rest_out[...] = (total[:slots] - half.astype(F32)).astype(BF)
    grad_out[...] = feature_grad(total[slots:], feat_w.shape[0])
    chips = message.shape[0]
    share = width // chips
    step = slots * share // 128
    for chip in range(chips):
        write_slots(message, chip, half)
        columns = extra[:, chip * share : (chip + 1) * share].astype(F32)
        columns = jnp.concatenate([columns[base : base + step] for base in range(0, slots, step)], 1)
        message[chip, slots * (width // 128) :, :] = columns.astype(BF)


def backward_kernel(
    place, first, second, same, mine, rest, agg_slope, dec_grad, to_edge, latent_turned, chain,
    send, feat, slope, dpx_far, dpx, give, sums_out, grads, dpx_sems,
):
    slots = same.shape[1]
    edges, width = grads.shape
    grid_rows = dpx.shape[0]
    feats = feat.shape[0]
    core = lax.rem(place[0], 2)
    dproj = mm(same[0], slot_rows(first, slots, width)) + mm(same[1], slot_rows(second, slots, width))
    dproj = dproj + mm(mine[...], rest[...])
    high = dproj.astype(BF)
    low = (dproj - high.astype(F32)).astype(BF)
    dact = mm(jnp.concatenate([high, low], 0), chain[...])
    dagg = (dact[:slots] + dact[slots:]) * agg_slope[...]
    dagg = jnp.concatenate([dagg, jnp.zeros((128 - slots, width), F32)], 0).astype(BF)
    block = math.gcd(edges, 1024)
    for start in range(0, edges, block):
        cut = slice(start, start + block)
        grads[cut, :] = (mm(to_edge[cut, :], dagg) * slope[cut, :].astype(F32)).astype(BF)
    step = math.gcd(grid_rows, 512)
    stores = []
    terms = stack_terms(feat[...], FEAT_ORDER).astype(BF)
    for start in range(0, grid_rows, step):
        cut = slice(start, start + step)
        left = hot(iota((step, edges), 0) + start == send[...])
        if start == 0:
            left = jnp.concatenate([left, terms], 0)
        product = mm(left, grads[...])
        if start == 0:
            enc_grad = feature_grad(product[step:], feats)
        dpx[cut, :] = product[:step].astype(BF)
        out = pltpu.make_async_copy(dpx.at[cut, :], dpx_far.at[cut, :], dpx_sems.at[len(stores)])
        out.start()
        stores.append(out)
    sums = jnp.where(iota(enc_grad.shape, 0) < feats, enc_grad, pltpu.roll(dec_grad[...], feats, 0))
    sums_out[...] = sums
    write_shares(give, 1 - core, latent_turned, dpx, sums)
    for out in stores:
        out.wait()


def write_shares(out, side, latent_turned, dpx, sums):
    chips = out.shape[0]
    width = dpx.shape[1]
    rows = width // (2 * chips)
    left = [latent_turned[pl.ds((2 * chip + side) * rows, rows), :] for chip in range(chips)]
    product = mm(jnp.concatenate(left, 0), dpx[...])
    blank = jnp.zeros((8, 128 - rows), F32)
    for chip in range(chips):
        block = product[chip * rows : (chip + 1) * rows]
        pair = [sums[:, base : base + rows] for base in (2 * chip * rows, (2 * chip + 1) * rows)]
        small = jnp.concatenate([jnp.where(side == 0, pair[0], pair[1]), blank], 1)
        pieces = [block[:, base : base + 128] for base in range(0, width, 128)]
        out[chip] = jnp.concatenate([*pieces, small], 0).astype(out.dtype)


def keep_kernel(place, latent_turned, dpx, sums, keep):
    write_shares(keep, lax.rem(place[0], 2), latent_turned, dpx, sums[...])


def pair_kernel(keep, given, out):
    out[...] = (keep[...] + given[...].astype(F32)).astype(BF)


def final_kernel(feats, arrived, out, enc_out, dec_out):
    total = jnp.sum(arrived[...].astype(F32), 0)
    rows, width = out.shape
    for part in range(width // 128):
        out[:, part * 128 : (part + 1) * 128] = total[part * rows : (part + 1) * rows]
    base = rows * (width // 128)
    enc_out[...] = total[base : base + feats, :rows]
    dec_out[...] = total[base + feats : base + 2 * feats, :rows]


def beside_kernel(
    cap, mesh_rows, place, keys, node_any, first_any, second_any, first_back_any, second_back_any, dec_any, dpx_any,
    weight_any, cot_any, mesh_out, dec_out, node_out, grid_out,
    node_w, first, second, first_back, second_back, dec_w, dpx, weight, cotangent, sems,
):
    sources = (
        first_any, second_any, node_any, first_back_any, second_back_any, dec_any, dpx_any, weight_any, cot_any,
    )
    targets = (first, second, node_w, first_back, second_back, dec_w, dpx, weight, cotangent)
    copies = fetch(sources, targets, sems)
    width = node_w.shape[0]
    chips = first.shape[0]
    owners = 2 * chips
    slots = owners * cap
    span = chips * slots
    me = place[0]
    core = lax.rem(me, 2)
    block = width // owners
    key = jnp.concatenate([keys[0:1, :], keys[1:2, :]], 1)
    down = jnp.broadcast_to(key, (128, 2 * span)).T
    scale = jnp.concatenate([keys[2:3, :], keys[3:4, :]], 1)
    same = [
        jnp.where(down == key[:, base : base + 128], scale[:, base : base + 128], 0.0).astype(BF)
        for base in range(0, 2 * span, 128)
    ]
    same = jnp.concatenate(same, 1)
    for copy in copies[:3]:
        copy.wait()
    forward = jnp.concatenate([slot_rows(ref, slots, width) for ref in (first, second)], 0)
    act = halves(0.5 * mm(same, forward.astype(F32).astype(BF)))[0].astype(BF)
    shape = (width, 128)
    mine = hot((iota(shape, 0) == block * me + iota(shape, 1)) & (iota(shape, 1) < block))
    node_cols = mm(node_w[...], mine).astype(BF)
    both = mm(act, jnp.concatenate([node_cols, mine], 1))
    step = slots * 2 * block // 128
    pieces = [gathered_slots(piece, chips, core, cap, (span, 1), 0) for piece in range(2)]
    band, owner, turn = [jnp.concatenate([a, b], 0) for a, b in zip(*pieces)]
    source = jnp.where(lax.rem(owner, 2) == core, 0, chips) + lax.div(owner, 2)
    number = cap * band + turn
    at = lax.div(number, step) * (owners * step) + source * step + lax.rem(number, step)
    for copy in copies[3:]:
        copy.wait()
    back = jnp.concatenate([slot_rows(ref, slots, width) for ref in (first_back, second_back)], 0)
    tail = slots * (width // 128)
    columns = [ref[chip, tail:, :] for ref in (first_back, second_back) for chip in range(chips)]
    columns = jnp.concatenate(columns, 0)
    shape = (128, 128)
    folded = []
    for base in range(0, 128, 2 * block):
        fold = hot((iota(shape, 0) == base + block * core + iota(shape, 1)) & (iota(shape, 1) < block))
        folded.append(mm(columns, fold).astype(BF))
    latent = mm(hot(iota((2 * span, 2 * span), 1) == at), jnp.concatenate(folded, 0))
    hmesh = (both[:, :128] + latent).astype(BF)
    left = jnp.concatenate([hmesh, both[:, 128:].astype(BF)], 1)
    sums = mm(left, back, TN)
    dec_out[...] = sums[:block]
    own = (me * mesh_rows + iota((mesh_out.shape[0], 2 * span), 0)).astype(F32)
    dproj = jnp.concatenate([mm(hot(own == key), back), sums[128 : 128 + block]], 0)
    high = dproj.astype(BF)
    low = (dproj - high.astype(F32)).astype(BF)
    turned = mm(high, dec_w[...], NT) + mm(low, dec_w[...], NT)
    mesh = mesh_out.shape[0]
    mesh_out[...] = turned[:mesh].astype(BF)
    node_out[...] = turned[mesh:]
    grid_out[...] = (cotangent[...].astype(F32) + mm(dpx[...], weight[...], NT)).astype(BF)


SMEM = pl.BlockSpec(memory_space=pltpu.SMEM)
VMEM = pl.BlockSpec(memory_space=pltpu.VMEM)
FAR = pl.BlockSpec(memory_space=pltpu.HBM)


def kernel_call(body, name, scalars, near, far, outs, scratch, flops, limit, out_specs=None, pin=False, last=(), kept=0):
    shapes = [jax.ShapeDtypeStruct(shape, dtype) for shape, dtype in outs]
    out_specs = out_specs or [VMEM] * len(shapes)
    pinned = [pltpu.HBM(s.shape, s.dtype) if spec is FAR else s for s, spec in zip(shapes, out_specs)]
    if pin:
        far = [pltpu.with_memory_space_constraint(a, pltpu.HBM) for a in far]
    moved = sum(a.size * a.dtype.itemsize for a in (*near, *far)) + sum(s.size * s.dtype.itemsize for s in shapes)
    buffers = [pltpu.VMEM(a.shape, a.dtype) for a in far[: len(far) - kept]]
    if far:
        buffers.append(pltpu.SemaphoreType.DMA((len(far),)))
    return pl.pallas_call(
        body,
        name=name,
        out_shape=pinned,
        in_specs=[SMEM] * len(scalars) + [VMEM] * len(near) + [FAR] * len(far),
        out_specs=out_specs,
        scratch_shapes=[*scratch, *buffers, *last],
        compiler_params=pltpu.CompilerParams(vmem_limit_bytes=limit * MIB),
        cost_estimate=pl.CostEstimate(flops=flops, bytes_accessed=moved, transcendentals=0),
    )(*scalars, *near, *far)


def gather_plan(
    grid_latent,
    mesh_latent,
    grid_cotangent,
    enc_sender,
    enc_receiver,
    enc_feat,
    enc_count,
    dec_sender,
    dec_feat,
    serve_rows,
    enc_proj,
    node_proj,
    dec_proj,
    enc_feat_w,
    dec_feat_w,
):
    owners = lax.axis_size("lat")
    chips = owners // 2
    cap = serve_rows.shape[2]
    slots = owners * cap
    mesh_rows, width = mesh_latent.shape
    grid_rows = grid_latent.shape[0]
    edges = enc_sender.shape[0]
    feats = enc_feat.shape[0]
    block = width // owners
    span = chips * slots
    parts = width // 128
    share = width // chips
    groups = [[core + 2 * chip for chip in range(chips)] for core in range(2)]
    swap = [(index, index ^ 1) for index in range(owners)]
    place = lax.axis_index("lat").astype(jnp.int32).reshape(1)

    def gather(message, *later):
        first = lax.all_to_all(message, "lat", 0, 0, tiled=True, axis_index_groups=groups)
        first, *later = lax.optimization_barrier((first, *later))
        return first, lax.ppermute(first, "lat", swap), *later

    send = enc_sender.reshape(1, edges)
    receive = enc_receiver.reshape(1, edges)
    message, slope, served, rest = kernel_call(
        lambda *refs: encoder_kernel(cap, *refs),
        "encoder",
        [enc_count],
        [],
        [grid_latent, enc_proj, mesh_latent, send, receive, enc_feat, enc_feat_w.T, serve_rows[0].T],
        [
            ((chips, parts * (slots + 8) + 8, 128), jnp.int16),
            ((edges, width), BF),
            ((slots, width), BF),
            ((slots, width), BF),
        ],
        [
            pltpu.VMEM((grid_rows + 128, width), BF),
            pltpu.VMEM((edges, grid_rows), BF),
            pltpu.VMEM((edges, width), BF),
            pltpu.VMEM((edges, width), BF),
            pltpu.SemaphoreType.DMA((edges // math.gcd(edges, 512),)),
        ],
        2 * edges * grid_rows * width,
        28,
        [VMEM, FAR, VMEM, VMEM],
        pin=True,
        last=[pltpu.SemaphoreType.DMA((grid_rows // math.gcd(grid_rows, 256),))],
    )
    term_rows = stack_rows(feats)
    first, second, served = gather(message, served)
    pick, pick_turned, near_node, near_dec, near_feat_w = kernel_call(
        decoder_picks,
        "decoder_picks",
        [],
        [served],
        [dec_sender, dec_feat, node_proj, dec_proj, dec_feat_w.T],
        [
            ((slots + term_rows, 3 * grid_rows), BF),
            ((3 * grid_rows, 128), BF),
            ((width, width), BF),
            ((width, width), BF),
            ((feats, width), F32),
        ],
        [],
        2000 * MIB,
        16,
        pin=True,
        kept=3,
    )
    message, keys, same, agg_slope, dec_grad, mine, rest = kernel_call(
        lambda *refs: decoder_kernel(cap, mesh_rows, *refs),
        "decoder",
        [place],
        [first, second, served, rest, pick, pick_turned, near_node, near_dec, near_feat_w, grid_cotangent],
        [],
        [
            ((chips, parts * slots + slots * share // 128, 128), BF),
            ((4, span), F32),
            ((2, slots, span), BF),
            ((slots, width), F32),
            ((2 * feats, width), F32),
            ((slots, slots), BF),
            ((slots, width), BF),
        ],
        [],
        24 * grid_rows * 128 * width,
        20,
    )
    first_back, second_back, pick_count = gather(message, enc_count)
    to_edge, latent_turned, chain, near_send, near_feat = kernel_call(
        encoder_picks,
        "encoder_picks",
        [pick_count],
        [grid_latent],
        [receive, dec_proj, node_proj, send, enc_feat],
        [
            ((edges, 128), BF),
            ((width, grid_rows), BF),
            ((width, width), BF),
            ((1, edges), jnp.int32),
            ((feats, edges), F32),
        ],
        [],
        2000 * MIB,
        16,
        pin=True,
        kept=2,
    )
    dpx_far, dpx, give, sums = kernel_call(
        backward_kernel,
        "backward",
        [place],
        [
            first_back,
            second_back,
            same,
            mine,
            rest,
            agg_slope,
            dec_grad,
            to_edge,
            latent_turned,
            chain,
            near_send,
            near_feat,
            slope,
        ],
        [],
        [
            ((grid_rows, width), BF),
            ((grid_rows, width), BF),
            ((chips, parts * block + 8, 128), BF),
            ((2 * feats, width), F32),
        ],
        [
            pltpu.VMEM((edges, width), BF),
            pltpu.SemaphoreType.DMA((grid_rows // math.gcd(grid_rows, 256),)),
        ],
        2 * edges * grid_rows * width,
        24,
        [FAR, VMEM, VMEM, VMEM],
    )
    (keep,) = kernel_call(
        keep_kernel,
        "keep",
        [place],
        [latent_turned, dpx, sums],
        [],
        [((chips, parts * block + 8, 128), F32)],
        [],
        grid_rows * width * width,
        16,
    )
    given = lax.ppermute(give, "lat", swap)
    (pair,) = kernel_call(pair_kernel, "pair", [], [keep, given], [], [(give.shape, BF)], [], keep.size, 8)
    pair, keys, dpx_far = lax.optimization_barrier((pair, keys, dpx_far))
    arrived = lax.all_to_all(pair, "lat", 0, 0, tiled=True, axis_index_groups=groups)
    mesh_grad, dec_proj_grad, node_proj_grad, grid_grad = kernel_call(
        lambda *refs: beside_kernel(cap, mesh_rows, *refs),
        "beside",
        [place],
        [keys],
        [
            node_proj,
            first,
            second,
            first_back,
            second_back,
            dec_proj,
            dpx_far,
            enc_proj,
            grid_cotangent,
        ],
        [
            ((mesh_rows, width), BF),
            ((block, width), F32),
            ((block, width), F32),
            ((grid_rows, width), BF),
        ],
        [],
        2 * (2 * span) * (2 * span) * width,
        30,
        pin=True,
    )
    enc_proj_grad, enc_feat_grad, dec_feat_grad = kernel_call(
        lambda *refs: final_kernel(feats, *refs),
        "final",
        [],
        [arrived],
        [],
        [((block, width), F32), ((feats, block), F32), ((feats, block), F32)],
        [],
        arrived.size,
        8,
    )
    return (
        grid_grad,
        mesh_grad,
        enc_proj_grad,
        node_proj_grad,
        dec_proj_grad,
        enc_feat_grad.T,
        dec_feat_grad.T,
    )


def gather_fits(args):
    mesh_latent, serve_rows = args[1], args[9]
    owners, cap = serve_rows.shape[1], serve_rows.shape[2]
    width = mesh_latent.shape[1]
    chips = owners // 2
    return (
        owners % 2 == 0
        and 2 * cap == 8
        and owners * cap <= 64
        and width % 128 == 0
        and width % (8 * owners) == 0
        and 128 % (width // chips) == 0
        and owners * cap * (width // chips) % 2048 == 0
        and mesh_latent.shape[0] <= 32768
        and mesh_latent.shape[0] * owners < 1 << 24
        and args[0].shape[0] % 128 == 0
        and args[3].shape[0] % 128 == 0
        and args[5].shape[0] == 4
    )


def per_device(*args):
    return gather_plan(*args) if gather_fits(args) else owner_plan(*args)


def solution(mesh):
    placed = (
        P(("member", "lat"), None),
        P(("member", "lat"), None),
        P(("member", "lat"), None),
        P(("member", "lat")),
        P(("member", "lat")),
        P(None, ("member", "lat")),
        P(("member", "lat")),
        P(None, ("member", "lat")),
        P(None, None, ("member", "lat")),
        P(("member", "lat"), None, None),
        P(),
        P(),
        P(),
        P(),
        P(),
    )
    return jax.shard_map(
        per_device,
        mesh=mesh,
        in_specs=placed,
        out_specs=(
            P(("member", "lat"), None),
            P(("member", "lat"), None),
            P(("member", "lat"), None),
            P(("member", "lat"), None),
            P(("member", "lat"), None),
            P(("member", "lat"), None),
            P(("member", "lat"), None),
        ),
        check_vma=False,
    )
```

```python
import math

import jax
import jax.numpy as jnp
from jax import lax
from jax.experimental import pallas as pl
from jax.experimental.pallas import tpu as pltpu
from jax.sharding import PartitionSpec as P

BF = jnp.bfloat16
F32 = jnp.float32
HI = lax.Precision.HIGHEST
MIB = 1 << 20
NN = (((1,), (0,)), ((), ()))
NT = (((1,), (1,)), ((), ()))
TN = (((0,), (0,)), ((), ()))


def silu_grad(value):
    sig = jax.nn.sigmoid(value)
    return sig * (1.0 + value * (1.0 - sig))


def owner_plan(
    grid_latent,
    mesh_latent,
    grid_cotangent,
    enc_sender,
    enc_receiver,
    enc_feat,
    enc_count,
    dec_sender,
    dec_feat,
    serve_rows,
    enc_proj,
    node_proj,
    dec_proj,
    enc_feat_w,
    dec_feat_w,
):
    highest = lax.Precision.HIGHEST
    owners_count = lax.axis_size("lat")
    serve_flat = serve_rows.reshape(-1)
    slot_total = serve_flat.shape[0]
    per_owner = slot_total // owners_count
    mesh_rows = mesh_latent.shape[0]
    grid_rows = grid_latent.shape[0]
    width = grid_latent.shape[1]
    edge_slots = enc_sender.shape[0]
    edge_block = math.gcd(edge_slots, 512)
    grid_block = math.gcd(grid_rows, 512)
    live_count = enc_count[0]
    slot_ids = lax.iota(jnp.int32, slot_total)[:, None]
    row_ids = lax.iota(jnp.int32, grid_rows)[:, None]

    def to_window(rows):
        outgoing = jnp.take(rows, serve_flat, axis=0).reshape(owners_count, per_owner, width)
        arrived = lax.all_to_all(outgoing, "lat", split_axis=0, concat_axis=0, tiled=True)
        return arrived.reshape(slot_total, width)

    def to_owners(partial_value):
        arrived = lax.all_to_all(
            partial_value.reshape(owners_count, per_owner, width),
            "lat",
            split_axis=0,
            concat_axis=0,
            tiled=True,
        )
        return jax.ops.segment_sum(
            arrived.reshape(slot_total, width), serve_flat, num_segments=mesh_rows
        )

    px = jnp.dot(grid_latent, enc_proj, preferred_element_type=jnp.float32).astype(jnp.bfloat16)

    def enc_block(start):
        senders = lax.dynamic_slice_in_dim(enc_sender, start, edge_block)
        receivers = lax.dynamic_slice_in_dim(enc_receiver, start, edge_block)
        feats = lax.dynamic_slice_in_dim(enc_feat, start, edge_block, 1)
        pre = jnp.take(px, senders, axis=0).astype(jnp.float32) + jnp.einsum(
            "fb,lf->bl", feats, enc_feat_w, precision=highest
        )
        live = (lax.iota(jnp.int32, edge_block) + start < live_count)[:, None]
        onehot = (receivers[None, :] == slot_ids).astype(jnp.bfloat16)
        return (pre, live, onehot, senders, feats)

    block_steps = edge_slots // edge_block

    def enc_forward(index, partial_value):
        pre, live, onehot, senders, feats = enc_block(index * edge_block)
        message = jnp.where(live, jax.nn.silu(pre), 0.0).astype(jnp.bfloat16)
        return partial_value + jnp.dot(onehot, message, preferred_element_type=jnp.float32)

    enc_partial = lax.fori_loop(
        0, block_steps, enc_forward, jnp.zeros((slot_total, width), jnp.float32)
    )
    agg = to_owners(enc_partial)
    act = jax.nn.silu(agg).astype(jnp.bfloat16)
    hmesh = (
        mesh_latent.astype(jnp.float32)
        + jnp.dot(act, node_proj, preferred_element_type=jnp.float32)
    ).astype(jnp.bfloat16)
    proj_window = to_window(
        jnp.dot(hmesh, dec_proj, preferred_element_type=jnp.float32).astype(jnp.bfloat16)
    )

    def dec_backward(index, carry):
        dproj, dfw = carry
        start = index * grid_block
        cot = lax.dynamic_slice_in_dim(grid_cotangent, start, grid_block).astype(jnp.float32)
        for k in range(3):
            senders = lax.dynamic_slice_in_dim(dec_sender[k], start, grid_block)
            feats = lax.dynamic_slice_in_dim(dec_feat[k], start, grid_block, 1)
            pre = jnp.take(proj_window, senders, axis=0).astype(jnp.float32) + jnp.einsum(
                "fg,lf->gl", feats, dec_feat_w, precision=highest
            )
            grad_half = (cot * silu_grad(pre)).astype(jnp.bfloat16)
            slot_hot = (senders[None, :] == slot_ids).astype(jnp.bfloat16)
            dproj = dproj + jnp.dot(slot_hot, grad_half, preferred_element_type=jnp.float32)
            dfw = dfw + jnp.einsum(
                "gl,fg->lf", grad_half.astype(jnp.float32), feats, precision=highest
            )
        return (dproj, dfw)

    start_carry = (
        jnp.zeros((slot_total, width), jnp.float32),
        jnp.zeros((width, dec_feat_w.shape[1]), jnp.float32),
    )
    dproj_window, dec_fw_part = lax.fori_loop(0, grid_rows // grid_block, dec_backward, start_carry)
    dec_weight = dec_proj.astype(jnp.float32)
    dproj = to_owners(dproj_window)
    dhmesh = jnp.dot(dproj, dec_weight.T, precision=highest)
    dec_proj_part = jnp.dot(hmesh.astype(jnp.float32).T, dproj, precision=highest)
    mesh_grad = dhmesh.astype(jnp.bfloat16)
    node_proj_part = jnp.dot(act.T, mesh_grad, preferred_element_type=jnp.float32)
    dagg = (
        jnp.dot(mesh_grad, node_proj.T, preferred_element_type=jnp.float32) * silu_grad(agg)
    ).astype(jnp.bfloat16)
    dagg_window = to_window(dagg)

    def enc_backward(index, carry):
        dpx, dew = carry
        pre, live, onehot, senders, feats = enc_block(index * edge_block)
        upstream = jnp.einsum("wb,wl->bl", onehot, dagg_window, preferred_element_type=jnp.float32)
        grad_half = jnp.where(live, upstream * silu_grad(pre), 0.0).astype(jnp.bfloat16)
        row_hot = (senders[None, :] == row_ids).astype(jnp.bfloat16)
        dpx = dpx + jnp.dot(row_hot, grad_half, preferred_element_type=jnp.float32)
        dew = dew + jnp.einsum("bl,fb->lf", grad_half.astype(jnp.float32), feats, precision=highest)
        return (dpx, dew)

    start_back = (
        jnp.zeros((grid_rows, width), jnp.float32),
        jnp.zeros((width, enc_feat_w.shape[1]), jnp.float32),
    )
    dpx_sum, enc_fw_part = lax.fori_loop(0, block_steps, enc_backward, start_back)
    dpx = dpx_sum.astype(jnp.bfloat16)
    enc_proj_part = jnp.dot(grid_latent.T, dpx, preferred_element_type=jnp.float32)
    grid_grad = (
        grid_cotangent.astype(jnp.float32)
        + jnp.dot(dpx, enc_proj.T, preferred_element_type=jnp.float32)
    ).astype(jnp.bfloat16)
    enc_proj_grad, node_proj_grad, dec_proj_grad, enc_feat_w_grad, dec_feat_w_grad = (
        lax.psum_scatter(enc_proj_part, "lat", scatter_dimension=0, tiled=True),
        lax.psum_scatter(node_proj_part, "lat", scatter_dimension=0, tiled=True),
        lax.psum_scatter(dec_proj_part, "lat", scatter_dimension=0, tiled=True),
        lax.psum_scatter(enc_fw_part, "lat", scatter_dimension=0, tiled=True),
        lax.psum_scatter(dec_fw_part, "lat", scatter_dimension=0, tiled=True),
    )
    return (
        grid_grad,
        mesh_grad,
        enc_proj_grad,
        node_proj_grad,
        dec_proj_grad,
        enc_feat_w_grad,
        dec_feat_w_grad,
    )


def mm(a, b, dims=NN, precision=None):
    return lax.dot_general(a, b, dims, precision=precision, preferred_element_type=F32)


def iota(shape, dim):
    return lax.broadcasted_iota(jnp.int32, shape, dim)


def halves(value):
    turn = jnp.tanh(value)
    up = 1.0 + turn
    silu = value * up
    return silu, up + silu * (1.0 - turn)


def hot(mask):
    return jnp.where(mask, 1.0, 0.0).astype(BF)


def split3(value):
    high = value.astype(BF).astype(F32)
    rest = value - high
    middle = rest.astype(BF).astype(F32)
    return high, middle, rest - middle


def stack_rows(feats):
    return -(-6 * feats // 16) * 16


def stack_terms(value, order):
    parts = split3(value)
    rows = len(order) * value.shape[0]
    blank = jnp.zeros((stack_rows(value.shape[0]) - rows, value.shape[1]), F32)
    return jnp.concatenate([*(parts[which] for which in order), blank], 0)


FEAT_ORDER = (0, 0, 1, 1, 2, 0)
WEIGHT_ORDER = (0, 1, 0, 1, 0, 2)


def fetch(sources, targets, sems):
    copies = [pltpu.make_async_copy(src, dst, sems.at[i]) for i, (src, dst) in enumerate(zip(sources, targets))]
    for copy in copies:
        copy.start()
    return copies


def feature_grad(terms, feats):
    total = terms[: 2 * feats] + terms[2 * feats : 4 * feats] + terms[4 * feats : 6 * feats]
    return jnp.where(iota(total.shape, 0) < feats, total, 0.0)


def encoder_kernel(
    cap, count, latent_any, weight_any, mesh_any, send_any, receive_any, feat_any, feat_w_any, serve_any,
    message, slope_far, served_out, own_out, px, picks, silus, slope, slope_sems,
    latent, weight, mesh, send, receive, feat, feat_w, serve, sems, latent_sems,
):
    sources = (send_any, feat_any, weight_any, feat_w_any, receive_any, mesh_any, serve_any)
    targets = (send, feat, weight, feat_w, receive, mesh, serve)
    copies = fetch(sources[:3], targets[:3], sems)
    edges = send.shape[1]
    grid_rows, width = latent.shape
    chips = message.shape[0]
    slots = served_out.shape[0]
    step = math.gcd(grid_rows, 256)
    cuts = [slice(start, start + step) for start in range(0, grid_rows, step)]
    chunks = fetch([latent_any.at[cut, :] for cut in cuts], [latent.at[cut, :] for cut in cuts], latent_sems)
    copies += fetch(sources[3:], targets[3:], sems.at[pl.ds(3, 4)])
    block = math.gcd(edges, 512)
    copies[0].wait()
    copies[1].wait()
    for start in range(0, edges, block):
        part = slice(start, start + block)
        ids = jnp.broadcast_to(send[:, part].astype(F32), (128, block)).T
        for base in range(0, grid_rows, 128):
            lane = (iota((block, 128), 1) + base).astype(F32)
            picks[part, base : base + 128] = hot(ids == lane)
    copies[2].wait()
    for cut, chunk in zip(cuts, chunks):
        chunk.wait()
    px[:grid_rows, :] = (0.5 * mm(latent[...], weight[...]).astype(BF).astype(F32)).astype(BF)
    for copy in copies[3:5]:
        copy.wait()
    terms = stack_terms(0.5 * feat_w[...], WEIGHT_ORDER)
    px[grid_rows:, :] = jnp.concatenate([terms, jnp.zeros((128 - terms.shape[0], width), F32)], 0).astype(BF)
    stores = []
    for start in range(0, edges, block):
        part = slice(start, start + block)
        pre = mm(picks[part, :grid_rows], px[:grid_rows, :])
        pre = pre + mm(stack_terms(feat[:, part], FEAT_ORDER).astype(BF), px[grid_rows : grid_rows + 32, :], TN)
        silu, double = halves(pre)
        slope[part, :] = double.astype(BF)
        out = pltpu.make_async_copy(slope.at[part, :], slope_far.at[part, :], slope_sems.at[len(stores)])
        out.start()
        stores.append(out)
        silus[part, :] = silu.astype(BF)
    live = iota((1, edges), 1) < count[0]
    total = mm(hot(iota((slots, edges), 0) == jnp.where(live, receive[...], -1)), silus[...])
    copies[5].wait()
    copies[6].wait()
    owners = slots // cap
    ids = serve[...]
    spread = hot(iota((owners, slots), 0) == lax.div(iota((owners, slots), 1), cap))
    turn = iota((cap, slots), 0) == iota((cap, slots), 1) % cap
    digits = []
    for value in (lax.shift_right_logical(ids, 8), ids & 255):
        wide = mm(value.astype(F32).astype(BF), spread)
        digits.append(jnp.sum(jnp.where(turn, wide, 0.0), 0, keepdims=True))
    id_row = (digits[0] * 256.0 + digits[1]).astype(jnp.int32)
    served = mm(hot(iota((mesh.shape[0], slots), 0) == id_row), mesh[...], TN)
    served_out[...] = served.astype(BF)
    code, scale, inverse = scale_codes(jnp.max(jnp.abs(total), 1, keepdims=True))
    fixed = to_fixed(total * inverse)
    own_out[...] = (total - fixed.astype(F32) * scale).astype(BF)
    half = fixed.astype(jnp.int16)
    latents = to_fixed(served * (1.0 / LATENT_STEP))
    code_row = jnp.broadcast_to(code.astype(F32), (slots, 128)).T[:1, :]
    lane = iota((slots, 128), 1)
    back = iota((slots, 128), 0)
    wide = 256.0 * mm(digits[0].astype(BF), hot(lane == back)) + mm(digits[1].astype(BF), hot(lane == back))
    wide = wide + mm(code_row.astype(BF), hot(lane == back + slots))
    id_rows = jnp.where(iota((8, 128), 0) == 0, wide, 0.0).astype(jnp.int32)
    for chip in range(chips):
        write_slots(message, chip, half)
        rows = latents[2 * cap * chip : 2 * cap * (chip + 1)]
        tail = [rows[:, base : base + 128] for base in range(0, width, 128)]
        message[chip, slots * (width // 128) :, :] = jnp.concatenate([*tail, id_rows], 0).astype(jnp.int16)
    for out in stores:
        out.wait()


LEAST_POWER = -40
LATENT_STEP = 6.0 / 32000.0


def scale_codes(peak):
    code = jnp.zeros(peak.shape, jnp.int32)
    scale = jnp.full(peak.shape, 2.0**LEAST_POWER, F32)
    inverse = jnp.full(peak.shape, 2.0**-LEAST_POWER, F32)
    for bit in (32, 16, 8, 4, 2, 1):
        more = peak > 32000.0 * (scale * 2.0 ** (bit - 1))
        code = code + jnp.where(more, bit, 0)
        scale = scale * jnp.where(more, 2.0**bit, 1.0)
        inverse = inverse * jnp.where(more, 2.0**-bit, 1.0)
    return code, scale, inverse


def scale_values(code):
    value = jnp.full(code.shape, 2.0**LEAST_POWER, F32)
    for bit in range(6):
        value = value * jnp.where((lax.shift_right_logical(code, bit) & 1) == 1, 2.0 ** (1 << bit), 1.0)
    return value


def to_fixed(value):
    return jnp.floor(value + 0.5).astype(jnp.int32)


def fixed_rows(ref, slots, width):
    parts = [
        jnp.concatenate([ref[chip, base : base + slots, :].astype(jnp.int32) for chip in range(ref.shape[0])], 0)
        for base in range(0, slots * (width // 128), slots)
    ]
    value = jnp.concatenate(parts, 1)
    return lax.shift_right_arithmetic(value, 8).astype(F32).astype(BF), (value & 255).astype(F32).astype(BF)


def write_slots(message, chip, value):
    slots = value.shape[0]
    for part in range(value.shape[1] // 128):
        message[chip, part * slots : (part + 1) * slots, :] = value[:, part * 128 : (part + 1) * 128]


def slot_rows(ref, slots, width):
    parts = [
        jnp.concatenate([ref[chip, base : base + slots, :] for chip in range(ref.shape[0])], 0)
        for base in range(0, slots * (width // 128), slots)
    ]
    return jnp.concatenate(parts, 1)


def gathered_slots(piece, chips, core, cap, shape, dim):
    slots = 2 * chips * cap
    index = iota(shape, dim)
    chip = lax.div(index, slots)
    slot = index - chip * slots
    band = 2 * chip + jnp.where(piece == 0, core, 1 - core)
    return band, lax.div(slot, cap), lax.rem(slot, cap)


def holder_of(shape, dim, chips, core):
    index = iota(shape, dim)
    return jnp.where(index < chips, 2 * index + core, 2 * (index - chips) + 1 - core)


def slot_matches(first, second, me, cap, mesh_rows, width):
    chips = first.shape[0]
    owners = 2 * chips
    slots = owners * cap
    span = chips * slots
    parts = width // 128
    core = lax.rem(me, 2)
    tables = [jnp.zeros((owners, 128), F32)] * 2
    latent = jnp.zeros((slots, width), F32)
    for piece, ref in enumerate((first, second)):
        ids, rows = [], []
        for chip in range(chips):
            tail = ref[chip, slots * parts :, :].astype(jnp.int32)
            ids.append(tail[8 * parts :])
            rows.append(jnp.concatenate([tail[8 * part : 8 * part + 8] for part in range(parts)], 1))
        ids = jnp.concatenate(ids, 0)
        rows = jnp.concatenate(rows, 0)
        shape = (owners, 8 * chips)
        take = hot(iota(shape, 1) == (iota(shape, 0) - piece * chips) * 8)
        for index, digit in enumerate((lax.shift_right_arithmetic(ids, 8), ids & 255)):
            tables[index] = tables[index] + mm(take, digit.astype(F32).astype(BF))
        shape = (slots, 8 * chips)
        window = iota(shape, 0)
        owner = lax.div(window, cap)
        held = lax.rem(owner, 2) == (core if piece == 0 else 1 - core)
        at = lax.div(owner, 2) * 8 + cap * core + lax.rem(window, cap)
        pick = hot(held & (iota(shape, 1) == at))
        high = lax.shift_right_arithmetic(rows, 8).astype(F32).astype(BF)
        latent = latent + 256.0 * mm(pick, high) + mm(pick, (rows & 255).astype(F32).astype(BF))
    latent = (latent * LATENT_STEP).astype(BF).astype(F32)
    digits = jnp.concatenate(tables, 0).astype(BF)
    shape = (slots, 2 * owners)
    half = lax.rem(iota(shape, 1), owners)
    holder = jnp.where(half < chips, 2 * half + core, 2 * (half - chips) + 1 - core)
    wanted = jnp.where(holder == lax.div(iota(shape, 0), cap), 1.0, 0.0)
    mine = mm((wanted * jnp.where(iota(shape, 1) < owners, 256.0, 1.0)).astype(BF), digits)
    lane = iota((slots, 128), 1) - cap * me - lax.rem(iota((slots, 128), 0), cap)
    own_key = jnp.sum(jnp.where(lane == 0, mine, 0.0), 1, keepdims=True)
    own_key = own_key + (lax.div(iota((slots, 1), 0), cap) * mesh_rows).astype(F32)
    keys, same, scales = [], [], []
    for piece in range(2):
        band, owner, place = gathered_slots(piece, chips, core, cap, (1, span), 1)
        spread = mm(digits, hot(iota((128, span), 0) == cap * band + place))
        value = 256.0 * spread[:owners] + spread[owners:]
        value = jnp.where(holder_of((owners, 1), 0, chips, core) == owner, value, 0.0)
        key = jnp.sum(value, 0, keepdims=True) + (owner * mesh_rows).astype(F32)
        keys.append(key)
        same.append(hot(key == own_key))
        index = iota((1, span), 1)
        spread = mm(digits[owners:], hot(iota((128, span), 0) == slots + lax.rem(index, slots)))
        source = iota((owners, 1), 0) - piece * chips == lax.div(index, slots)
        code = jnp.sum(jnp.where(source, spread, 0.0), 0, keepdims=True)
        scales.append(scale_values(code.astype(jnp.int32)))
    return keys, same, scales, latent


def decoder_picks(
    after, send_any, feat_any, node_any, dec_any, feat_w_any,
    pick, pick_turned, node_w, dec_w, feat_w, send, feat, sems,
):
    sources = (send_any, feat_any, node_any, dec_any, feat_w_any)
    copies = fetch(sources, (send, feat, node_w, dec_w, feat_w), sems)
    slots = after.shape[0]
    grid_rows = send.shape[1]
    copies[0].wait()
    copies[1].wait()
    block = math.gcd(grid_rows, 512)
    for k in range(3):
        for start in range(0, grid_rows, block):
            part = slice(start, start + block)
            to = slice(k * grid_rows + start, k * grid_rows + start + block)
            to_slot = jnp.where(iota((slots, block), 0) == send[k : k + 1, part], 1.0, 0.0)
            rows = jnp.concatenate([to_slot, stack_terms(feat[k, :, part], FEAT_ORDER)], 0)
            pick[:, to] = rows.astype(BF)
            rows = jnp.concatenate([rows, jnp.zeros((128 - rows.shape[0], block), F32)], 0)
            pick_turned[to, :] = rows.T.astype(BF)
    for copy in copies[2:]:
        copy.wait()


def encoder_picks(
    count, latent, receive_any, dec_any, node_any, send_any, feat_any,
    to_edge, latent_turned, chain, send, feat, receive, dec_w, node_w, sems,
):
    sources = (receive_any, dec_any, node_any, send_any, feat_any)
    copies = fetch(sources, (receive, dec_w, node_w, send, feat), sems)
    edges = receive.shape[1]
    copies[0].wait()
    block = math.gcd(edges, 512)
    for start in range(0, edges, block):
        part = slice(start, start + block)
        live = iota((1, block), 1) + start < count[0]
        slot = jnp.where(live, receive[:, part], -1)
        to_edge[part, :] = jnp.where(iota((128, block), 0) == slot, 1.0, 0.0).T.astype(BF)
    for copy in copies[1:3]:
        copy.wait()
    chain[...] = mm(node_w[...], dec_w[...]).T.astype(BF)
    latent_turned[...] = latent[...].T
    for copy in copies[3:]:
        copy.wait()


def decoder_kernel(
    cap, mesh_rows, place, first, second, extra, rest, pick, pick_turned, node_w, dec_w, feat_w, cotangent,
    message, keys_out, same_out, slope_out, grad_out, mine_out, rest_out,
):
    slots, width = extra.shape
    keys, same, scales, latent = slot_matches(first, second, place[0], cap, mesh_rows, width)
    weights, values = [], []
    for piece, ref in enumerate((first, second)):
        keys_out[piece : piece + 1, :] = keys[piece]
        same_out[piece] = same[piece]
        keys_out[2 + piece : 3 + piece, :] = scales[piece]
        weight = same[piece].astype(F32) * scales[piece]
        weights += [(256.0 * weight).astype(BF), weight.astype(BF)]
        values += fixed_rows(ref, slots, width)
    shape = (same[0].shape[1], slots)
    chosen = hot(iota(shape, 0) == slots * lax.div(place[0], 2) + iota(shape, 1))
    mine = mm(same[0], chosen).astype(BF)
    mine_out[...] = mine
    agg = mm(jnp.concatenate([*weights, mine], 1), jnp.concatenate([*values, rest[...]], 0))
    silu, double = halves(0.5 * agg)
    slope_out[...] = 0.25 * double
    hmesh = (latent + mm(silu.astype(BF), node_w[...])).astype(BF)
    proj = mm(hmesh, dec_w[...]).astype(BF)
    rows = pick.shape[0]
    blank = jnp.zeros((128 - rows, width), F32)
    terms = jnp.concatenate([stack_terms(0.5 * feat_w[...], WEIGHT_ORDER), blank], 0).astype(BF)
    table = jnp.concatenate([(0.5 * proj.astype(F32)).astype(BF), terms], 0)
    grid_rows = cotangent.shape[0]
    block = math.gcd(grid_rows, 1024)
    total = jnp.zeros((rows, width), F32)
    for start in range(0, grid_rows, block):
        cot = cotangent[start : start + block, :].astype(F32)
        for base in range(start, 3 * grid_rows, grid_rows):
            part = slice(base, base + block)
            double = halves(mm(pick_turned[part, :], table))[1]
            total = total + mm(pick[:, part], (cot * double).astype(BF))
    total = 0.5 * total
    half = total[:slots].astype(BF)
    rest_out[...] = (total[:slots] - half.astype(F32)).astype(BF)
    grad_out[...] = feature_grad(total[slots:], feat_w.shape[0])
    chips = message.shape[0]
    share = width // chips
    step = slots * share // 128
    for chip in range(chips):
        write_slots(message, chip, half)
        columns = extra[:, chip * share : (chip + 1) * share].astype(F32)
        columns = jnp.concatenate([columns[base : base + step] for base in range(0, slots, step)], 1)
        message[chip, slots * (width // 128) :, :] = columns.astype(BF)


def backward_kernel(
    place, first, second, same, mine, rest, agg_slope, dec_grad, to_edge, latent_turned, chain,
    send, feat, slope, dpx_far, dpx, give, sums_out, grads, dpx_sems,
):
    slots = same.shape[1]
    edges, width = grads.shape
    grid_rows = dpx.shape[0]
    feats = feat.shape[0]
    core = lax.rem(place[0], 2)
    dproj = mm(same[0], slot_rows(first, slots, width)) + mm(same[1], slot_rows(second, slots, width))
    dproj = dproj + mm(mine[...], rest[...])
    high = dproj.astype(BF)
    low = (dproj - high.astype(F32)).astype(BF)
    dact = mm(jnp.concatenate([high, low], 0), chain[...])
    dagg = (dact[:slots] + dact[slots:]) * agg_slope[...]
    dagg = jnp.concatenate([dagg, jnp.zeros((128 - slots, width), F32)], 0).astype(BF)
    block = math.gcd(edges, 1024)
    for start in range(0, edges, block):
        cut = slice(start, start + block)
        grads[cut, :] = (mm(to_edge[cut, :], dagg) * slope[cut, :].astype(F32)).astype(BF)
    step = math.gcd(grid_rows, 512)
    stores = []
    terms = stack_terms(feat[...], FEAT_ORDER).astype(BF)
    for start in range(0, grid_rows, step):
        cut = slice(start, start + step)
        left = hot(iota((step, edges), 0) + start == send[...])
        if start == 0:
            left = jnp.concatenate([left, terms], 0)
        product = mm(left, grads[...])
        if start == 0:
            enc_grad = feature_grad(product[step:], feats)
        dpx[cut, :] = product[:step].astype(BF)
        out = pltpu.make_async_copy(dpx.at[cut, :], dpx_far.at[cut, :], dpx_sems.at[len(stores)])
        out.start()
        stores.append(out)
    sums = jnp.where(iota(enc_grad.shape, 0) < feats, enc_grad, pltpu.roll(dec_grad[...], feats, 0))
    sums_out[...] = sums
    write_shares(give, 1 - core, latent_turned, dpx, sums)
    for out in stores:
        out.wait()


def write_shares(out, side, latent_turned, dpx, sums):
    chips = out.shape[0]
    width = dpx.shape[1]
    rows = width // (2 * chips)
    left = [latent_turned[pl.ds((2 * chip + side) * rows, rows), :] for chip in range(chips)]
    product = mm(jnp.concatenate(left, 0), dpx[...])
    blank = jnp.zeros((8, 128 - rows), F32)
    for chip in range(chips):
        block = product[chip * rows : (chip + 1) * rows]
        pair = [sums[:, base : base + rows] for base in (2 * chip * rows, (2 * chip + 1) * rows)]
        small = jnp.concatenate([jnp.where(side == 0, pair[0], pair[1]), blank], 1)
        pieces = [block[:, base : base + 128] for base in range(0, width, 128)]
        out[chip] = jnp.concatenate([*pieces, small], 0).astype(out.dtype)


def keep_kernel(place, latent_turned, dpx, sums, keep):
    write_shares(keep, lax.rem(place[0], 2), latent_turned, dpx, sums[...])


def pair_kernel(keep, given, out):
    out[...] = (keep[...] + given[...].astype(F32)).astype(BF)


def final_kernel(feats, arrived, out, enc_out, dec_out):
    total = jnp.sum(arrived[...].astype(F32), 0)
    rows, width = out.shape
    for part in range(width // 128):
        out[:, part * 128 : (part + 1) * 128] = total[part * rows : (part + 1) * rows]
    base = rows * (width // 128)
    enc_out[...] = total[base : base + feats, :rows]
    dec_out[...] = total[base + feats : base + 2 * feats, :rows]


def beside_kernel(
    cap, mesh_rows, place, keys, node_any, first_any, second_any, first_back_any, second_back_any, dec_any, dpx_any,
    weight_any, cot_any, mesh_out, dec_out, node_out, grid_out,
    node_w, first, second, first_back, second_back, dec_w, dpx, weight, cotangent, sems,
):
    sources = (
        first_any, second_any, node_any, first_back_any, second_back_any, dec_any, dpx_any, weight_any, cot_any,
    )
    targets = (first, second, node_w, first_back, second_back, dec_w, dpx, weight, cotangent)
    copies = fetch(sources, targets, sems)
    width = node_w.shape[0]
    chips = first.shape[0]
    owners = 2 * chips
    slots = owners * cap
    span = chips * slots
    me = place[0]
    core = lax.rem(me, 2)
    block = width // owners
    key = jnp.concatenate([keys[0:1, :], keys[1:2, :]], 1)
    down = jnp.broadcast_to(key, (128, 2 * span)).T
    scale = jnp.concatenate([keys[2:3, :], keys[3:4, :]], 1)
    same = [
        jnp.where(down == key[:, base : base + 128], scale[:, base : base + 128], 0.0).astype(BF)
        for base in range(0, 2 * span, 128)
    ]
    same = jnp.concatenate(same, 1)
    for copy in copies[:3]:
        copy.wait()
    forward = jnp.concatenate([slot_rows(ref, slots, width) for ref in (first, second)], 0)
    act = halves(0.5 * mm(same, forward.astype(F32).astype(BF)))[0].astype(BF)
    shape = (width, 128)
    mine = hot((iota(shape, 0) == block * me + iota(shape, 1)) & (iota(shape, 1) < block))
    node_cols = mm(node_w[...], mine).astype(BF)
    both = mm(act, jnp.concatenate([node_cols, mine], 1))
    step = slots * 2 * block // 128
    pieces = [gathered_slots(piece, chips, core, cap, (span, 1), 0) for piece in range(2)]
    band, owner, turn = [jnp.concatenate([a, b], 0) for a, b in zip(*pieces)]
    source = jnp.where(lax.rem(owner, 2) == core, 0, chips) + lax.div(owner, 2)
    number = cap * band + turn
    at = lax.div(number, step) * (owners * step) + source * step + lax.rem(number, step)
    for copy in copies[3:]:
        copy.wait()
    back = jnp.concatenate([slot_rows(ref, slots, width) for ref in (first_back, second_back)], 0)
    tail = slots * (width // 128)
    columns = [ref[chip, tail:, :] for ref in (first_back, second_back) for chip in range(chips)]
    columns = jnp.concatenate(columns, 0)
    shape = (128, 128)
    folded = []
    for base in range(0, 128, 2 * block):
        fold = hot((iota(shape, 0) == base + block * core + iota(shape, 1)) & (iota(shape, 1) < block))
        folded.append(mm(columns, fold).astype(BF))
    latent = mm(hot(iota((2 * span, 2 * span), 1) == at), jnp.concatenate(folded, 0))
    hmesh = (both[:, :128] + latent).astype(BF)
    left = jnp.concatenate([hmesh, both[:, 128:].astype(BF)], 1)
    sums = mm(left, back, TN)
    dec_out[...] = sums[:block]
    own = (me * mesh_rows + iota((mesh_out.shape[0], 2 * span), 0)).astype(F32)
    dproj = jnp.concatenate([mm(hot(own == key), back), sums[128 : 128 + block]], 0)
    high = dproj.astype(BF)
    low = (dproj - high.astype(F32)).astype(BF)
    turned = mm(high, dec_w[...], NT) + mm(low, dec_w[...], NT)
    mesh = mesh_out.shape[0]
    mesh_out[...] = turned[:mesh].astype(BF)
    node_out[...] = turned[mesh:]
    grid_out[...] = (cotangent[...].astype(F32) + mm(dpx[...], weight[...], NT)).astype(BF)


SMEM = pl.BlockSpec(memory_space=pltpu.SMEM)
VMEM = pl.BlockSpec(memory_space=pltpu.VMEM)
FAR = pl.BlockSpec(memory_space=pltpu.HBM)


def kernel_call(body, name, scalars, near, far, outs, scratch, flops, limit, out_specs=None, pin=False, last=(), kept=0):
    shapes = [jax.ShapeDtypeStruct(shape, dtype) for shape, dtype in outs]
    out_specs = out_specs or [VMEM] * len(shapes)
    pinned = [pltpu.HBM(s.shape, s.dtype) if spec is FAR else s for s, spec in zip(shapes, out_specs)]
    if pin:
        far = [pltpu.with_memory_space_constraint(a, pltpu.HBM) for a in far]
    moved = sum(a.size * a.dtype.itemsize for a in (*near, *far)) + sum(s.size * s.dtype.itemsize for s in shapes)
    buffers = [pltpu.VMEM(a.shape, a.dtype) for a in far[: len(far) - kept]]
    if far:
        buffers.append(pltpu.SemaphoreType.DMA((len(far),)))
    return pl.pallas_call(
        body,
        name=name,
        out_shape=pinned,
        in_specs=[SMEM] * len(scalars) + [VMEM] * len(near) + [FAR] * len(far),
        out_specs=out_specs,
        scratch_shapes=[*scratch, *buffers, *last],
        compiler_params=pltpu.CompilerParams(vmem_limit_bytes=limit * MIB),
        cost_estimate=pl.CostEstimate(flops=flops, bytes_accessed=moved, transcendentals=0),
    )(*scalars, *near, *far)


def gather_plan(
    grid_latent,
    mesh_latent,
    grid_cotangent,
    enc_sender,
    enc_receiver,
    enc_feat,
    enc_count,
    dec_sender,
    dec_feat,
    serve_rows,
    enc_proj,
    node_proj,
    dec_proj,
    enc_feat_w,
    dec_feat_w,
):
    owners = lax.axis_size("lat")
    chips = owners // 2
    cap = serve_rows.shape[2]
    slots = owners * cap
    mesh_rows, width = mesh_latent.shape
    grid_rows = grid_latent.shape[0]
    edges = enc_sender.shape[0]
    feats = enc_feat.shape[0]
    block = width // owners
    span = chips * slots
    parts = width // 128
    share = width // chips
    groups = [[core + 2 * chip for chip in range(chips)] for core in range(2)]
    swap = [(index, index ^ 1) for index in range(owners)]
    place = lax.axis_index("lat").astype(jnp.int32).reshape(1)

    def gather(message, *later):
        first = lax.all_to_all(message, "lat", 0, 0, tiled=True, axis_index_groups=groups)
        first, *later = lax.optimization_barrier((first, *later))
        return first, lax.ppermute(first, "lat", swap), *later

    send = enc_sender.reshape(1, edges)
    receive = enc_receiver.reshape(1, edges)
    message, slope, served, rest = kernel_call(
        lambda *refs: encoder_kernel(cap, *refs),
        "encoder",
        [enc_count],
        [],
        [grid_latent, enc_proj, mesh_latent, send, receive, enc_feat, enc_feat_w.T, serve_rows[0].T],
        [
            ((chips, parts * (slots + 8) + 8, 128), jnp.int16),
            ((edges, width), BF),
            ((slots, width), BF),
            ((slots, width), BF),
        ],
        [
            pltpu.VMEM((grid_rows + 128, width), BF),
            pltpu.VMEM((edges, grid_rows), BF),
            pltpu.VMEM((edges, width), BF),
            pltpu.VMEM((edges, width), BF),
            pltpu.SemaphoreType.DMA((edges // math.gcd(edges, 512),)),
        ],
        2 * edges * grid_rows * width,
        28,
        [VMEM, FAR, VMEM, VMEM],
        pin=True,
        last=[pltpu.SemaphoreType.DMA((grid_rows // math.gcd(grid_rows, 256),))],
    )
    term_rows = stack_rows(feats)
    first, second, served = gather(message, served)
    pick, pick_turned, near_node, near_dec, near_feat_w = kernel_call(
        decoder_picks,
        "decoder_picks",
        [],
        [served],
        [dec_sender, dec_feat, node_proj, dec_proj, dec_feat_w.T],
        [
            ((slots + term_rows, 3 * grid_rows), BF),
            ((3 * grid_rows, 128), BF),
            ((width, width), BF),
            ((width, width), BF),
            ((feats, width), F32),
        ],
        [],
        2000 * MIB,
        16,
        pin=True,
        kept=3,
    )
    message, keys, same, agg_slope, dec_grad, mine, rest = kernel_call(
        lambda *refs: decoder_kernel(cap, mesh_rows, *refs),
        "decoder",
        [place],
        [first, second, served, rest, pick, pick_turned, near_node, near_dec, near_feat_w, grid_cotangent],
        [],
        [
            ((chips, parts * slots + slots * share // 128, 128), BF),
            ((4, span), F32),
            ((2, slots, span), BF),
            ((slots, width), F32),
            ((2 * feats, width), F32),
            ((slots, slots), BF),
            ((slots, width), BF),
        ],
        [],
        24 * grid_rows * 128 * width,
        20,
    )
    first_back, second_back, pick_count = gather(message, enc_count)
    to_edge, latent_turned, chain, near_send, near_feat = kernel_call(
        encoder_picks,
        "encoder_picks",
        [pick_count],
        [grid_latent],
        [receive, dec_proj, node_proj, send, enc_feat],
        [
            ((edges, 128), BF),
            ((width, grid_rows), BF),
            ((width, width), BF),
            ((1, edges), jnp.int32),
            ((feats, edges), F32),
        ],
        [],
        2000 * MIB,
        16,
        pin=True,
        kept=2,
    )
    dpx_far, dpx, give, sums = kernel_call(
        backward_kernel,
        "backward",
        [place],
        [
            first_back,
            second_back,
            same,
            mine,
            rest,
            agg_slope,
            dec_grad,
            to_edge,
            latent_turned,
            chain,
            near_send,
            near_feat,
            slope,
        ],
        [],
        [
            ((grid_rows, width), BF),
            ((grid_rows, width), BF),
            ((chips, parts * block + 8, 128), BF),
            ((2 * feats, width), F32),
        ],
        [
            pltpu.VMEM((edges, width), BF),
            pltpu.SemaphoreType.DMA((grid_rows // math.gcd(grid_rows, 256),)),
        ],
        2 * edges * grid_rows * width,
        24,
        [FAR, VMEM, VMEM, VMEM],
    )
    (keep,) = kernel_call(
        keep_kernel,
        "keep",
        [place],
        [latent_turned, dpx, sums],
        [],
        [((chips, parts * block + 8, 128), F32)],
        [],
        grid_rows * width * width,
        16,
    )
    given = lax.ppermute(give, "lat", swap)
    (pair,) = kernel_call(pair_kernel, "pair", [], [keep, given], [], [(give.shape, BF)], [], keep.size, 8)
    pair, keys, dpx_far = lax.optimization_barrier((pair, keys, dpx_far))
    arrived = lax.all_to_all(pair, "lat", 0, 0, tiled=True, axis_index_groups=groups)
    mesh_grad, dec_proj_grad, node_proj_grad, grid_grad = kernel_call(
        lambda *refs: beside_kernel(cap, mesh_rows, *refs),
        "beside",
        [place],
        [keys],
        [
            node_proj,
            first,
            second,
            first_back,
            second_back,
            dec_proj,
            dpx_far,
            enc_proj,
            grid_cotangent,
        ],
        [
            ((mesh_rows, width), BF),
            ((block, width), F32),
            ((block, width), F32),
            ((grid_rows, width), BF),
        ],
        [],
        2 * (2 * span) * (2 * span) * width,
        30,
        pin=True,
    )
    enc_proj_grad, enc_feat_grad, dec_feat_grad = kernel_call(
        lambda *refs: final_kernel(feats, *refs),
        "final",
        [],
        [arrived],
        [],
        [((block, width), F32), ((feats, block), F32), ((feats, block), F32)],
        [],
        arrived.size,
        8,
    )
    return (
        grid_grad,
        mesh_grad,
        enc_proj_grad,
        node_proj_grad,
        dec_proj_grad,
        enc_feat_grad.T,
        dec_feat_grad.T,
    )


def gather_fits(args):
    mesh_latent, serve_rows = args[1], args[9]
    owners, cap = serve_rows.shape[1], serve_rows.shape[2]
    width = mesh_latent.shape[1]
    chips = owners // 2
    return (
        owners % 2 == 0
        and 2 * cap == 8
        and owners * cap <= 64
        and width % 128 == 0
        and width % (8 * owners) == 0
        and 128 % (width // chips) == 0
        and owners * cap * (width // chips) % 2048 == 0
        and mesh_latent.shape[0] <= 32768
        and mesh_latent.shape[0] * owners < 1 << 24
        and args[0].shape[0] % 128 == 0
        and args[3].shape[0] % 128 == 0
        and args[5].shape[0] == 4
    )


def per_device(*args):
    return gather_plan(*args) if gather_fits(args) else owner_plan(*args)


def solution(mesh):
    placed = (
        P(("member", "lat"), None),
        P(("member", "lat"), None),
        P(("member", "lat"), None),
        P(("member", "lat")),
        P(("member", "lat")),
        P(None, ("member", "lat")),
        P(("member", "lat")),
        P(None, ("member", "lat")),
        P(None, None, ("member", "lat")),
        P(("member", "lat"), None, None),
        P(),
        P(),
        P(),
        P(),
        P(),
    )
    return jax.shard_map(
        per_device,
        mesh=mesh,
        in_specs=placed,
        out_specs=(
            P(("member", "lat"), None),
            P(("member", "lat"), None),
            P(("member", "lat"), None),
            P(("member", "lat"), None),
            P(("member", "lat"), None),
            P(("member", "lat"), None),
            P(("member", "lat"), None),
        ),
        check_vma=False,
    )
```
